32 devices in a mesh: sec: 2 (over core), seq: 8 (over z, x), tp: 2 (over y).
Axes of the slice: x: 2, y: 2, z: 4, core: 2. Of those that a mesh axis runs over, the one named last changes fastest.
Arguments:
- hidden_rows: bfloat16 [2, 512, 5120], P('sec', 'seq'), may hold values from -10 to 10
- carried: bfloat16 [2, 512, 5120], P('sec', 'seq'), may hold values from -6 to 6
- query_weight: bfloat16 [2, 5120, 4096], P('sec', 'seq', 'tp'), may hold values from -6 to 6
- response_cache: bfloat16 [2, 512, 2048], P('sec', 'seq', 'tp'), may hold values from -8.375 to 8.375
- prompt_cache: bfloat16 [2, 8, 16384, 2048], P('sec', None, 'seq', 'tp'), may hold values from -5 to 5
- prompt_lengths: int32 [8], replicated, may hold values from 1 to 16384, 81920 in all
- response_lengths: int32 [2, 8], replicated, may hold values from 1 to 64, 320 in all within a row
- block_prompts: int32 [2, 8, 1], replicated, may hold values from 0 to 7
Outputs:
- attended: bfloat16 [2, 512, 4096], P('sec', 'seq', 'tp')
The draws below stay inside these ranges and needn't reach their ends.
All inputs are finite; a program needn't handle non-finite values.
Results may differ from the reference program's by a relative error of at most 0.0096.
Values may be sent and summed in bfloat16 or wider, within the bound.
No kernel may reach another device: no remote copies, remote signals or barrier semaphores. Data moves between devices by JAX's collectives and lax.ppermute only.
A program may use at most 192 MiB of HBM per device.

```python
import math
import jax
import jax.numpy as jnp
import numpy as np
from jax import lax

D = 5120
H = 32
KVH = 8
HD = 128
NP = 8
BL = 64
PL = 16384
GR = 4
NB = 8
ROWS = 512
N_SEQ = 8


def draw_prompt_cache(key, part):
    key = jax.random.fold_in(key, 5)
    base_key = jax.random.fold_in(key, 0)
    values = jnp.clip(jax.random.normal(base_key, (2, NP, PL, KVH, 2, HD), jnp.float32), -4.5, 4.5)
    return values.reshape(2, NP, PL, KVH * 2 * HD).astype(jnp.bfloat16)


def draw_hidden_rows(key, part):
    key = jax.random.fold_in(key, 9)
    values = jnp.clip(2.6 * jax.random.normal(key, (2, NB, BL, D), jnp.float32), -10.0, 10.0)
    return values.reshape(2, NB * BL, D).astype(jnp.bfloat16)


def draw_carried(key, part):
    key = jax.random.fold_in(key, 11)
    values = jnp.clip(jax.random.normal(key, (2, ROWS, D), jnp.float32), -6.0, 6.0)
    return values.astype(jnp.bfloat16)


def draw_query_weight(key, part):
    key = jax.random.fold_in(key, 13)
    values = jnp.clip(jax.random.normal(key, (2, D, H * HD), jnp.float32), -4.0, 4.0) * D ** (-0.5)
    return values.astype(jnp.bfloat16)


def levels(own_key, extent, cuts, low, high):
    level, own = 1.0, jax.random.fold_in(own_key, 6)
    for axis_at, blocks in cuts:
        steps = jnp.exp(jax.random.uniform(jax.random.fold_in(own, axis_at), (blocks,), jnp.float32, low / len(cuts), high / len(cuts)))
        level = level * jnp.repeat(steps, extent[axis_at] // blocks).reshape([-1 if axis == axis_at else 1 for axis in range(len(extent))])
    return level


def picks_of(own_key, rows, number_of, top, lift):
    order = jax.random.permutation(jax.random.fold_in(own_key, 1), number_of)
    boost = order
    for power in range(3):
        boost = boost * boost // number_of
    boost = boost * lift // number_of
    tickets = jax.random.randint(jax.random.fold_in(own_key, 2), (rows, number_of), 0, 4096) + boost
    sure = jax.random.permutation(jax.random.fold_in(own_key, 3), rows)[jnp.arange(number_of) % rows]
    tickets = jnp.where(jnp.arange(rows)[:, None] == sure[None, :], 1 << 14, tickets)
    score = tickets * number_of + jnp.arange(number_of)
    return lax.top_k(score.astype(jnp.int32), top)[1].astype(jnp.int32)


def length_profile(amount, total, reach, lean):
    portions = [(1 << 20) // math.isqrt(standing ** lean) + 1 for standing in range(2, amount + 1)]
    rest, given = total - reach - (amount - 1), [1] * (amount - 1)
    while rest > 0:
        candidates = [i for i in range(amount - 1) if given[i] < reach]
        pool, left = sum([portions[i] for i in candidates]), rest
        for i in candidates:
            more = min(reach - given[i], max(1, left * portions[i] // pool), rest)
            given[i] = given[i] + more
            rest = rest - more
    return np.array([reach] + given)


def ragged(own_key, number_of, total, bound, lean):
    if number_of == 2:
        one = jax.random.randint(own_key, (), max(1, total - bound), min(bound, total - 1) + 1)
        return jnp.stack([one, total - one])
    tallies = jnp.asarray(length_profile(number_of, total, bound, lean), jnp.int32)
    twos = (number_of - 1) // 2
    giver, sink = tallies[1:1 + 2 * twos:2], tallies[2:2 + 2 * twos:2]
    room = jnp.minimum(giver - 1, bound - sink)
    moved = jax.random.randint(jax.random.fold_in(own_key, 1), (twos,), 0, 1 << 20) % (room + 1)
    tallies = tallies.at[1:1 + 2 * twos:2].set(giver - moved).at[2:2 + 2 * twos:2].set(sink + moved)
    return tallies[jax.random.permutation(jax.random.fold_in(own_key, 2), number_of)]


def noise(rng, extent, deviation, bound, cuts=(), held_as=jnp.bfloat16):
    values = jax.random.normal(rng, extent, jnp.float32) * deviation
    if len(cuts) > 0:
        values = levels(rng, extent, cuts, -0.22, 0.18) * values
    return jnp.clip(values, min=-bound, max=bound).astype(held_as)


def setup_inputs(seed: int = 0) -> dict:
    key_list = jax.random.split(jax.random.key(seed), 9)
    hidden_rows = draw_hidden_rows(jax.random.fold_in(key_list[8], 71), 0)
    carried = draw_carried(jax.random.fold_in(key_list[8], 71), 0)
    query_weight = draw_query_weight(jax.random.fold_in(key_list[8], 71), 0)
    response_cache = noise(key_list[3], (2, ROWS, KVH * 2 * HD), 1.4, 8.375, ((0, 2), (1, 8), (2, 2)))
    prompt_cache = draw_prompt_cache(jax.random.fold_in(key_list[8], 71), 0)
    prompt_lengths = ragged(key_list[5], NP, NP * PL * 5 // 8, PL, 2).astype(jnp.int32)
    response_lengths = jax.vmap(lambda own: ragged(own, NB, NB * BL * 5 // 8, BL, 1))(jax.random.split(key_list[6], 2)).reshape((2, NB)).astype(jnp.int32)
    block_prompts = picks_of(key_list[7], 2 * NB, NP, 1, 2048).reshape((2, NB, 1))
    return dict(hidden_rows=hidden_rows, carried=carried, query_weight=query_weight, response_cache=response_cache, prompt_cache=prompt_cache, prompt_lengths=prompt_lengths, response_lengths=response_lengths, block_prompts=block_prompts)


NEG_FILL = -1e30


def attend_block(query_block, cache_block, response_block, prompt_valid, response_length):
    queries = query_block.astype(jnp.float32)
    prompt_keys = cache_block[:, :, 0].astype(jnp.float32)
    prompt_values = cache_block[:, :, 1].astype(jnp.float32)
    own_keys = response_block[:, :, 0].astype(jnp.float32)
    own_values = response_block[:, :, 1].astype(jnp.float32)
    score_scale = HD ** -0.5
    prompt_scores = jnp.einsum("igqd,jgd->igqj", queries, prompt_keys) * score_scale
    own_scores = jnp.einsum("igqd,tgd->igqt", queries, own_keys) * score_scale
    positions = jnp.arange(BL, dtype=jnp.int32)
    causal = (positions[:, None] >= positions[None, :])[:, None, None, :]
    prompt_mask = prompt_valid[None, None, None, :]
    row_peak = jnp.maximum(
        jnp.max(jnp.where(prompt_mask, prompt_scores, NEG_FILL), axis=-1),
        jnp.max(jnp.where(causal, own_scores, NEG_FILL), axis=-1))
    prompt_weights = jnp.where(prompt_mask, jnp.exp(prompt_scores - row_peak[..., None]), 0.0)
    prompt_weights = lax.optimization_barrier(prompt_weights.astype(jnp.bfloat16)).astype(jnp.float32)
    own_weights = jnp.where(causal, jnp.exp(own_scores - row_peak[..., None]), 0.0)
    own_weights = lax.optimization_barrier(own_weights.astype(jnp.bfloat16)).astype(jnp.float32)
    row_total = jnp.sum(prompt_weights, axis=-1) + jnp.sum(own_weights, axis=-1)
    row_sum = jnp.einsum("igqj,jgd->igqd", prompt_weights, prompt_values)
    row_sum = row_sum + jnp.einsum("igqt,tgd->igqd", own_weights, own_values)
    output = row_sum / row_total[..., None]
    output = jnp.where((positions < response_length)[:, None, None, None], output, 0.0)
    return output.reshape(BL, H * HD).astype(jnp.bfloat16)


def reference(hidden_rows, carried, query_weight, response_cache, prompt_cache, prompt_lengths, response_lengths, block_prompts):
    results = []
    for section in range(2):
        inputs = hidden_rows[section].astype(jnp.float32)
        if section == 1:
            inputs = inputs + carried[0].astype(jnp.float32)
        inputs = inputs.astype(jnp.bfloat16)
        queries = jnp.dot(inputs, query_weight[section], preferred_element_type=jnp.float32)
        queries = queries.astype(jnp.bfloat16).reshape(N_SEQ, BL, KVH, GR, HD)
        responses = response_cache[section].reshape(N_SEQ, BL, KVH, 2, HD)
        caches = prompt_cache[section].reshape(NP, PL, KVH, 2, HD)
        chosen = block_prompts[section, :, 0].astype(jnp.int32)
        lengths = response_lengths[section].astype(jnp.int32)

        def one_block(block_inputs, caches=caches):
            query_block, response_block, prompt_index, response_length = block_inputs
            cache_block = lax.dynamic_index_in_dim(caches, prompt_index, 0, keepdims=False)
            prompt_valid = jnp.arange(PL, dtype=jnp.int32) < prompt_lengths[prompt_index]
            return attend_block(query_block, cache_block, response_block, prompt_valid, response_length)

        blocks = lax.map(one_block, (queries, responses, chosen, lengths))
        results.append(blocks.reshape(N_SEQ * BL, H * HD))
    return jnp.stack(results)
```

```python
import functools
import math

import jax
import jax.numpy as jnp
from jax import lax
from jax.experimental import pallas as pl
from jax.experimental.pallas import tpu as pltpu
from jax.sharding import PartitionSpec as P

HD = 128
GR = 4
NEG = -1e30
LOG2E = 1.4426950408889634
CHUNK = 512
EXTRA = 128
VMEM = 56 * 1024 * 1024


def from_behind(value, axis, steps):
    count = lax.axis_size(axis)
    first, last = (max(0, -steps), min(count, count - steps))
    return lax.ppermute(value, axis, [(source, source + steps) for source in range(first, last)])


def dot_nt(a, b):
    return lax.dot_general(a, b, (((1,), (1,)), ((), ())), preferred_element_type=jnp.float32)


def project_kernel(nb, bl, packed, meta, x_ref, w_ref, out_ref, xp_ref):
    @pl.when(pl.program_id(0) == 0)
    def _():
        total = jnp.zeros(xp_ref.shape, jnp.float32)
        offset = jnp.int32(0)
        place = lax.broadcasted_iota(jnp.int32, (packed, bl), 0)
        order = lax.broadcasted_iota(jnp.int32, (packed, bl), 1)
        parts = []
        for b in range(nb):
            length = meta[b]
            pick = (place == order + offset) & (order < length)
            parts.append(jnp.where(pick, 1.0, 0.0).astype(jnp.bfloat16))
            offset = offset + length
        pick = jnp.concatenate(parts, axis=1)
        total = jnp.dot(pick, x_ref[...], preferred_element_type=jnp.float32)
        xp_ref[...] = total.astype(jnp.bfloat16)

    out_ref[...] = jnp.dot(xp_ref[...], w_ref[...], preferred_element_type=jnp.float32)


def project(lengths, x, w, nb, bl, packed):
    k, cols = w.shape
    tile = min(512, cols)
    return pl.pallas_call(
        functools.partial(project_kernel, nb, bl, packed),
        grid_spec=pltpu.PrefetchScalarGridSpec(
            num_scalar_prefetch=1,
            grid=(cols // tile,),
            in_specs=[
                pl.BlockSpec((nb * bl, k), lambda j, m: (0, 0)),
                pl.BlockSpec((k, tile), lambda j, m: (0, j)),
            ],
            out_specs=pl.BlockSpec((packed, tile), lambda j, m: (0, j)),
            scratch_shapes=[pltpu.VMEM((packed, k), jnp.bfloat16)],
        ),
        out_shape=jax.ShapeDtypeStruct((packed, cols), jnp.float32),
        compiler_params=pltpu.CompilerParams(vmem_limit_bytes=VMEM),
        cost_estimate=pl.CostEstimate(
            flops=2 * packed * k * cols, bytes_accessed=2 * k * cols + 4 * packed * cols,
            transcendentals=0,
        ),
        name="project",
    )(lengths, x, w)


def attend_kernel(nb, bl, packed, tile_len, heads, meta, q_ref, kv_ref, own_ref, o_ref,
                  q32_ref, s_ref, acc_ref, m_ref):
    b = pl.program_id(0)
    valid = meta[nb + b]
    offset = meta[2 * nb + b]
    mine = meta[3 * nb] == b
    m_rows = GR * bl
    c2 = LOG2E / math.sqrt(HD)
    chunk = min(CHUNK, tile_len)
    ones_of = lambda rows: jnp.ones((rows, HD), jnp.bfloat16)

    @pl.when(b == 0)
    def _():
        q32_ref[:packed, :] = q_ref[...].astype(jnp.float32)
        q32_ref[packed:, :] = jnp.zeros((bl + 8, q32_ref.shape[1]), jnp.float32)

    lane = lax.broadcasted_iota(jnp.int32, (bl, EXTRA), 1)
    lse_tile = jnp.zeros((bl, EXTRA), jnp.float32)
    rest = offset % 8
    window = q32_ref[pl.ds(pl.multiple_of(offset - rest, 8), bl + 8), :]
    window = pltpu.roll(window, jnp.where(rest == 0, 0, bl + 8 - rest), 0)
    queries = window[:bl].astype(jnp.bfloat16)
    for g in range(heads):
        q = jnp.concatenate(
            [queries[:, (g * GR + r) * HD:(g * GR + r + 1) * HD] for r in range(GR)], axis=0
        )
        keys = pl.ds(g * 2 * HD, HD)
        vals = pl.ds(g * 2 * HD + HD, HD)

        @pl.when(valid == tile_len)
        def _():
            s = dot_nt(q, kv_ref[0, 0, :, keys]) * c2
            m = jnp.max(s, axis=1, keepdims=True)
            p = jnp.exp2(s - m).astype(jnp.bfloat16)
            v = jnp.concatenate([kv_ref[0, 0, :, vals], ones_of(tile_len)], axis=1)
            acc_ref[...] = jnp.dot(p, v, preferred_element_type=jnp.float32)
            m_ref[...] = jnp.broadcast_to(m, m_ref.shape)

        @pl.when(valid < tile_len)
        def _():
            count = (valid + chunk - 1) // chunk
            acc_ref[...] = jnp.zeros_like(acc_ref)
            m_ref[...] = jnp.full_like(m_ref, NEG)

            def scores(c, carry):
                at = pl.multiple_of(c * chunk, chunk)
                s = dot_nt(q, kv_ref[0, 0, pl.ds(at, chunk), keys]) * c2
                here = lax.broadcasted_iota(jnp.int32, s.shape, 1) + at
                s = jnp.where(here < valid, s, NEG)
                s_ref[c] = s
                m_ref[...] = jnp.maximum(m_ref[...], jnp.max(s, axis=1, keepdims=True))
                return carry

            lax.fori_loop(0, count, scores, 0)

            def sums(c, carry):
                at = pl.multiple_of(c * chunk, chunk)
                s = s_ref[c]
                here = lax.broadcasted_iota(jnp.int32, s.shape, 1) + at
                p = jnp.where(here < valid, jnp.exp2(s - m_ref[:, :1]), 0.0).astype(jnp.bfloat16)
                v = jnp.concatenate([kv_ref[0, 0, pl.ds(at, chunk), vals], ones_of(chunk)], axis=1)
                acc_ref[...] += jnp.dot(p, v, preferred_element_type=jnp.float32)
                return carry

            lax.fori_loop(0, count, sums, 0)

        @pl.when(mine)
        def _():
            s = dot_nt(q, own_ref[:, keys]) * c2
            row = lax.broadcasted_iota(jnp.int32, s.shape, 0) % bl
            col = lax.broadcasted_iota(jnp.int32, s.shape, 1)
            seen = col <= row
            s = jnp.where(seen, s, NEG)
            before = m_ref[:, :1]
            m = jnp.maximum(before, jnp.max(s, axis=1, keepdims=True))
            p = jnp.where(seen, jnp.exp2(s - m), 0.0).astype(jnp.bfloat16)
            v = jnp.concatenate([own_ref[:, vals], ones_of(bl)], axis=1)
            acc_ref[...] = acc_ref[...] * jnp.exp2(before - m) + jnp.dot(
                p, v, preferred_element_type=jnp.float32
            )
            m_ref[...] = jnp.broadcast_to(m, m_ref.shape)

        total = acc_ref[:, HD:]
        some = total > 0.0
        safe = jnp.where(some, total, 1.0)
        out = (acc_ref[:, :HD] / safe).astype(jnp.bfloat16)
        lse = jnp.where(some, m_ref[...] + jnp.log2(safe), NEG)
        for r in range(GR):
            h = g * GR + r
            o_ref[0, :, h * HD:(h + 1) * HD] = out[r * bl:(r + 1) * bl]
            lse_tile = jnp.where(lane == h, lse[r * bl:(r + 1) * bl], lse_tile)
    high = lse_tile.astype(jnp.bfloat16)
    rest = lse_tile - high.astype(jnp.float32)
    mid = rest.astype(jnp.bfloat16)
    low = (rest - mid.astype(jnp.float32)).astype(jnp.bfloat16)
    base = heads * GR * HD
    o_ref[0, :, base:base + EXTRA] = high
    o_ref[0, :, base + EXTRA:base + 2 * EXTRA] = mid
    o_ref[0, :, base + 2 * EXTRA:base + 3 * EXTRA] = low


def attend(meta, q, cache, own, nb, bl, first, heads):
    packed, cols = q.shape
    tile_len = cache.shape[2]
    chunk = min(CHUNK, tile_len)
    width = heads * GR * HD + 3 * EXTRA
    return pl.pallas_call(
        functools.partial(attend_kernel, nb, bl, packed, tile_len, heads),
        grid_spec=pltpu.PrefetchScalarGridSpec(
            num_scalar_prefetch=1,
            grid=(nb,),
            in_specs=[
                pl.BlockSpec((packed, cols), lambda b, m: (0, 0)),
                pl.BlockSpec(
                    (1, 1, tile_len, heads * 2 * HD), lambda b, m: (0, m[b], 0, first // heads)
                ),
                pl.BlockSpec((bl, heads * 2 * HD), lambda b, m: (0, first // heads)),
            ],
            out_specs=pl.BlockSpec((1, bl, width), lambda b, m: (b, 0, 0)),
            scratch_shapes=[
                pltpu.VMEM((packed + bl + 8, cols), jnp.float32),
                pltpu.VMEM((tile_len // chunk, GR * bl, chunk), jnp.float32),
                pltpu.VMEM((GR * bl, 2 * HD), jnp.float32),
                pltpu.VMEM((GR * bl, HD), jnp.float32),
            ],
        ),
        out_shape=jax.ShapeDtypeStruct((nb, bl, width), jnp.bfloat16),
        compiler_params=pltpu.CompilerParams(vmem_limit_bytes=VMEM),
        cost_estimate=pl.CostEstimate(
            flops=4 * nb * bl * cols * tile_len,
            bytes_accessed=2 * nb * tile_len * heads * 2 * HD,
            transcendentals=nb * bl * heads * GR * tile_len,
        ),
        name="attend",
    )(meta, q, cache, own)


def shards(
    hidden_rows,
    carried,
    query_weight,
    response_cache,
    prompt_cache,
    prompt_lengths,
    response_lengths,
    block_prompts,
):
    section = lax.axis_index("sec")
    shard = lax.axis_index("seq")
    nb = lax.axis_size("seq")
    bl = hidden_rows.shape[1]
    local_kv = response_cache.shape[2] // (2 * HD)
    packed = nb * bl * 5 // 8
    share = packed // nb
    tile_len = prompt_cache.shape[2]
    cols = query_weight.shape[2]
    lengths = lax.dynamic_index_in_dim(response_lengths, section, 0, keepdims=False)
    prompts = lax.dynamic_index_in_dim(block_prompts, section, 0, keepdims=False)[:, 0]
    valid = jnp.clip(prompt_lengths[prompts] - shard * tile_len, 0, tile_len)
    offsets = jnp.cumsum(lengths) - lengths
    meta = jnp.concatenate([prompts, valid, offsets, shard[None]]).astype(jnp.int32)

    handed = from_behind(carried, "sec", 1)
    inputs = (hidden_rows[0].astype(jnp.float32) + handed[0].astype(jnp.float32)).astype(
        jnp.bfloat16
    )
    depth = query_weight.shape[1]
    slices = inputs.reshape(bl, nb, depth).transpose(1, 0, 2)
    x = lax.all_to_all(slices, "seq", split_axis=0, concat_axis=0, tiled=True)
    part = project(lengths, x.reshape(nb * bl, depth), query_weight[0], nb, bl, packed)
    part = (part * 0.125).astype(jnp.float16).reshape(nb, share, cols)
    part = lax.all_to_all(part, "seq", split_axis=0, concat_axis=0, tiled=True)
    mine = (jnp.sum(part.astype(jnp.float32), axis=0) * 8.0).astype(jnp.bfloat16)
    queries = lax.all_gather(mine, "seq", axis=0, tiled=True)
    out = attend(meta, queries, prompt_cache, response_cache[0], nb, bl, 0, local_kv)
    back = lax.all_to_all(out, "seq", split_axis=0, concat_axis=0, tiled=True)
    heads = local_kv * GR
    base = heads * HD
    terms = back[:, :, base:].astype(jnp.float32).reshape(nb, bl, 3, EXTRA)[:, :, :, :heads]
    lse = terms[:, :, 0] + terms[:, :, 1] + terms[:, :, 2]
    weight = jnp.exp2(lse - jnp.max(lse, axis=0, keepdims=True))
    weight = weight / jnp.sum(weight, axis=0, keepdims=True)
    values = back[:, :, :base].reshape(nb, bl, heads, HD).astype(jnp.float32)
    output = jnp.sum(values * weight[..., None], axis=0)
    order = jnp.arange(bl, dtype=jnp.int32)
    output = jnp.where((order < lengths[shard])[:, None, None], output, 0.0)
    return output.reshape(1, bl, base).astype(jnp.bfloat16)


def solution(mesh):
    placed = (
        P("sec", "seq", None),
        P("sec", "seq", None),
        P("sec", "seq", "tp"),
        P("sec", "seq", "tp"),
        P("sec", None, "seq", "tp"),
        P(),
        P(),
        P(),
    )
    return jax.shard_map(
        shards, mesh=mesh, in_specs=placed, out_specs=P("sec", "seq", "tp"), check_vma=False
    )
```

```python
import functools
import math

import jax
import jax.numpy as jnp
from jax import lax
from jax.experimental import pallas as pl
from jax.experimental.pallas import tpu as pltpu
from jax.sharding import PartitionSpec as P

HD = 128
GR = 4
NEG = -1e30
LOG2E = 1.4426950408889634
CHUNK = 512
LONG = 1024
ROUND = 16
EXTRA = 128
SLOT = 32
BIG = 2.0 ** 100
MIB = 1024 * 1024


def dot_nt(a, b):
    return lax.dot_general(a, b, (((1,), (1,)), ((), ())), preferred_element_type=jnp.float32)


class Grid:
    def __init__(self, count):
        self.n = count
        self.xs = 1 << ((count.bit_length() - 1) // 2)
        self.zs = count // self.xs

    def owner(self, shard, kx, kz):
        z, x = shard // self.xs, shard % self.xs
        return (z ^ kz) * self.xs + (x ^ kx)

    def swap(self, value, kx, kz):
        pairs = [(s, self.owner(s, kx, kz)) for s in range(self.n)]
        return lax.ppermute(value, "seq", pairs)


def split_kernel(grid, depth, place, hidden_ref, handed_ref, *out_refs):
    for kx in range(grid.xs):
        for kz in range(grid.zs):
            at = pl.multiple_of(grid.owner(place[1], kx, kz) * depth, HD)
            total = hidden_ref[0, :, pl.ds(at, depth)].astype(jnp.float32) + handed_ref[
                0, :, pl.ds(at, depth)
            ].astype(jnp.float32)
            out_refs[kx * grid.zs + kz][...] = total.astype(jnp.bfloat16)


def split(grid, place, hidden, handed, depth):
    bl = hidden.shape[1]
    if depth % HD:
        total = (hidden[0].astype(jnp.float32) + handed[0].astype(jnp.float32)).astype(jnp.bfloat16)
        return [
            lax.dynamic_slice_in_dim(total, grid.owner(place[1], kx, kz) * depth, depth, 1)
            for kx in range(grid.xs) for kz in range(grid.zs)
        ]
    whole = pl.BlockSpec(hidden.shape, lambda i, *m: (0, 0, 0))
    return pl.pallas_call(
        functools.partial(split_kernel, grid, depth),
        grid_spec=pltpu.PrefetchScalarGridSpec(
            num_scalar_prefetch=1,
            grid=(1,),
            in_specs=[whole, whole],
            out_specs=[pl.BlockSpec((bl, depth), lambda i, *m: (0, 0))] * grid.n,
        ),
        out_shape=[jax.ShapeDtypeStruct((bl, depth), jnp.bfloat16)] * grid.n,
        compiler_params=pltpu.CompilerParams(vmem_limit_bytes=16 * MIB),
        name="split",
    )(place, hidden, handed)


def project_kernel(grid, bl, share, place, lengths, *refs):
    x_refs, (w_ref, out_ref, xp_ref, starts) = refs[:grid.n], refs[grid.n:]

    @pl.when(pl.program_id(0) == 0)
    def _():
        section, shard = place[0], place[1]
        offset = jnp.int32(0)
        for b in range(grid.n):
            starts[b] = offset
            offset = offset + lengths[section, b]
        lane = lax.broadcasted_iota(jnp.int32, (8, grid.n * bl), 1)
        target = jnp.full(lane.shape, -1, jnp.int32)
        owners = [
            grid.owner(shard, kx, kz) for kx in range(grid.xs) for kz in range(grid.zs)
        ]
        for k, b in enumerate(owners):
            order = lane - k * bl
            used = (order >= 0) & (order < lengths[section, b])
            target = jnp.where(used, order + starts[b], target)
        row = lax.broadcasted_iota(jnp.int32, (share, grid.n * bl), 0)
        target = jnp.broadcast_to(target[:1], row.shape)
        picks = [jnp.where(row + b * share == target, 1.0, 0.0) for b in owners]
        pick = jnp.concatenate(picks, axis=0).astype(jnp.bfloat16)
        x = jnp.concatenate([ref[...] for ref in x_refs], axis=0)
        chosen = jnp.dot(pick, x, preferred_element_type=jnp.float32)
        xp_ref[...] = chosen.astype(jnp.bfloat16)

    result = jnp.dot(xp_ref[...], w_ref[...], preferred_element_type=jnp.float32)
    out_ref[...] = result.reshape(out_ref.shape)


def project(grid, place, lengths, xs, w, bl, share, chunks):
    k, cols = w.shape
    rows = grid.n * share
    tile = cols // chunks
    shape = (chunks, grid.xs, grid.zs * share, tile)
    return pl.pallas_call(
        functools.partial(project_kernel, grid, bl, share),
        grid_spec=pltpu.PrefetchScalarGridSpec(
            num_scalar_prefetch=2,
            grid=(chunks,),
            in_specs=[pl.BlockSpec((bl, k), lambda j, *m: (0, 0))] * grid.n
            + [pl.BlockSpec((k, tile), lambda j, *m: (0, j))],
            out_specs=pl.BlockSpec((1,) + shape[1:], lambda j, *m: (j, 0, 0, 0)),
            scratch_shapes=[
                pltpu.VMEM((rows, k), jnp.bfloat16), pltpu.SMEM((grid.n,), jnp.int32)
            ],
        ),
        out_shape=jax.ShapeDtypeStruct(shape, jnp.float32),
        compiler_params=pltpu.CompilerParams(vmem_limit_bytes=32 * MIB),
        cost_estimate=pl.CostEstimate(
            flops=2 * rows * k * cols, bytes_accessed=2 * k * cols + 4 * rows * cols,
            transcendentals=0,
        ),
        name="project",
    )(place, lengths, *xs, w)


def encode(lse):
    lane = lax.broadcasted_iota(jnp.int32, lse.shape, 1)
    high = lse.astype(jnp.bfloat16).astype(jnp.float32)
    rest = lse - high
    mid = rest.astype(jnp.bfloat16).astype(jnp.float32)
    low = rest - mid
    return jnp.where(lane < SLOT, high, jnp.where(lane < 2 * SLOT, mid, low)).astype(jnp.bfloat16)


def decode(tile):
    terms = tile.astype(jnp.float32)
    return terms + pltpu.roll(terms, EXTRA - SLOT, 1) + pltpu.roll(terms, EXTRA - 2 * SLOT, 1)


def merge(values, lses, heads):
    bl = lses[0].shape[0]
    lane = lax.broadcasted_iota(jnp.int32, lses[0].shape, 1)
    peak = functools.reduce(jnp.maximum, lses)
    weights = [jnp.exp2(lse - peak) for lse in lses]
    total = functools.reduce(jnp.add, weights)
    weights = [weight / total for weight in weights]
    merged = peak + jnp.log2(total)
    out = []
    spread = jnp.zeros((bl, EXTRA), jnp.float32)
    for h in range(heads):
        terms = [
            jnp.broadcast_to(weight[:, h:h + 1], (bl, HD)) * value(h).astype(jnp.float32)
            for weight, value in zip(weights, values)
        ]
        out.append(functools.reduce(jnp.add, terms))
        spread = jnp.where(lane % SLOT == h, merged[:, h:h + 1], spread)
    return out, spread


def attend_kernel(grid, kx, bl, share, heads, tile_len, *refs):
    place, lengths, prompts, prompt_lengths = refs[:4]
    refs = refs[4:]
    near_ref, refs = refs[0], refs[1:]
    far_refs, refs = refs[:grid.xs - 1], refs[grid.xs - 1:]
    kv_refs, refs = refs[:heads], refs[heads:]
    own_ref, refs = refs[0], refs[1:]
    met = grid.xs - 1 if kx == 0 else 0
    met_refs, refs = refs[:met], refs[met:]
    outs = grid.zs if kx == 0 else 1
    out_refs, refs = refs[:outs], refs[outs:]
    q32_ref, acc_ref, m_ref = refs

    step = pl.program_id(0)
    section, shard = place[0], place[1]
    rows = grid.n * share
    block = grid.owner(shard, kx, step)
    offset = jnp.int32(0)
    for b in range(grid.n):
        offset = offset + jnp.where(b < block, lengths[section, b], 0)
    valid = jnp.clip(
        prompt_lengths[prompts[section, block]] - shard * tile_len, 0, tile_len
    )
    c2 = LOG2E / math.sqrt(HD)
    chunk = min(CHUNK, tile_len)
    width = heads * GR * HD

    @pl.when(step == 0)
    def _():
        for fx in range(grid.xs):
            for fz in range(grid.zs):
                source = near_ref if fx == 0 else far_refs[fx - 1]
                at = pl.multiple_of(grid.owner(shard, fx, fz) * share, 8)
                q32_ref[pl.ds(at, share), :] = source[fz].astype(jnp.float32)
        q32_ref[rows:, :] = jnp.zeros((bl + 8, width), jnp.float32)

    rest = offset % 8
    window = q32_ref[pl.ds(pl.multiple_of(offset - rest, 8), bl + 8), :]
    window = pltpu.roll(window, jnp.where(rest == 0, 0, bl + 8 - rest), 0)
    queries = window[:bl].astype(jnp.bfloat16)

    def group(g, used):
        return jnp.concatenate(
            [queries[:used, (g * GR + r) * HD:(g * GR + r + 1) * HD] for r in range(GR)], axis=0
        )

    def with_ones(v):
        return jnp.concatenate([v, jnp.ones(v.shape, jnp.bfloat16)], axis=1)

    def sums(p, v):
        return jnp.dot(p, with_ones(v), preferred_element_type=jnp.float32)

    def keys(g, at, size):
        return kv_refs[g][0, 0, pl.ds(at, size), :HD]

    def vals(g, at, size):
        return kv_refs[g][0, 0, pl.ds(at, size), HD:]

    def put(g, used, acc, m):
        m = jnp.broadcast_to(m, (GR * used, HD))
        for r in range(GR):
            acc_ref[g, r * bl:r * bl + used] = acc[r * used:(r + 1) * used]
            m_ref[g, r * bl:r * bl + used] = m[r * used:(r + 1) * used]

    def update(g, s, seen, v):
        s = jnp.where(seen, s, NEG)
        before = m_ref[g][:, :1]
        m = jnp.maximum(before, jnp.max(s, axis=1, keepdims=True))
        p = jnp.where(seen, jnp.exp2((s - m) * c2), 0.0).astype(jnp.bfloat16)
        acc_ref[g] = acc_ref[g] * jnp.exp2((before - m) * c2) + sums(p, v)
        m_ref[g] = jnp.broadcast_to(m, m_ref.shape[1:])

    def exact():
        acc_ref[...] = jnp.zeros_like(acc_ref)
        m_ref[...] = jnp.full_like(m_ref, NEG)

        def one(c, carry):
            at = pl.multiple_of(c * chunk, chunk)
            for g in range(heads):
                s = dot_nt(group(g, bl), keys(g, at, chunk))
                here = lax.broadcasted_iota(jnp.int32, s.shape, 1) + at
                update(g, s, here < valid, vals(g, at, chunk))
            return carry

        lax.fori_loop(0, (valid + chunk - 1) // chunk, one, 0)

    length = lengths[section, block]
    acc_ref[...] = jnp.zeros_like(acc_ref)
    m_ref[...] = jnp.full_like(m_ref, NEG)

    long = min(LONG, tile_len)
    for used in range(ROUND, bl + 1, ROUND):
        @pl.when((valid == tile_len) & (length <= used) & (length > used - ROUND))
        def _(used=used):
            items = [(g, c) for g in range(heads) for c in range(tile_len // long)]
            q = [group(g, used) for g in range(heads)]
            peaks = [None] * heads
            accs = [None] * heads
            ahead = dot_nt(q[0], keys(0, 0, long))
            for i, (g, c) in enumerate(items):
                s = ahead
                if i + 1 < len(items):
                    ng, nc = items[i + 1]
                    ahead = dot_nt(q[ng], keys(ng, nc * long, long))
                if c == 0:
                    peaks[g] = jnp.max(s, axis=1, keepdims=True)
                p = jnp.exp2((s - peaks[g]) * c2).astype(jnp.bfloat16)
                part = sums(p, vals(g, c * long, long))
                accs[g] = part if c == 0 else accs[g] + part
            for g in range(heads):
                put(g, used, accs[g], peaks[g])

    @pl.when((valid < tile_len) & (valid > 0))
    def _():
        def scores(g, at):
            s = dot_nt(group(g, bl), keys(g, at, chunk))
            here = lax.broadcasted_iota(jnp.int32, s.shape, 1) + at
            return jnp.where(here < valid, s, NEG)

        for g in range(heads):
            s = scores(g, 0)
            m = jnp.max(s, axis=1, keepdims=True)
            p = jnp.exp2((s - m) * c2).astype(jnp.bfloat16)
            put(g, bl, sums(p, vals(g, 0, chunk)), m)

        def one(c, carry):
            at = pl.multiple_of(c * chunk, chunk)
            for g in range(heads):
                p = jnp.exp2((scores(g, at) - m_ref[g][:, :1]) * c2).astype(jnp.bfloat16)
                acc_ref[g] += sums(p, vals(g, at, chunk))
            return carry

        lax.fori_loop(1, (valid + chunk - 1) // chunk, one, 0)

    top = jnp.where(acc_ref[:, :, HD:] < BIG, 0.0, 1.0)

    @pl.when(jnp.max(top) > 0.5)
    def _():
        exact()

    if kx == 0:
        @pl.when(step == 0)
        def _():
            for g in range(heads):
                base = g * 2 * HD
                s = dot_nt(group(g, bl), own_ref[:, base:base + HD])
                row = lax.broadcasted_iota(jnp.int32, s.shape, 0) % bl
                col = lax.broadcasted_iota(jnp.int32, s.shape, 1)
                update(g, s, col <= row, own_ref[:, base + HD:base + 2 * HD])

    lane = lax.broadcasted_iota(jnp.int32, (bl, EXTRA), 1)
    lse_tile = jnp.zeros((bl, EXTRA), jnp.float32)
    parts = []
    for g in range(heads):
        total = acc_ref[g][:, HD:]
        some = total > 0.0
        safe = jnp.where(some, total, 1.0)
        out = acc_ref[g][:, :HD] / safe
        lse = jnp.where(some, m_ref[g] * c2 + jnp.log2(safe), NEG)
        for r in range(GR):
            h = g * GR + r
            parts.append(out[r * bl:(r + 1) * bl])
            lse_tile = jnp.where(lane % SLOT == h, lse[r * bl:(r + 1) * bl], lse_tile)
    if met:
        values = [lambda h: parts[h]]
        lses = [lse_tile]
        for met_ref in met_refs:
            values.append(lambda h, met_ref=met_ref: met_ref[0, :, h * HD:(h + 1) * HD])
            lses.append(decode(met_ref[0, :, width:]))
        parts, lse_tile = merge(values, lses, heads * GR)
    terms = encode(lse_tile)

    def write(out_ref, lead):
        for h in range(heads * GR):
            out_ref[lead + (slice(None), slice(h * HD, (h + 1) * HD))] = parts[h].astype(
                jnp.bfloat16
            )
        out_ref[lead + (slice(None), slice(width, width + EXTRA))] = terms

    if kx == 0:
        for kz in range(grid.zs):
            @pl.when(step == kz)
            def _():
                write(out_refs[kz], ())
    else:
        write(out_refs[0], (0,))


def attend(grid, kx, place, lengths, prompts, prompt_lengths, near, fars, cache, own, mets, first,
           heads):
    zs, share, cols = near.shape
    bl = own.shape[0]
    tile_len = cache.shape[2]
    width = heads * GR * HD + EXTRA

    def cache_at(head):
        def index(i, place, lengths, prompts, prompt_lengths):
            section, shard = place[0], place[1]
            at = prompts[section, grid.owner(shard, kx, 0)]
            for kz in range(1, zs):
                prompt = prompts[section, grid.owner(shard, kx, kz)]
                here = (kz <= i) & (prompt_lengths[prompt] > shard * tile_len)
                at = jnp.where(here, prompt, at)
            return (0, at, 0, first + head)

        return pl.BlockSpec((1, 1, tile_len, 2 * HD), index)

    piece = jax.ShapeDtypeStruct((bl, width), jnp.bfloat16)
    if kx == 0:
        out_shape = [piece] * zs
        out_specs = [pl.BlockSpec((bl, width), lambda i, *m: (0, 0))] * zs
    else:
        out_shape = jax.ShapeDtypeStruct((zs, bl, width), jnp.bfloat16)
        out_specs = pl.BlockSpec((1, bl, width), lambda i, *m: (i, 0, 0))
    return pl.pallas_call(
        functools.partial(attend_kernel, grid, kx, bl, share, heads, tile_len),
        grid_spec=pltpu.PrefetchScalarGridSpec(
            num_scalar_prefetch=4,
            grid=(zs,),
            in_specs=[pl.BlockSpec((zs, share, cols), lambda i, *m: (0, 0, 0))] * grid.xs
            + [cache_at(head) for head in range(heads)]
            + [pl.BlockSpec((bl, heads * 2 * HD), lambda i, *m: (0, first // heads))]
            + [pl.BlockSpec((1, bl, width), lambda i, *m: (i, 0, 0))] * len(mets),
            out_specs=out_specs,
            scratch_shapes=[
                pltpu.VMEM((grid.n * share + bl + 8, cols), jnp.float32),
                pltpu.VMEM((heads, GR * bl, 2 * HD), jnp.float32),
                pltpu.VMEM((heads, GR * bl, HD), jnp.float32),
            ],
        ),
        out_shape=out_shape,
        compiler_params=pltpu.CompilerParams(vmem_limit_bytes=40 * MIB),
        cost_estimate=pl.CostEstimate(
            flops=8 * zs * bl * cols * tile_len,
            bytes_accessed=2 * zs * tile_len * heads * 2 * HD,
            transcendentals=zs * bl * heads * GR * tile_len,
        ),
        name="attend",
    )(place, lengths, prompts, prompt_lengths, near, *fars, *([cache] * heads), own, *mets)


def finish_kernel(chunks, zs, heads, bl, place, lengths, *refs):
    out_ref = refs[-1]
    length = lengths[place[0], place[1]]
    row = lax.broadcasted_iota(jnp.int32, (bl, HD), 0)
    width = heads * GR * HD
    for c in range(chunks):
        pieces = refs[c * zs:(c + 1) * zs]
        values = [lambda h, ref=ref: ref[:, h * HD:(h + 1) * HD] for ref in pieces]
        lses = [decode(ref[:, width:]) for ref in pieces]
        parts, _ = merge(values, lses, heads * GR)
        for h in range(heads * GR):
            at = c * width + h * HD
            out_ref[0, :, at:at + HD] = jnp.where(row < length, parts[h], 0.0).astype(jnp.bfloat16)


def finish(place, lengths, pieces, chunks, zs, heads):
    bl = pieces[0].shape[0]
    cols = chunks * heads * GR * HD
    return pl.pallas_call(
        functools.partial(finish_kernel, chunks, zs, heads, bl),
        grid_spec=pltpu.PrefetchScalarGridSpec(
            num_scalar_prefetch=2,
            grid=(1,),
            in_specs=[pl.BlockSpec(piece.shape, lambda i, *m: (0, 0)) for piece in pieces],
            out_specs=pl.BlockSpec((1, bl, cols), lambda i, *m: (0, 0, 0)),
        ),
        out_shape=jax.ShapeDtypeStruct((1, bl, cols), jnp.bfloat16),
        compiler_params=pltpu.CompilerParams(vmem_limit_bytes=16 * MIB),
        name="finish",
    )(place, lengths, *pieces)


def shards(
    hidden_rows,
    carried,
    query_weight,
    response_cache,
    prompt_cache,
    prompt_lengths,
    response_lengths,
    block_prompts,
):
    grid = Grid(lax.axis_size("seq"))
    bl = hidden_rows.shape[1]
    local_kv = response_cache.shape[2] // (2 * HD)
    share = bl * 5 // 8
    chunks = 2 if local_kv % 2 == 0 else 1
    heads = local_kv // chunks
    part_cols = heads * GR * HD
    place = jnp.stack([lax.axis_index("sec"), lax.axis_index("seq")]).astype(jnp.int32)
    prompts = block_prompts[:, :, 0]

    handed = lax.ppermute(carried, "sec", [(0, 1)])
    depth = query_weight.shape[1]
    slices = split(grid, place, hidden_rows, handed, depth)
    x = [grid.swap(piece, k // grid.zs, k % grid.zs) if k else piece for k, piece in enumerate(slices)]
    part = project(grid, place, response_lengths, x, query_weight[0], bl, share, chunks)
    part = part.reshape(chunks, grid.xs, grid.zs, share, part_cols)

    def narrow(value):
        return (value * 0.125).astype(jnp.float16)

    def widen(value):
        return value.astype(jnp.float32) * 8.0

    def after(value, done):
        return lax.optimization_barrier((value, done))[0]

    def sum_x(c, done):
        parts = [part[c, kx] for kx in range(grid.xs)]
        got = [grid.swap(after(narrow(parts[kx]), done), kx, 0) for kx in range(1, grid.xs)]
        return functools.reduce(jnp.add, [parts[0]] + [widen(value) for value in got]), got

    def sum_z(held, done):
        got = [grid.swap(after(narrow(held[kz]), done), 0, kz) for kz in range(1, grid.zs)]
        total = functools.reduce(jnp.add, [held[0]] + [widen(value) for value in got])
        return total.astype(jnp.bfloat16)

    def gather_z(mine):
        return [mine] + [grid.swap(mine, 0, kz) for kz in range(1, grid.zs)]

    def gather_x(near):
        return [near] + [grid.swap(near, kx, 0) for kx in range(1, grid.xs)]

    def call(c, kx, queries, mets):
        return attend(
            grid, kx, place, response_lengths, prompts, prompt_lengths, queries[0], queries[1:],
            prompt_cache, response_cache[0], mets, c * heads, heads,
        )

    queries = [None] * chunks
    sent = [[] for _ in range(chunks)]
    held, got = sum_x(0, ())
    mine = sum_z(held, ())
    column = gather_z(mine)
    near = jnp.stack(column)
    if chunks > 1:
        held, _ = sum_x(1, got)
        mine = sum_z(held, column)
    queries[0] = gather_x(near)
    if chunks > 1:
        column = gather_z(mine)
        queries[0][0] = after(queries[0][0], mine)
    for kx in range(1, grid.xs):
        out = call(0, kx, queries[0], [])
        sent[0].append(grid.swap(out, kx, 0))
    if chunks > 1:
        near = jnp.stack(after(column, out))
        queries[1] = gather_x(near)
        queries[0][0] = after(queries[0][0], near)
        for kx in range(1, grid.xs):
            sent[1].append(None)
    pieces = []
    for c in range(chunks):
        if c:
            for kx in range(1, grid.xs):
                sent[c][kx - 1] = grid.swap(call(c, kx, queries[c], []), kx, 0)
        held = call(c, 0, queries[c], sent[c])
        pieces.append(held[0])
        pieces.extend(grid.swap(held[kz], 0, kz) for kz in range(1, grid.zs))
    return finish(place, response_lengths, pieces, chunks, grid.zs, heads)


def solution(mesh):
    placed = (
        P("sec", "seq", None),
        P("sec", "seq", None),
        P("sec", "seq", "tp"),
        P("sec", "seq", "tp"),
        P("sec", None, "seq", "tp"),
        P(),
        P(),
        P(),
    )
    return jax.shard_map(
        shards, mesh=mesh, in_specs=placed, out_specs=P("sec", "seq", "tp"), check_vma=False
    )
```

```python
import functools
import math

import jax
import jax.numpy as jnp
from jax import lax
from jax.experimental import pallas as pl
from jax.experimental.pallas import tpu as pltpu
from jax.sharding import PartitionSpec as P

HD = 128
GR = 4
NEG = -1e30
LOG2E = 1.4426950408889634
CHUNK = 512
LONG = 1024
ROUND = 16
EXTRA = 128
SLOT = 32
BIG = 2.0 ** 100
MIB = 1024 * 1024


def dot_nt(a, b):
    return lax.dot_general(a, b, (((1,), (1,)), ((), ())), preferred_element_type=jnp.float32)


class Grid:
    def __init__(self, count):
        self.n = count
        self.xs = 1 << ((count.bit_length() - 1) // 2)
        self.zs = count // self.xs

    def owner(self, shard, kx, kz):
        z, x = shard // self.xs, shard % self.xs
        return (z ^ kz) * self.xs + (x ^ kx)

    def swap(self, value, kx, kz):
        pairs = [(s, self.owner(s, kx, kz)) for s in range(self.n)]
        return lax.ppermute(value, "seq", pairs)


def split_kernel(grid, depth, place, hidden_ref, handed_ref, *out_refs):
    for kx in range(grid.xs):
        for kz in range(grid.zs):
            at = pl.multiple_of(grid.owner(place[1], kx, kz) * depth, HD)
            total = hidden_ref[0, :, pl.ds(at, depth)].astype(jnp.float32) + handed_ref[
                0, :, pl.ds(at, depth)
            ].astype(jnp.float32)
            out_refs[kx * grid.zs + kz][...] = total.astype(jnp.bfloat16)


def split(grid, place, hidden, handed, depth):
    bl = hidden.shape[1]
    if depth % HD:
        total = (hidden[0].astype(jnp.float32) + handed[0].astype(jnp.float32)).astype(jnp.bfloat16)
        return [
            lax.dynamic_slice_in_dim(total, grid.owner(place[1], kx, kz) * depth, depth, 1)
            for kx in range(grid.xs) for kz in range(grid.zs)
        ]
    whole = pl.BlockSpec(hidden.shape, lambda i, *m: (0, 0, 0))
    return pl.pallas_call(
        functools.partial(split_kernel, grid, depth),
        grid_spec=pltpu.PrefetchScalarGridSpec(
            num_scalar_prefetch=1,
            grid=(1,),
            in_specs=[whole, whole],
            out_specs=[pl.BlockSpec((bl, depth), lambda i, *m: (0, 0))] * grid.n,
        ),
        out_shape=[jax.ShapeDtypeStruct((bl, depth), jnp.bfloat16)] * grid.n,
        compiler_params=pltpu.CompilerParams(vmem_limit_bytes=16 * MIB),
        name="split",
    )(place, hidden, handed)


def fetch_kernel(chunk, width, first, place, prompts, prompt_lengths, cache_ref, *refs):
    plain = (len(refs) - 3) // 2
    sources, (kv_ref, *copies), (kv_sem, sem) = refs[:plain], refs[plain:-2], refs[-2:]
    count, tile_len = kv_ref.shape[:2]
    section, shard = place[0], place[1]
    moves = [
        (None, pltpu.make_async_copy(source, copy, sem.at[i]))
        for i, (source, copy) in enumerate(zip(sources, copies))
    ]
    for p in range(count if first is not None else 0):
        asked = prompts[section, 0] == p
        for b in range(1, prompts.shape[1]):
            asked = asked | (prompts[section, b] == p)
        for c in range(tile_len // chunk):
            at = pl.ds(c * chunk, chunk)
            needed = asked & (prompt_lengths[p] > shard * tile_len + c * chunk)
            moves.append((needed, pltpu.make_async_copy(
                cache_ref.at[0, p, at, pl.ds(first * width, width)], kv_ref.at[p, at],
                kv_sem.at[p, c],
            )))
    for needed, move in moves:
        if needed is None:
            move.start()
        else:
            pl.when(needed)(move.start)
    for needed, move in moves:
        if needed is None:
            move.wait()
        else:
            pl.when(needed)(move.wait)


def fetch(place, prompts, prompt_lengths, cache, width, first, plain):
    count, tile_len = cache.shape[1:3]
    chunk = min(CHUNK, tile_len)
    shape = (count, tile_len, width) if first is not None else (1, 16, HD)
    anywhere, near = pl.BlockSpec(memory_space=pltpu.HBM), pl.BlockSpec(memory_space=pltpu.VMEM)
    size = math.prod(shape) + sum(math.prod(array.shape) for array in plain)
    return pl.pallas_call(
        functools.partial(fetch_kernel, chunk, width, first),
        grid_spec=pltpu.PrefetchScalarGridSpec(
            num_scalar_prefetch=3,
            grid=(1,),
            in_specs=[anywhere] * (1 + len(plain)),
            out_specs=[near] * (1 + len(plain)),
            scratch_shapes=[
                pltpu.SemaphoreType.DMA((count, tile_len // chunk)),
                pltpu.SemaphoreType.DMA((len(plain) + 1,)),
            ],
        ),
        out_shape=[pltpu.VMEM(shape, cache.dtype)]
        + [pltpu.VMEM(array.shape, array.dtype) for array in plain],
        compiler_params=pltpu.CompilerParams(vmem_limit_bytes=4 * MIB),
        cost_estimate=pl.CostEstimate(flops=0, bytes_accessed=2 * size, transcendentals=0),
        name="fetch",
    )(
        place, prompts, prompt_lengths,
        *[pltpu.with_memory_space_constraint(array, pltpu.HBM) for array in (cache, *plain)],
    )


def project_kernel(grid, bl, share, place, lengths, *refs):
    x_refs, w_ref, refs = refs[:grid.n], refs[grid.n], refs[grid.n + 1:]
    out_refs, (xp_ref, starts) = refs[:-2], refs[-2:]

    @pl.when(pl.program_id(0) == 0)
    def _():
        section, shard = place[0], place[1]
        offset = jnp.int32(0)
        for b in range(grid.n):
            starts[b] = offset
            offset = offset + lengths[section, b]
        lane = lax.broadcasted_iota(jnp.int32, (8, grid.n * bl), 1)
        target = jnp.full(lane.shape, -1, jnp.int32)
        owners = [
            grid.owner(shard, kx, kz) for kx in range(grid.xs) for kz in range(grid.zs)
        ]
        for k, b in enumerate(owners):
            order = lane - k * bl
            used = (order >= 0) & (order < lengths[section, b])
            target = jnp.where(used, order + starts[b], target)
        row = lax.broadcasted_iota(jnp.int32, (share, grid.n * bl), 0)
        target = jnp.broadcast_to(target[:1], row.shape)
        picks = [jnp.where(row + b * share == target, 1.0, 0.0) for b in owners]
        pick = jnp.concatenate(picks, axis=0).astype(jnp.bfloat16)
        x = jnp.concatenate([ref[...] for ref in x_refs], axis=0)
        chosen = jnp.dot(pick, x, preferred_element_type=jnp.float32)
        xp_ref[...] = chosen.astype(jnp.bfloat16)

    result = jnp.dot(xp_ref[...], w_ref[0], preferred_element_type=jnp.float32)
    rows = grid.zs * share
    for i, out_ref in enumerate(out_refs):
        chunk, kx = i // grid.xs, i % grid.xs

        @pl.when(pl.program_id(0) == chunk)
        def _(out_ref=out_ref, kx=kx):
            out_ref[...] = result[kx * rows:(kx + 1) * rows]


def project(grid, place, lengths, xs, w, bl, share, chunks):
    k, cols = w.shape[1:]
    rows = grid.n * share
    tile = cols // chunks
    piece = (grid.zs * share, tile)
    return pl.pallas_call(
        functools.partial(project_kernel, grid, bl, share),
        grid_spec=pltpu.PrefetchScalarGridSpec(
            num_scalar_prefetch=2,
            grid=(chunks,),
            in_specs=[pl.BlockSpec((bl, k), lambda j, *m: (0, 0))] * grid.n
            + [pl.BlockSpec((1, k, tile), lambda j, *m: (0, 0, j))],
            out_specs=[pl.BlockSpec(piece, lambda j, *m: (0, 0))] * (chunks * grid.xs),
            scratch_shapes=[
                pltpu.VMEM((rows, k), jnp.bfloat16), pltpu.SMEM((grid.n,), jnp.int32)
            ],
        ),
        out_shape=[jax.ShapeDtypeStruct(piece, jnp.float32)] * (chunks * grid.xs),
        compiler_params=pltpu.CompilerParams(vmem_limit_bytes=20 * MIB),
        cost_estimate=pl.CostEstimate(
            flops=2 * rows * k * cols, bytes_accessed=2 * k * cols + 4 * rows * cols,
            transcendentals=0,
        ),
        name="project",
    )(place, lengths, *xs, w)


def encode(lse):
    lane = lax.broadcasted_iota(jnp.int32, lse.shape, 1)
    high = lse.astype(jnp.bfloat16).astype(jnp.float32)
    rest = lse - high
    mid = rest.astype(jnp.bfloat16).astype(jnp.float32)
    low = rest - mid
    return jnp.where(lane < SLOT, high, jnp.where(lane < 2 * SLOT, mid, low)).astype(jnp.bfloat16)


def decode(tile):
    terms = tile.astype(jnp.float32)
    return terms + pltpu.roll(terms, EXTRA - SLOT, 1) + pltpu.roll(terms, EXTRA - 2 * SLOT, 1)


def merge(values, lses, heads):
    bl = lses[0].shape[0]
    lane = lax.broadcasted_iota(jnp.int32, lses[0].shape, 1)
    peak = functools.reduce(jnp.maximum, lses)
    weights = [jnp.exp2(lse - peak) for lse in lses]
    total = functools.reduce(jnp.add, weights)
    weights = [weight / total for weight in weights]
    merged = peak + jnp.log2(total)
    out = []
    spread = jnp.zeros((bl, EXTRA), jnp.float32)
    for h in range(heads):
        terms = [
            jnp.broadcast_to(weight[:, h:h + 1], (bl, HD)) * value(h).astype(jnp.float32)
            for weight, value in zip(weights, values)
        ]
        out.append(functools.reduce(jnp.add, terms))
        spread = jnp.where(lane % SLOT == h, merged[:, h:h + 1], spread)
    return out, spread


def attend_kernel(grid, kx, bl, share, heads, tile_len, *refs):
    place, lengths, prompts, prompt_lengths = refs[:4]
    refs = refs[4:]
    near_ref, refs = refs[0], refs[1:]
    far_refs, refs = refs[:grid.xs - 1], refs[grid.xs - 1:]
    kv_ref, refs = refs[0], refs[1:]
    own_ref, refs = refs[0], refs[1:]
    met = grid.xs - 1 if kx == 0 else 0
    met_refs, refs = refs[:met], refs[met:]
    outs = grid.zs if kx == 0 else 1
    out_refs, refs = refs[:outs], refs[outs:]
    q32_ref, acc_ref, m_ref = refs

    step = pl.program_id(0)
    section, shard = place[0], place[1]
    rows = grid.n * share
    block = grid.owner(shard, kx, step)
    offset = jnp.int32(0)
    for b in range(grid.n):
        offset = offset + jnp.where(b < block, lengths[section, b], 0)
    prompt = prompts[section, block]
    valid = jnp.clip(prompt_lengths[prompt] - shard * tile_len, 0, tile_len)
    c2 = LOG2E / math.sqrt(HD)
    chunk = min(CHUNK, tile_len)
    width = heads * GR * HD

    @pl.when(step == 0)
    def _():
        for fx in range(grid.xs):
            for fz in range(grid.zs):
                source = near_ref if fx == 0 else far_refs[fx - 1]
                at = pl.multiple_of(grid.owner(shard, fx, fz) * share, 8)
                q32_ref[pl.ds(at, share), :] = source[fz].astype(jnp.float32)
        q32_ref[rows:, :] = jnp.zeros((bl + 8, width), jnp.float32)

    rest = offset % 8
    window = q32_ref[pl.ds(pl.multiple_of(offset - rest, 8), bl + 8), :]
    window = pltpu.roll(window, jnp.where(rest == 0, 0, bl + 8 - rest), 0)
    queries = window[:bl].astype(jnp.bfloat16)

    def group(g, used):
        return jnp.concatenate(
            [queries[:used, (g * GR + r) * HD:(g * GR + r + 1) * HD] for r in range(GR)], axis=0
        )

    def with_ones(v):
        return jnp.concatenate([v, jnp.ones(v.shape, jnp.bfloat16)], axis=1)

    def sums(p, v):
        return jnp.dot(p, with_ones(v), preferred_element_type=jnp.float32)

    def keys(g, at, size):
        return kv_ref[prompt, pl.ds(at, size), pl.ds(g * 2 * HD, HD)]

    def vals(g, at, size):
        return kv_ref[prompt, pl.ds(at, size), pl.ds(g * 2 * HD + HD, HD)]

    def put(g, used, acc, m):
        m = jnp.broadcast_to(m, (GR * used, HD))
        for r in range(GR):
            acc_ref[g, r * bl:r * bl + used] = acc[r * used:(r + 1) * used]
            m_ref[g, r * bl:r * bl + used] = m[r * used:(r + 1) * used]

    def update(g, s, seen, v):
        s = jnp.where(seen, s, NEG)
        before = m_ref[g][:, :1]
        m = jnp.maximum(before, jnp.max(s, axis=1, keepdims=True))
        p = jnp.where(seen, jnp.exp2((s - m) * c2), 0.0).astype(jnp.bfloat16)
        acc_ref[g] = acc_ref[g] * jnp.exp2((before - m) * c2) + sums(p, v)
        m_ref[g] = jnp.broadcast_to(m, m_ref.shape[1:])

    def exact():
        acc_ref[...] = jnp.zeros_like(acc_ref)
        m_ref[...] = jnp.full_like(m_ref, NEG)

        def one(c, carry):
            at = pl.multiple_of(c * chunk, chunk)
            for g in range(heads):
                s = dot_nt(group(g, bl), keys(g, at, chunk))
                here = lax.broadcasted_iota(jnp.int32, s.shape, 1) + at
                update(g, s, here < valid, vals(g, at, chunk))
            return carry

        lax.fori_loop(0, (valid + chunk - 1) // chunk, one, 0)

    length = lengths[section, block]
    acc_ref[...] = jnp.zeros_like(acc_ref)
    m_ref[...] = jnp.full_like(m_ref, NEG)

    long = min(LONG, tile_len)
    for used in range(ROUND, bl + 1, ROUND):
        @pl.when((valid == tile_len) & (length <= used) & (length > used - ROUND))
        def _(used=used):
            items = [(g, c) for g in range(heads) for c in range(tile_len // long)]
            q = [group(g, used) for g in range(heads)]
            peaks = [None] * heads
            accs = [None] * heads
            ahead = dot_nt(q[0], keys(0, 0, long))
            for i, (g, c) in enumerate(items):
                s = ahead
                if i + 1 < len(items):
                    ng, nc = items[i + 1]
                    ahead = dot_nt(q[ng], keys(ng, nc * long, long))
                if c == 0:
                    peaks[g] = jnp.max(s, axis=1, keepdims=True)
                p = jnp.exp2((s - peaks[g]) * c2).astype(jnp.bfloat16)
                part = sums(p, vals(g, c * long, long))
                accs[g] = part if c == 0 else accs[g] + part
            for g in range(heads):
                put(g, used, accs[g], peaks[g])

    @pl.when((valid < tile_len) & (valid > 0))
    def _():
        def scores(g, at):
            s = dot_nt(group(g, bl), keys(g, at, chunk))
            here = lax.broadcasted_iota(jnp.int32, s.shape, 1) + at
            return jnp.where(here < valid, s, NEG)

        for g in range(heads):
            s = scores(g, 0)
            m = jnp.max(s, axis=1, keepdims=True)
            p = jnp.exp2((s - m) * c2).astype(jnp.bfloat16)
            put(g, bl, sums(p, vals(g, 0, chunk)), m)

        def one(c, carry):
            at = pl.multiple_of(c * chunk, chunk)
            for g in range(heads):
                p = jnp.exp2((scores(g, at) - m_ref[g][:, :1]) * c2).astype(jnp.bfloat16)
                acc_ref[g] += sums(p, vals(g, at, chunk))
            return carry

        lax.fori_loop(1, (valid + chunk - 1) // chunk, one, 0)

    top = jnp.where(acc_ref[:, :, HD:] < BIG, 0.0, 1.0)

    @pl.when(jnp.max(top) > 0.5)
    def _():
        exact()

    if kx == 0:
        @pl.when(step == 0)
        def _():
            for g in range(heads):
                base = g * 2 * HD
                s = dot_nt(group(g, bl), own_ref[0, :, base:base + HD])
                row = lax.broadcasted_iota(jnp.int32, s.shape, 0) % bl
                col = lax.broadcasted_iota(jnp.int32, s.shape, 1)
                update(g, s, col <= row, own_ref[0, :, base + HD:base + 2 * HD])

    lane = lax.broadcasted_iota(jnp.int32, (bl, EXTRA), 1)
    lse_tile = jnp.zeros((bl, EXTRA), jnp.float32)
    parts = []
    for g in range(heads):
        total = acc_ref[g][:, HD:]
        some = total > 0.0
        safe = jnp.where(some, total, 1.0)
        out = acc_ref[g][:, :HD] / safe
        lse = jnp.where(some, m_ref[g] * c2 + jnp.log2(safe), NEG)
        for r in range(GR):
            h = g * GR + r
            parts.append(out[r * bl:(r + 1) * bl])
            lse_tile = jnp.where(lane % SLOT == h, lse[r * bl:(r + 1) * bl], lse_tile)
    if met:
        values = [lambda h: parts[h]]
        lses = [lse_tile]
        for met_ref in met_refs:
            values.append(lambda h, met_ref=met_ref: met_ref[0, :, h * HD:(h + 1) * HD])
            lses.append(decode(met_ref[0, :, width:]))
        parts, lse_tile = merge(values, lses, heads * GR)
    terms = encode(lse_tile)

    def write(out_ref, lead):
        for h in range(heads * GR):
            out_ref[lead + (slice(None), slice(h * HD, (h + 1) * HD))] = parts[h].astype(
                jnp.bfloat16
            )
        out_ref[lead + (slice(None), slice(width, width + EXTRA))] = terms

    if kx == 0:
        for kz in range(grid.zs):
            @pl.when(step == kz)
            def _():
                write(out_refs[kz], ())
    else:
        write(out_refs[0], (0,))


def attend(grid, kx, place, lengths, prompts, prompt_lengths, near, fars, cache, own, mets, first,
           heads):
    zs, share, cols = near.shape
    bl = own.shape[1]
    tile_len = cache.shape[1]
    width = heads * GR * HD + EXTRA

    piece = jax.ShapeDtypeStruct((bl, width), jnp.bfloat16)
    if kx == 0:
        out_shape = [piece] * zs
        out_specs = [pl.BlockSpec((bl, width), lambda i, *m: (0, 0))] * zs
    else:
        out_shape = jax.ShapeDtypeStruct((zs, bl, width), jnp.bfloat16)
        out_specs = pl.BlockSpec((1, bl, width), lambda i, *m: (i, 0, 0))
    return pl.pallas_call(
        functools.partial(attend_kernel, grid, kx, bl, share, heads, tile_len),
        grid_spec=pltpu.PrefetchScalarGridSpec(
            num_scalar_prefetch=4,
            grid=(zs,),
            in_specs=[pl.BlockSpec((zs, share, cols), lambda i, *m: (0, 0, 0))] * grid.xs
            + [pl.BlockSpec(memory_space=pltpu.VMEM)]
            + [pl.BlockSpec((1, bl, heads * 2 * HD), lambda i, *m: (0, 0, first // heads))]
            + [pl.BlockSpec((1, bl, width), lambda i, *m: (i, 0, 0))] * len(mets),
            out_specs=out_specs,
            scratch_shapes=[
                pltpu.VMEM((grid.n * share + bl + 8, cols), jnp.float32),
                pltpu.VMEM((heads, GR * bl, 2 * HD), jnp.float32),
                pltpu.VMEM((heads, GR * bl, HD), jnp.float32),
            ],
        ),
        out_shape=out_shape,
        compiler_params=pltpu.CompilerParams(vmem_limit_bytes=20 * MIB),
        cost_estimate=pl.CostEstimate(
            flops=8 * zs * bl * cols * tile_len,
            bytes_accessed=2 * zs * tile_len * heads * 2 * HD,
            transcendentals=zs * bl * heads * GR * tile_len,
        ),
        name="attend",
    )(place, lengths, prompts, prompt_lengths, near, *fars, cache, own, *mets)


def finish_kernel(chunks, zs, heads, bl, place, lengths, *refs):
    out_ref = refs[-1]
    length = lengths[place[0], place[1]]
    row = lax.broadcasted_iota(jnp.int32, (bl, HD), 0)
    width = heads * GR * HD
    for c in range(chunks):
        pieces = refs[c * zs:(c + 1) * zs]
        values = [lambda h, ref=ref: ref[:, h * HD:(h + 1) * HD] for ref in pieces]
        lses = [decode(ref[:, width:]) for ref in pieces]
        parts, _ = merge(values, lses, heads * GR)
        for h in range(heads * GR):
            at = c * width + h * HD
            out_ref[0, :, at:at + HD] = jnp.where(row < length, parts[h], 0.0).astype(jnp.bfloat16)


def finish(place, lengths, pieces, chunks, zs, heads):
    bl = pieces[0].shape[0]
    cols = chunks * heads * GR * HD
    return pl.pallas_call(
        functools.partial(finish_kernel, chunks, zs, heads, bl),
        grid_spec=pltpu.PrefetchScalarGridSpec(
            num_scalar_prefetch=2,
            grid=(1,),
            in_specs=[pl.BlockSpec(piece.shape, lambda i, *m: (0, 0)) for piece in pieces],
            out_specs=pl.BlockSpec((1, bl, cols), lambda i, *m: (0, 0, 0)),
        ),
        out_shape=jax.ShapeDtypeStruct((1, bl, cols), jnp.bfloat16),
        compiler_params=pltpu.CompilerParams(vmem_limit_bytes=16 * MIB),
        name="finish",
    )(place, lengths, *pieces)


def shards(
    hidden_rows,
    carried,
    query_weight,
    response_cache,
    prompt_cache,
    prompt_lengths,
    response_lengths,
    block_prompts,
):
    grid = Grid(lax.axis_size("seq"))
    bl = hidden_rows.shape[1]
    local_kv = response_cache.shape[2] // (2 * HD)
    share = bl * 5 // 8
    chunks = 2 if local_kv % 2 == 0 else 1
    heads = local_kv // chunks
    part_cols = heads * GR * HD
    place = jnp.stack([lax.axis_index("sec"), lax.axis_index("seq")]).astype(jnp.int32)
    prompts = block_prompts[:, :, 0]

    def after(value, done):
        return lax.optimization_barrier((value, done))[0]

    def fetched(first, plain):
        out = fetch(
            place, prompts, prompt_lengths, prompt_cache, heads * 2 * HD, first, plain
        )
        return [pltpu.with_memory_space_constraint(array, pltpu.VMEM) for array in out]

    handed = lax.ppermute(carried, "sec", [(0, 1)])
    _, hidden, weight, own = fetched(None, [hidden_rows, query_weight, response_cache])
    depth = query_weight.shape[1]
    if depth % HD:
        hidden = hidden_rows
    slices = split(grid, place, hidden, handed, depth)
    x = [grid.swap(piece, k // grid.zs, k % grid.zs) if k else piece for k, piece in enumerate(slices)]
    caches = [fetched(0, [])[0]]
    x[0] = after(x[0], caches[0])
    part = project(grid, place, response_lengths, x, weight, bl, share, chunks)
    part = [piece.reshape(grid.zs, share, part_cols) for piece in part]
    part = [part[c * grid.xs:(c + 1) * grid.xs] for c in range(chunks)]

    def narrow(value):
        return (value * 0.125).astype(jnp.float16)

    def widen(value):
        return value.astype(jnp.float32) * 8.0

    def sum_x(c, done):
        parts = part[c]
        got = [grid.swap(after(narrow(parts[kx]), done), kx, 0) for kx in range(1, grid.xs)]
        return functools.reduce(jnp.add, [parts[0]] + [widen(value) for value in got]), got

    def sum_z(held, done):
        got = [grid.swap(after(narrow(held[kz]), done), 0, kz) for kz in range(1, grid.zs)]
        total = functools.reduce(jnp.add, [held[0]] + [widen(value) for value in got])
        return total.astype(jnp.bfloat16)

    def gather_z(mine):
        return [mine] + [grid.swap(mine, 0, kz) for kz in range(1, grid.zs)]

    def gather_x(near):
        return [near] + [grid.swap(near, kx, 0) for kx in range(1, grid.xs)]

    def call(c, kx, queries, mets):
        return attend(
            grid, kx, place, response_lengths, prompts, prompt_lengths, queries[0], queries[1:],
            caches[c], own, mets, c * heads, heads,
        )

    queries = [None] * chunks
    sent = [[] for _ in range(chunks)]
    if chunks > 1:
        caches.append(fetched(1, [])[0])
        part[0][0] = after(part[0][0], caches[1])
    held, got = sum_x(0, ())
    mine = sum_z(held, ())
    column = gather_z(mine)
    near = jnp.stack(column)
    if chunks > 1:
        held, _ = sum_x(1, got)
        mine = sum_z(held, column)
    queries[0] = gather_x(near)
    if chunks > 1:
        column = gather_z(mine)
        queries[0][0] = after(queries[0][0], mine)
    for kx in range(1, grid.xs):
        out = call(0, kx, queries[0], [])
        sent[0].append(grid.swap(out, kx, 0))
    if chunks > 1:
        near = jnp.stack(after(column, out))
        queries[1] = gather_x(near)
        queries[0][0] = after(queries[0][0], near)
        for kx in range(1, grid.xs):
            sent[1].append(None)
    pieces = []
    for c in range(chunks):
        if c:
            for kx in range(1, grid.xs):
                sent[c][kx - 1] = grid.swap(call(c, kx, queries[c], []), kx, 0)
        held = call(c, 0, queries[c], sent[c])
        pieces.append(held[0])
        pieces.extend(grid.swap(held[kz], 0, kz) for kz in range(1, grid.zs))
    return finish(place, response_lengths, pieces, chunks, grid.zs, heads)


def solution(mesh):
    placed = (
        P("sec", "seq", None),
        P("sec", "seq", None),
        P("sec", "seq", "tp"),
        P("sec", "seq", "tp"),
        P("sec", None, "seq", "tp"),
        P(),
        P(),
        P(),
    )
    return jax.shard_map(
        shards, mesh=mesh, in_specs=placed, out_specs=P("sec", "seq", "tp"), check_vma=False
    )
```

```python
import functools
import math

import jax
import jax.numpy as jnp
from jax import lax
from jax.experimental import pallas as pl
from jax.experimental.pallas import tpu as pltpu
from jax.sharding import PartitionSpec as P

HD = 128
GR = 4
NEG = -1e30
LOG2E = 1.4426950408889634
CHUNK = 512
LONG = 1024
ROUND = 16
EXTRA = 128
SLOT = 32
BIG = 2.0 ** 100
MIB = 1024 * 1024


def dot_nt(a, b):
    return lax.dot_general(a, b, (((1,), (1,)), ((), ())), preferred_element_type=jnp.float32)


class Grid:
    def __init__(self, count):
        self.n = count
        self.xs = 1 << ((count.bit_length() - 1) // 2)
        self.zs = count // self.xs

    def owner(self, shard, kx, kz):
        z, x = shard // self.xs, shard % self.xs
        return (z ^ kz) * self.xs + (x ^ kx)

    def swap(self, value, kx, kz):
        pairs = [(s, self.owner(s, kx, kz)) for s in range(self.n)]
        return lax.ppermute(value, "seq", pairs)


def split_kernel(grid, depth, place, hidden_ref, handed_ref, *out_refs):
    for kx in range(grid.xs):
        for kz in range(grid.zs):
            at = pl.multiple_of(grid.owner(place[1], kx, kz) * depth, HD)
            total = hidden_ref[0, :, pl.ds(at, depth)].astype(jnp.float32) + handed_ref[
                0, :, pl.ds(at, depth)
            ].astype(jnp.float32)
            out_refs[kx * grid.zs + kz][...] = total.astype(jnp.bfloat16)


def split(grid, place, hidden, handed, depth):
    bl = hidden.shape[1]
    if depth % HD:
        total = (hidden[0].astype(jnp.float32) + handed[0].astype(jnp.float32)).astype(jnp.bfloat16)
        return [
            lax.dynamic_slice_in_dim(total, grid.owner(place[1], kx, kz) * depth, depth, 1)
            for kx in range(grid.xs) for kz in range(grid.zs)
        ]
    whole = pl.BlockSpec(hidden.shape, lambda i, *m: (0, 0, 0))
    return pl.pallas_call(
        functools.partial(split_kernel, grid, depth),
        grid_spec=pltpu.PrefetchScalarGridSpec(
            num_scalar_prefetch=1,
            grid=(1,),
            in_specs=[whole, whole],
            out_specs=[pl.BlockSpec((bl, depth), lambda i, *m: (0, 0))] * grid.n,
        ),
        out_shape=[jax.ShapeDtypeStruct((bl, depth), jnp.bfloat16)] * grid.n,
        compiler_params=pltpu.CompilerParams(vmem_limit_bytes=16 * MIB),
        name="split",
    )(place, hidden, handed)


def run_moves(moves):
    for needed, move in moves:
        if needed is None:
            move.start()
        else:
            pl.when(needed)(move.start)
    for needed, move in moves:
        if needed is None:
            move.wait()
        else:
            pl.when(needed)(move.wait)


def fetch_kernel(*refs):
    count = len(refs) // 2
    run_moves([
        (None, pltpu.make_async_copy(refs[i], refs[count + i], refs[-1].at[i]))
        for i in range(count)
    ])


def fetch(arrays):
    anywhere, near = pl.BlockSpec(memory_space=pltpu.HBM), pl.BlockSpec(memory_space=pltpu.VMEM)
    size = sum(math.prod(array.shape) for array in arrays)
    out = pl.pallas_call(
        fetch_kernel,
        in_specs=[anywhere] * len(arrays),
        out_specs=[near] * len(arrays),
        scratch_shapes=[pltpu.SemaphoreType.DMA((len(arrays),))],
        out_shape=[pltpu.VMEM(array.shape, array.dtype) for array in arrays],
        compiler_params=pltpu.CompilerParams(vmem_limit_bytes=4 * MIB),
        cost_estimate=pl.CostEstimate(flops=0, bytes_accessed=2 * size, transcendentals=0),
        name="fetch",
    )(*[pltpu.with_memory_space_constraint(array, pltpu.HBM) for array in arrays])
    return [pltpu.with_memory_space_constraint(array, pltpu.VMEM) for array in out]


def fetch_cache_kernel(chunk, width, first, place, prompts, prompt_lengths, cache_ref, kv_ref, sem):
    count, tile_len = kv_ref.shape[:2]
    section, shard = place[0], place[1]
    moves = []
    for p in range(count):
        asked = prompts[section, 0] == p
        for b in range(1, prompts.shape[1]):
            asked = asked | (prompts[section, b] == p)
        for c in range(tile_len // chunk):
            at = pl.ds(c * chunk, chunk)
            needed = asked & (prompt_lengths[p] > shard * tile_len + c * chunk)
            moves.append((needed, pltpu.make_async_copy(
                cache_ref.at[0, p, at, pl.ds(first * width, width)], kv_ref.at[p, at],
                sem.at[p, c],
            )))
    run_moves(moves)


def fetch_cache(place, prompts, prompt_lengths, cache, width, first):
    count, tile_len = cache.shape[1:3]
    chunk = min(CHUNK, tile_len)
    shape = (count, tile_len, width)
    out = pl.pallas_call(
        functools.partial(fetch_cache_kernel, chunk, width, first),
        grid_spec=pltpu.PrefetchScalarGridSpec(
            num_scalar_prefetch=3,
            grid=(1,),
            in_specs=[pl.BlockSpec(memory_space=pltpu.HBM)],
            out_specs=pl.BlockSpec(memory_space=pltpu.VMEM),
            scratch_shapes=[pltpu.SemaphoreType.DMA((count, tile_len // chunk))],
        ),
        out_shape=pltpu.VMEM(shape, cache.dtype),
        compiler_params=pltpu.CompilerParams(vmem_limit_bytes=4 * MIB),
        cost_estimate=pl.CostEstimate(
            flops=0, bytes_accessed=2 * math.prod(shape), transcendentals=0
        ),
        name="fetch_cache",
    )(place, prompts, prompt_lengths, pltpu.with_memory_space_constraint(cache, pltpu.HBM))
    return pltpu.with_memory_space_constraint(out, pltpu.VMEM)


def project_kernel(grid, bl, share, place, lengths, *refs):
    x_refs, w_ref, refs = refs[:grid.n], refs[grid.n], refs[grid.n + 1:]
    out_refs, (xp_ref, starts) = refs[:-2], refs[-2:]

    @pl.when(pl.program_id(0) == 0)
    def _():
        section, shard = place[0], place[1]
        offset = jnp.int32(0)
        for b in range(grid.n):
            starts[b] = offset
            offset = offset + lengths[section, b]
        lane = lax.broadcasted_iota(jnp.int32, (8, grid.n * bl), 1)
        target = jnp.full(lane.shape, -1, jnp.int32)
        owners = [
            grid.owner(shard, kx, kz) for kx in range(grid.xs) for kz in range(grid.zs)
        ]
        for k, b in enumerate(owners):
            order = lane - k * bl
            used = (order >= 0) & (order < lengths[section, b])
            target = jnp.where(used, order + starts[b], target)
        row = lax.broadcasted_iota(jnp.int32, (share, grid.n * bl), 0)
        target = jnp.broadcast_to(target[:1], row.shape)
        picks = [jnp.where(row + b * share == target, 1.0, 0.0) for b in owners]
        pick = jnp.concatenate(picks, axis=0).astype(jnp.bfloat16)
        x = jnp.concatenate([ref[...] for ref in x_refs], axis=0)
        chosen = jnp.dot(pick, x, preferred_element_type=jnp.float32)
        xp_ref[...] = chosen.astype(jnp.bfloat16)

    result = jnp.dot(xp_ref[...], w_ref[0], preferred_element_type=jnp.float32)
    rows = grid.zs * share
    for i, out_ref in enumerate(out_refs):
        chunk, kx = i // grid.xs, i % grid.xs

        @pl.when(pl.program_id(0) == chunk)
        def _(out_ref=out_ref, kx=kx):
            out_ref[...] = result[kx * rows:(kx + 1) * rows]


def project(grid, place, lengths, xs, w, bl, share, chunks):
    k, cols = w.shape[1:]
    rows = grid.n * share
    tile = cols // chunks
    piece = (grid.zs * share, tile)
    return pl.pallas_call(
        functools.partial(project_kernel, grid, bl, share),
        grid_spec=pltpu.PrefetchScalarGridSpec(
            num_scalar_prefetch=2,
            grid=(chunks,),
            in_specs=[pl.BlockSpec((bl, k), lambda j, *m: (0, 0))] * grid.n
            + [pl.BlockSpec((1, k, tile), lambda j, *m: (0, 0, j))],
            out_specs=[pl.BlockSpec(piece, lambda j, *m: (0, 0))] * (chunks * grid.xs),
            scratch_shapes=[
                pltpu.VMEM((rows, k), jnp.bfloat16), pltpu.SMEM((grid.n,), jnp.int32)
            ],
        ),
        out_shape=[jax.ShapeDtypeStruct(piece, jnp.float32)] * (chunks * grid.xs),
        compiler_params=pltpu.CompilerParams(vmem_limit_bytes=20 * MIB),
        cost_estimate=pl.CostEstimate(
            flops=2 * rows * k * cols, bytes_accessed=2 * k * cols + 4 * rows * cols,
            transcendentals=0,
        ),
        name="project",
    )(place, lengths, *xs, w)


def encode(lse):
    lane = lax.broadcasted_iota(jnp.int32, lse.shape, 1)
    lse = jnp.where(lane < SLOT, lse, 0.0)
    high = lse.astype(jnp.bfloat16).astype(jnp.float32)
    rest = lse - high
    mid = rest.astype(jnp.bfloat16).astype(jnp.float32)
    low = rest - mid
    terms = high + pltpu.roll(mid, SLOT, 1) + pltpu.roll(low, 2 * SLOT, 1)
    return terms.astype(jnp.bfloat16)


def decode(tile):
    terms = tile.astype(jnp.float32)
    return terms + pltpu.roll(terms, EXTRA - SLOT, 1) + pltpu.roll(terms, EXTRA - 2 * SLOT, 1)


def merge(refs, heads):
    width = heads * HD
    lses = [decode(ref[:, width:]) for ref in refs]
    rows = lses[0].shape[0]
    peak = functools.reduce(jnp.maximum, lses)
    weights = [jnp.exp2(lse - peak) for lse in lses]
    total = functools.reduce(jnp.add, weights)
    weights = [weight / total for weight in weights]
    out = []
    for h in range(heads):
        terms = [
            jnp.broadcast_to(weight[:, h:h + 1], (rows, HD))
            * ref[:, h * HD:(h + 1) * HD].astype(jnp.float32)
            for weight, ref in zip(weights, refs)
        ]
        out.append(functools.reduce(jnp.add, terms))
    return out, peak + jnp.log2(total)


def merge_kernel(zs, heads, *refs):
    sources, outs = refs[:-zs], refs[-zs:]
    for kz in range(zs):
        parts, lse = merge([ref.at[kz] for ref in sources], heads)
        for h in range(heads):
            outs[kz][:, h * HD:(h + 1) * HD] = parts[h].astype(jnp.bfloat16)
        outs[kz][:, heads * HD:] = encode(lse)


def merge_column(sources, heads):
    zs, bl, width = sources[0].shape
    return pl.pallas_call(
        functools.partial(merge_kernel, zs, heads),
        out_shape=[jax.ShapeDtypeStruct((bl, width), jnp.bfloat16)] * zs,
        compiler_params=pltpu.CompilerParams(vmem_limit_bytes=16 * MIB),
        name="merge",
    )(*sources)


def attend_kernel(grid, kx, bl, share, heads, tile_len, *refs):
    place, lengths, prompts, prompt_lengths = refs[:4]
    near_ref, far_refs = refs[4], refs[5:4 + grid.xs]
    kv_ref, own_ref, out_ref, q32_ref, acc_ref, m_ref = refs[4 + grid.xs:]
    shard = place[1]
    rows = grid.n * share
    for fx in range(grid.xs):
        for fz in range(grid.zs):
            source = near_ref if fx == 0 else far_refs[fx - 1]
            at = pl.multiple_of(grid.owner(shard, fx, fz) * share, 8)
            q32_ref[pl.ds(at, share), :] = source[fz].astype(jnp.float32)
    q32_ref[rows:, :] = jnp.zeros((bl + 8, q32_ref.shape[1]), jnp.float32)
    acc_ref[...] = jnp.zeros_like(acc_ref)
    m_ref[...] = jnp.full_like(m_ref, NEG)

    def one(kz, carry):
        attend_block(
            grid, kx, bl, heads, tile_len, kz, place, lengths, prompts, prompt_lengths,
            kv_ref, own_ref, out_ref, q32_ref, acc_ref, m_ref,
        )
        return carry

    lax.fori_loop(0, grid.zs, one, 0)


def attend_block(grid, kx, bl, heads, tile_len, step, place, lengths, prompts, prompt_lengths,
                 kv_ref, own_ref, out_ref, q32_ref, acc_ref, m_ref):
    section, shard = place[0], place[1]
    block = grid.owner(shard, kx, step)
    offset = jnp.int32(0)
    for b in range(grid.n):
        offset = offset + jnp.where(b < block, lengths[section, b], 0)
    prompt = prompts[section, block]
    valid = jnp.clip(prompt_lengths[prompt] - shard * tile_len, 0, tile_len)
    c2 = LOG2E / math.sqrt(HD)
    chunk = min(CHUNK, tile_len)
    width = heads * GR * HD

    rest = offset % 8
    window = q32_ref[pl.ds(pl.multiple_of(offset - rest, 8), bl + 8), :]
    window = pltpu.roll(window, jnp.where(rest == 0, 0, bl + 8 - rest), 0)
    queries = window[:bl].astype(jnp.bfloat16)

    def group(g, used):
        return jnp.concatenate(
            [queries[:used, (g * GR + r) * HD:(g * GR + r + 1) * HD] for r in range(GR)], axis=0
        )

    def with_ones(v):
        return jnp.concatenate([v, jnp.ones(v.shape, jnp.bfloat16)], axis=1)

    def sums(p, v):
        return jnp.dot(p, with_ones(v), preferred_element_type=jnp.float32)

    def keys(g, at, size):
        return kv_ref[prompt, pl.ds(at, size), pl.ds(g * 2 * HD, HD)]

    def vals(g, at, size):
        return kv_ref[prompt, pl.ds(at, size), pl.ds(g * 2 * HD + HD, HD)]

    def put(g, used, acc, m):
        m = jnp.broadcast_to(m, (GR * used, HD))
        for r in range(GR):
            acc_ref[g, r * bl:r * bl + used] = acc[r * used:(r + 1) * used]
            m_ref[g, r * bl:r * bl + used] = m[r * used:(r + 1) * used]

    def update(g, s, seen, v):
        s = jnp.where(seen, s, NEG)
        before = m_ref[g][:, :1]
        m = jnp.maximum(before, jnp.max(s, axis=1, keepdims=True))
        p = jnp.where(seen, jnp.exp2((s - m) * c2), 0.0).astype(jnp.bfloat16)
        acc_ref[g] = acc_ref[g] * jnp.exp2((before - m) * c2) + sums(p, v)
        m_ref[g] = jnp.broadcast_to(m, m_ref.shape[1:])

    def exact():
        acc_ref[...] = jnp.zeros_like(acc_ref)
        m_ref[...] = jnp.full_like(m_ref, NEG)

        def one(c, carry):
            at = pl.multiple_of(c * chunk, chunk)
            for g in range(heads):
                s = dot_nt(group(g, bl), keys(g, at, chunk))
                here = lax.broadcasted_iota(jnp.int32, s.shape, 1) + at
                update(g, s, here < valid, vals(g, at, chunk))
            return carry

        lax.fori_loop(0, (valid + chunk - 1) // chunk, one, 0)

    length = lengths[section, block]

    @pl.when(valid == 0)
    def _():
        acc_ref[...] = jnp.zeros_like(acc_ref)
        m_ref[...] = jnp.full_like(m_ref, NEG)

    long = min(LONG, tile_len)
    for used in range(ROUND, bl + 1, ROUND):
        @pl.when((valid == tile_len) & (length <= used) & (length > used - ROUND))
        def _(used=used):
            items = [(g, c) for g in range(heads) for c in range(tile_len // long)]
            q = [group(g, used) for g in range(heads)]
            peaks = [None] * heads
            accs = [None] * heads
            ahead = dot_nt(q[0], keys(0, 0, long))
            for i, (g, c) in enumerate(items):
                s = ahead
                if i + 1 < len(items):
                    ng, nc = items[i + 1]
                    ahead = dot_nt(q[ng], keys(ng, nc * long, long))
                if c == 0:
                    peaks[g] = jnp.max(s, axis=1, keepdims=True)
                p = jnp.exp2((s - peaks[g]) * c2).astype(jnp.bfloat16)
                part = sums(p, vals(g, c * long, long))
                accs[g] = part if c == 0 else accs[g] + part
            for g in range(heads):
                put(g, used, accs[g], peaks[g])

    @pl.when((valid < tile_len) & (valid > 0))
    def _():
        def scores(g, at):
            s = dot_nt(group(g, bl), keys(g, at, chunk))
            here = lax.broadcasted_iota(jnp.int32, s.shape, 1) + at
            return jnp.where(here < valid, s, NEG)

        for g in range(heads):
            s = scores(g, 0)
            m = jnp.max(s, axis=1, keepdims=True)
            p = jnp.exp2((s - m) * c2).astype(jnp.bfloat16)
            put(g, bl, sums(p, vals(g, 0, chunk)), m)

        def one(c, carry):
            at = pl.multiple_of(c * chunk, chunk)
            for g in range(heads):
                p = jnp.exp2((scores(g, at) - m_ref[g][:, :1]) * c2).astype(jnp.bfloat16)
                acc_ref[g] += sums(p, vals(g, at, chunk))
            return carry

        lax.fori_loop(1, (valid + chunk - 1) // chunk, one, 0)

    top = jnp.where(acc_ref[:, :, HD:] < BIG, 0.0, 1.0)

    @pl.when(jnp.max(top) > 0.5)
    def _():
        exact()

    if kx == 0:
        @pl.when(step == 0)
        def _():
            for g in range(heads):
                base = g * 2 * HD
                s = dot_nt(group(g, bl), own_ref[0, :, base:base + HD])
                row = lax.broadcasted_iota(jnp.int32, s.shape, 0) % bl
                col = lax.broadcasted_iota(jnp.int32, s.shape, 1)
                update(g, s, col <= row, own_ref[0, :, base + HD:base + 2 * HD])

    lane = lax.broadcasted_iota(jnp.int32, (bl, EXTRA), 1)
    lse_tile = jnp.zeros((bl, EXTRA), jnp.float32)
    for g in range(heads):
        total = acc_ref[g][:, HD:]
        some = total > 0.0
        safe = jnp.where(some, total, 1.0)
        out = (acc_ref[g][:, :HD] / safe).astype(jnp.bfloat16)
        lse = jnp.where(some, m_ref[g] * c2 + jnp.log2(safe), NEG)
        for r in range(GR):
            h = g * GR + r
            out_ref[step, :, h * HD:(h + 1) * HD] = out[r * bl:(r + 1) * bl]
            lse_tile = jnp.where(lane == h, lse[r * bl:(r + 1) * bl], lse_tile)
    out_ref[step, :, width:] = encode(lse_tile)


def attend(grid, kx, place, lengths, prompts, prompt_lengths, near, fars, cache, own, first, heads):
    zs, share, cols = near.shape
    bl = own.shape[1]
    tile_len = cache.shape[1]
    width = heads * GR * HD + EXTRA
    return pl.pallas_call(
        functools.partial(attend_kernel, grid, kx, bl, share, heads, tile_len),
        grid_spec=pltpu.PrefetchScalarGridSpec(
            num_scalar_prefetch=4,
            grid=(1,),
            in_specs=[pl.BlockSpec((zs, share, cols), lambda i, *m: (0, 0, 0))] * grid.xs
            + [pl.BlockSpec(memory_space=pltpu.VMEM)]
            + [pl.BlockSpec((1, bl, heads * 2 * HD), lambda i, *m: (0, 0, first // heads))],
            out_specs=pl.BlockSpec((zs, bl, width), lambda i, *m: (0, 0, 0)),
            scratch_shapes=[
                pltpu.VMEM((grid.n * share + bl + 8, cols), jnp.float32),
                pltpu.VMEM((heads, GR * bl, 2 * HD), jnp.float32),
                pltpu.VMEM((heads, GR * bl, HD), jnp.float32),
            ],
        ),
        out_shape=jax.ShapeDtypeStruct((zs, bl, width), jnp.bfloat16),
        compiler_params=pltpu.CompilerParams(vmem_limit_bytes=20 * MIB),
        cost_estimate=pl.CostEstimate(
            flops=8 * zs * bl * cols * tile_len,
            bytes_accessed=2 * zs * tile_len * heads * 2 * HD,
            transcendentals=zs * bl * heads * GR * tile_len,
        ),
        name="attend",
    )(place, lengths, prompts, prompt_lengths, near, *fars, cache, own)


def finish_kernel(chunks, zs, heads, bl, place, lengths, *refs):
    out_ref = refs[-1]
    length = lengths[place[0], place[1]]
    row = lax.broadcasted_iota(jnp.int32, (bl, HD), 0)
    width = heads * GR * HD
    for c in range(chunks):
        pieces = refs[c * zs:(c + 1) * zs]
        parts, _ = merge(pieces, heads * GR)
        for h in range(heads * GR):
            at = c * width + h * HD
            out_ref[0, :, at:at + HD] = jnp.where(row < length, parts[h], 0.0).astype(jnp.bfloat16)


def finish(place, lengths, pieces, chunks, zs, heads):
    bl = pieces[0].shape[0]
    cols = chunks * heads * GR * HD
    return pl.pallas_call(
        functools.partial(finish_kernel, chunks, zs, heads, bl),
        grid_spec=pltpu.PrefetchScalarGridSpec(
            num_scalar_prefetch=2,
            grid=(1,),
            in_specs=[pl.BlockSpec(piece.shape, lambda i, *m: (0, 0)) for piece in pieces],
            out_specs=pl.BlockSpec((1, bl, cols), lambda i, *m: (0, 0, 0)),
        ),
        out_shape=jax.ShapeDtypeStruct((1, bl, cols), jnp.bfloat16),
        compiler_params=pltpu.CompilerParams(vmem_limit_bytes=16 * MIB),
        name="finish",
    )(place, lengths, *pieces)


def shards(
    hidden_rows,
    carried,
    query_weight,
    response_cache,
    prompt_cache,
    prompt_lengths,
    response_lengths,
    block_prompts,
):
    grid = Grid(lax.axis_size("seq"))
    bl = hidden_rows.shape[1]
    local_kv = response_cache.shape[2] // (2 * HD)
    share = bl * 5 // 8
    chunks = 2 if local_kv % 2 == 0 else 1
    heads = local_kv // chunks
    part_cols = heads * GR * HD
    place = jnp.stack([lax.axis_index("sec"), lax.axis_index("seq")]).astype(jnp.int32)
    prompts = block_prompts[:, :, 0]

    def after(value, done):
        return lax.optimization_barrier((value, done))[0]

    def fetched(c):
        return fetch_cache(place, prompts, prompt_lengths, prompt_cache, heads * 2 * HD, c)

    handed = lax.ppermute(carried, "sec", [(0, 1)])
    depth = query_weight.shape[1]
    hidden = hidden_rows if depth % HD else fetch([hidden_rows])[0]
    slices = split(grid, place, hidden, handed, depth)
    weight, own = fetch([query_weight, response_cache])
    x = [slices[0]] + [None] * (grid.n - 1)
    for kz in reversed(range(grid.zs)):
        for kx in reversed(range(grid.xs)):
            k = kx * grid.zs + kz
            if k:
                x[k] = grid.swap(slices[k], kx, kz)
    part = project(grid, place, response_lengths, x, weight, bl, share, chunks)
    part = [piece.reshape(grid.zs, share, part_cols) for piece in part]
    part = [part[c * grid.xs:(c + 1) * grid.xs] for c in range(chunks)]

    def narrow(value):
        return (value * 0.125).astype(jnp.float16)

    def widen(value):
        return value.astype(jnp.float32) * 8.0

    def sum_x(c, done):
        parts = part[c]
        got = [grid.swap(after(narrow(parts[kx]), done), kx, 0) for kx in range(1, grid.xs)]
        return functools.reduce(jnp.add, [parts[0]] + [widen(value) for value in got]), got

    def sum_z(held, done):
        got = [grid.swap(after(narrow(held[kz]), done), 0, kz) for kz in range(1, grid.zs)]
        total = functools.reduce(jnp.add, [held[0]] + [widen(value) for value in got])
        return total.astype(jnp.bfloat16)

    def gather_z(mine):
        return [mine] + [grid.swap(mine, 0, kz) for kz in range(1, grid.zs)]

    def gather_x(near):
        return [near] + [grid.swap(near, kx, 0) for kx in range(1, grid.xs)]

    def call(c, kx, queries):
        return attend(
            grid, kx, place, response_lengths, prompts, prompt_lengths, queries[0], queries[1:],
            caches[c], own, c * heads, heads,
        )

    def call_far(c, queries):
        outs = [call(c, kx, queries) for kx in range(1, grid.xs)]
        return outs, [grid.swap(out, kx + 1, 0) for kx, out in enumerate(outs)]

    def send_z(merged):
        return [merged[0]] + [grid.swap(merged[kz], 0, kz) for kz in range(1, grid.zs)]

    caches = [None] * chunks
    if chunks > 1:
        caches[1] = fetched(1)
        part[0][0] = after(part[0][0], caches[1])
    held, got = sum_x(0, ())
    mine = sum_z(held, ())
    column = gather_z(mine)
    caches[0] = fetched(0)
    near = jnp.stack(after(column, caches[0]))
    if chunks > 1:
        held, _ = sum_x(1, got)
        mine = sum_z(held, column)
    queries = gather_x(near)
    if chunks > 1:
        column = gather_z(mine)
        queries[0] = after(queries[0], mine)
    outs, mets = call_far(0, queries)
    if chunks > 1:
        near = jnp.stack(after(column, outs))
        later = gather_x(near)
        queries[0] = after(queries[0], near)
    held = call(0, 0, queries)
    if chunks > 1:
        later[0] = after(later[0], held)
        outs, later_mets = call_far(1, later)
        held = after(held, outs)
    merged = merge_column([held] + mets, heads * GR)
    pieces = send_z(merged)
    if chunks > 1:
        later[0] = after(later[0], merged)
        held = call(1, 0, later)
        pieces += send_z(merge_column([held] + later_mets, heads * GR))
    return finish(place, response_lengths, pieces, chunks, grid.zs, heads)


def solution(mesh):
    placed = (
        P("sec", "seq", None),
        P("sec", "seq", None),
        P("sec", "seq", "tp"),
        P("sec", "seq", "tp"),
        P("sec", None, "seq", "tp"),
        P(),
        P(),
        P(),
    )
    return jax.shard_map(
        shards, mesh=mesh, in_specs=placed, out_specs=P("sec", "seq", "tp"), check_vma=False
    )
```

```python
import functools
import math

import jax
import jax.numpy as jnp
from jax import lax
from jax.experimental import pallas as pl
from jax.experimental.pallas import tpu as pltpu
from jax.sharding import PartitionSpec as P

HD = 128
GR = 4
NEG = -1e30
LOG2E = 1.4426950408889634
CHUNK = 512
ROUND = 32
EXTRA = 128
SLOT = 32
BIG = 2.0 ** 100
MIB = 1024 * 1024


def dot_nt(a, b):
    return lax.dot_general(a, b, (((1,), (1,)), ((), ())), preferred_element_type=jnp.float32)


class Grid:
    def __init__(self, count):
        self.n = count
        self.xs = 1 << ((count.bit_length() - 1) // 2)
        self.zs = count // self.xs

    def owner(self, shard, kx, kz):
        z, x = shard // self.xs, shard % self.xs
        return (z ^ kz) * self.xs + (x ^ kx)

    def swap(self, value, kx, kz):
        pairs = [(s, self.owner(s, kx, kz)) for s in range(self.n)]
        return lax.ppermute(value, "seq", pairs)


class Facts:
    def __init__(self, n, meta):
        self.n, self.meta = n, meta
        self.section, self.shard = meta[0], meta[1]

    def length(self, block):
        return self.meta[2 + self.section * self.n + block]

    def prompt(self, block):
        return self.meta[2 + (2 + self.section) * self.n + block]

    def prompt_length(self, prompt):
        return self.meta[2 + 4 * self.n + prompt]


def split_kernel(grid, depth, meta, hidden_ref, handed_ref, *out_refs):
    for kx in range(grid.xs):
        for kz in range(grid.zs):
            at = pl.multiple_of(grid.owner(meta[1], kx, kz) * depth, HD)
            total = hidden_ref[0, :, pl.ds(at, depth)].astype(jnp.float32) + handed_ref[
                0, :, pl.ds(at, depth)
            ].astype(jnp.float32)
            out_refs[kx * grid.zs + kz][...] = total.astype(jnp.bfloat16)


def split(grid, meta, hidden, handed, depth):
    bl = hidden.shape[1]
    if depth % HD:
        total = (hidden[0].astype(jnp.float32) + handed[0].astype(jnp.float32)).astype(jnp.bfloat16)
        return [
            lax.dynamic_slice_in_dim(total, grid.owner(meta[1], kx, kz) * depth, depth, 1)
            for kx in range(grid.xs) for kz in range(grid.zs)
        ]
    whole = pl.BlockSpec(hidden.shape, lambda i, *m: (0, 0, 0))
    return pl.pallas_call(
        functools.partial(split_kernel, grid, depth),
        grid_spec=pltpu.PrefetchScalarGridSpec(
            num_scalar_prefetch=1,
            grid=(1,),
            in_specs=[whole, whole],
            out_specs=[pl.BlockSpec((bl, depth), lambda i, *m: (0, 0))] * grid.n,
        ),
        out_shape=[jax.ShapeDtypeStruct((bl, depth), jnp.bfloat16)] * grid.n,
        compiler_params=pltpu.CompilerParams(vmem_limit_bytes=16 * MIB),
        name="split",
    )(meta, hidden, handed)


def run_moves(moves):
    for needed, move in moves:
        if needed is None:
            move.start()
        else:
            pl.when(needed)(move.start)
    for needed, move in moves:
        if needed is None:
            move.wait()
        else:
            pl.when(needed)(move.wait)


def fetch_kernel(*refs):
    count = len(refs) // 2
    run_moves([
        (None, pltpu.make_async_copy(refs[i], refs[count + i], refs[-1].at[i]))
        for i in range(count)
    ])


def fetch(arrays):
    anywhere, near = pl.BlockSpec(memory_space=pltpu.HBM), pl.BlockSpec(memory_space=pltpu.VMEM)
    size = sum(math.prod(array.shape) for array in arrays)
    out = pl.pallas_call(
        fetch_kernel,
        in_specs=[anywhere] * len(arrays),
        out_specs=[near] * len(arrays),
        scratch_shapes=[pltpu.SemaphoreType.DMA((len(arrays),))],
        out_shape=[pltpu.VMEM(array.shape, array.dtype) for array in arrays],
        compiler_params=pltpu.CompilerParams(vmem_limit_bytes=4 * MIB),
        cost_estimate=pl.CostEstimate(flops=0, bytes_accessed=2 * size, transcendentals=0),
        name="fetch",
    )(*[pltpu.with_memory_space_constraint(array, pltpu.HBM) for array in arrays])
    return [pltpu.with_memory_space_constraint(array, pltpu.VMEM) for array in out]


def fetch_cache_kernel(n, chunk, width, first, meta, cache_ref, kv_ref, sem):
    count, tile_len = kv_ref.shape[:2]
    facts = Facts(n, meta)
    moves = []
    for p in range(count):
        asked = facts.prompt(0) == p
        for b in range(1, n):
            asked = asked | (facts.prompt(b) == p)
        for c in range(tile_len // chunk):
            at = pl.ds(c * chunk, chunk)
            needed = asked & (facts.prompt_length(p) > facts.shard * tile_len + c * chunk)
            moves.append((needed, pltpu.make_async_copy(
                cache_ref.at[0, p, at, pl.ds(first * width, width)], kv_ref.at[p, at],
                sem.at[p, c],
            )))
    run_moves(moves)


def fetch_cache(n, meta, cache, width, first):
    count, tile_len = cache.shape[1:3]
    chunk = min(CHUNK, tile_len)
    shape = (count, tile_len, width)
    out = pl.pallas_call(
        functools.partial(fetch_cache_kernel, n, chunk, width, first),
        grid_spec=pltpu.PrefetchScalarGridSpec(
            num_scalar_prefetch=1,
            grid=(1,),
            in_specs=[pl.BlockSpec(memory_space=pltpu.HBM)],
            out_specs=pl.BlockSpec(memory_space=pltpu.VMEM),
            scratch_shapes=[pltpu.SemaphoreType.DMA((count, tile_len // chunk))],
        ),
        out_shape=pltpu.VMEM(shape, cache.dtype),
        compiler_params=pltpu.CompilerParams(vmem_limit_bytes=4 * MIB),
        cost_estimate=pl.CostEstimate(
            flops=0, bytes_accessed=2 * math.prod(shape), transcendentals=0
        ),
        name="fetch_cache",
    )(meta, pltpu.with_memory_space_constraint(cache, pltpu.HBM))
    return pltpu.with_memory_space_constraint(out, pltpu.VMEM)


def project_kernel(grid, bl, share, meta, *refs):
    x_refs, w_ref, refs = refs[:grid.n], refs[grid.n], refs[grid.n + 1:]
    out_refs, (xp_ref, starts) = refs[:-2], refs[-2:]

    @pl.when(pl.program_id(0) == 0)
    def _():
        facts = Facts(grid.n, meta)
        shard = facts.shard
        offset = jnp.int32(0)
        for b in range(grid.n):
            starts[b] = offset
            offset = offset + facts.length(b)
        lane = lax.broadcasted_iota(jnp.int32, (8, grid.n * bl), 1)
        target = jnp.full(lane.shape, -1, jnp.int32)
        owners = [
            grid.owner(shard, kx, kz) for kx in range(grid.xs) for kz in range(grid.zs)
        ]
        for k, b in enumerate(owners):
            order = lane - k * bl
            used = (order >= 0) & (order < facts.length(b))
            target = jnp.where(used, order + starts[b], target)
        row = lax.broadcasted_iota(jnp.int32, (share, grid.n * bl), 0)
        target = jnp.broadcast_to(target[:1], row.shape)
        picks = [jnp.where(row + b * share == target, 1.0, 0.0) for b in owners]
        pick = jnp.concatenate(picks, axis=0).astype(jnp.bfloat16)
        x = jnp.concatenate([ref[...] for ref in x_refs], axis=0)
        chosen = jnp.dot(pick, x, preferred_element_type=jnp.float32)
        xp_ref[...] = chosen.astype(jnp.bfloat16)

    result = jnp.dot(xp_ref[...], w_ref[0], preferred_element_type=jnp.float32)
    rows = grid.zs * share
    for i, out_ref in enumerate(out_refs):
        chunk, kx = i // grid.xs, i % grid.xs

        @pl.when(pl.program_id(0) == chunk)
        def _(out_ref=out_ref, kx=kx):
            out_ref[...] = result[kx * rows:(kx + 1) * rows]


def project(grid, meta, xs, w, bl, share, chunks):
    k, cols = w.shape[1:]
    rows = grid.n * share
    tile = cols // chunks
    piece = (grid.zs * share, tile)
    return pl.pallas_call(
        functools.partial(project_kernel, grid, bl, share),
        grid_spec=pltpu.PrefetchScalarGridSpec(
            num_scalar_prefetch=1,
            grid=(chunks,),
            in_specs=[pl.BlockSpec((bl, k), lambda j, *m: (0, 0))] * grid.n
            + [pl.BlockSpec((1, k, tile), lambda j, *m: (0, 0, j))],
            out_specs=[pl.BlockSpec(piece, lambda j, *m: (0, 0))] * (chunks * grid.xs),
            scratch_shapes=[
                pltpu.VMEM((rows, k), jnp.bfloat16), pltpu.SMEM((grid.n,), jnp.int32)
            ],
        ),
        out_shape=[jax.ShapeDtypeStruct(piece, jnp.float32)] * (chunks * grid.xs),
        compiler_params=pltpu.CompilerParams(vmem_limit_bytes=20 * MIB),
        cost_estimate=pl.CostEstimate(
            flops=2 * rows * k * cols, bytes_accessed=2 * k * cols + 4 * rows * cols,
            transcendentals=0,
        ),
        name="project",
    )(meta, *xs, w)


def encode(lse):
    lane = lax.broadcasted_iota(jnp.int32, lse.shape, 1)
    lse = jnp.where(lane < SLOT, lse, 0.0)
    high = lse.astype(jnp.bfloat16).astype(jnp.float32)
    rest = lse - high
    mid = rest.astype(jnp.bfloat16).astype(jnp.float32)
    low = rest - mid
    terms = high + pltpu.roll(mid, SLOT, 1) + pltpu.roll(low, 2 * SLOT, 1)
    return terms.astype(jnp.bfloat16)


def decode(tile):
    terms = tile.astype(jnp.float32)
    return terms + pltpu.roll(terms, EXTRA - SLOT, 1) + pltpu.roll(terms, EXTRA - 2 * SLOT, 1)


def merge(refs, heads):
    width = heads * HD
    lses = [decode(ref[:, width:]) for ref in refs]
    rows = lses[0].shape[0]
    peak = functools.reduce(jnp.maximum, lses)
    weights = [jnp.exp2(lse - peak) for lse in lses]
    total = functools.reduce(jnp.add, weights)
    weights = [weight / total for weight in weights]
    out = []
    for h in range(heads):
        terms = [
            jnp.broadcast_to(weight[:, h:h + 1], (rows, HD))
            * ref[:, h * HD:(h + 1) * HD].astype(jnp.float32)
            for weight, ref in zip(weights, refs)
        ]
        out.append(functools.reduce(jnp.add, terms))
    return out, peak + jnp.log2(total)


def merge_kernel(zs, heads, *refs):
    sources, outs = refs[:-zs], refs[-zs:]
    for kz in range(zs):
        parts, lse = merge([ref.at[kz] for ref in sources], heads)
        for h in range(heads):
            outs[kz][:, h * HD:(h + 1) * HD] = parts[h].astype(jnp.bfloat16)
        outs[kz][:, heads * HD:] = encode(lse)


def merge_column(sources, heads):
    zs, bl, width = sources[0].shape
    return pl.pallas_call(
        functools.partial(merge_kernel, zs, heads),
        out_shape=[jax.ShapeDtypeStruct((bl, width), jnp.bfloat16)] * zs,
        compiler_params=pltpu.CompilerParams(vmem_limit_bytes=16 * MIB),
        name="merge",
    )(*sources)


def attend_kernel(grid, kx, bl, share, first, heads, tile_len, meta, *refs):
    near_ref, far_refs = refs[0], refs[1:grid.xs]
    kv_ref, own_ref, out_ref, q32_ref, acc_ref, m_ref = refs[grid.xs:]
    facts = Facts(grid.n, meta)
    shard = facts.shard
    rows = grid.n * share
    for fx in range(grid.xs):
        for fz in range(grid.zs):
            source = near_ref if fx == 0 else far_refs[fx - 1]
            at = pl.multiple_of(grid.owner(shard, fx, fz) * share, 8)
            q32_ref[pl.ds(at, share), :] = source[fz].astype(jnp.float32)
    q32_ref[rows:, :] = jnp.zeros((bl + 8, q32_ref.shape[1]), jnp.float32)
    acc_ref[...] = jnp.zeros_like(acc_ref)
    m_ref[...] = jnp.full_like(m_ref, NEG)

    def one(kz, carry):
        attend_block(
            grid, kx, bl, first, heads, tile_len, kz, facts,
            kv_ref, own_ref, out_ref, q32_ref, acc_ref, m_ref,
        )
        return carry

    lax.fori_loop(0, grid.zs, one, 0)


def attend_block(grid, kx, bl, first, heads, tile_len, step, facts,
                 kv_ref, own_ref, out_ref, q32_ref, acc_ref, m_ref):
    block = grid.owner(facts.shard, kx, step)
    offset = jnp.int32(0)
    for b in range(grid.n):
        offset = offset + jnp.where(b < block, facts.length(b), 0)
    prompt = facts.prompt(block)
    valid = jnp.clip(facts.prompt_length(prompt) - facts.shard * tile_len, 0, tile_len)
    c2 = LOG2E / math.sqrt(HD)
    chunk = min(CHUNK, tile_len)
    width = heads * GR * HD

    rest = offset % 8
    window = q32_ref[pl.ds(pl.multiple_of(offset - rest, 8), bl + 8), :]
    window = pltpu.roll(window, jnp.where(rest == 0, 0, bl + 8 - rest), 0)
    queries = window[:bl].astype(jnp.bfloat16)

    def group(g, used):
        return jnp.concatenate(
            [queries[:used, (g * GR + r) * HD:(g * GR + r + 1) * HD] for r in range(GR)], axis=0
        )

    def with_ones(v):
        return jnp.concatenate([v, jnp.ones(v.shape, jnp.bfloat16)], axis=1)

    def sums(p, v):
        return jnp.dot(p, with_ones(v), preferred_element_type=jnp.float32)

    def keys(g, at, size):
        return kv_ref[prompt, pl.ds(at, size), pl.ds(g * 2 * HD, HD)]

    def vals(g, at, size):
        return kv_ref[prompt, pl.ds(at, size), pl.ds(g * 2 * HD + HD, HD)]

    def put(g, used, acc, m):
        m = jnp.broadcast_to(m, (GR * used, HD))
        for r in range(GR):
            acc_ref[g, r * bl:r * bl + used] = acc[r * used:(r + 1) * used]
            m_ref[g, r * bl:r * bl + used] = m[r * used:(r + 1) * used]

    def update(g, s, seen, v):
        s = jnp.where(seen, s, NEG)
        before = m_ref[g][:, :1]
        m = jnp.maximum(before, jnp.max(s, axis=1, keepdims=True))
        p = jnp.where(seen, jnp.exp2((s - m) * c2), 0.0).astype(jnp.bfloat16)
        acc_ref[g] = acc_ref[g] * jnp.exp2((before - m) * c2) + sums(p, v)
        m_ref[g] = jnp.broadcast_to(m, m_ref.shape[1:])

    def exact():
        acc_ref[...] = jnp.zeros_like(acc_ref)
        m_ref[...] = jnp.full_like(m_ref, NEG)

        def one(c, carry):
            at = pl.multiple_of(c * chunk, chunk)
            for g in range(heads):
                s = dot_nt(group(g, bl), keys(g, at, chunk))
                here = lax.broadcasted_iota(jnp.int32, s.shape, 1) + at
                update(g, s, here < valid, vals(g, at, chunk))
            return carry

        lax.fori_loop(0, (valid + chunk - 1) // chunk, one, 0)

    length = facts.length(block)

    @pl.when(valid == 0)
    def _():
        acc_ref[...] = jnp.zeros_like(acc_ref)
        m_ref[...] = jnp.full_like(m_ref, NEG)

    def single_pass(used, count):
        items = [(g, c) for c in range(count) for g in range(heads)]
        q = [group(g, used) for g in range(heads)]
        peaks = [None] * heads
        accs = [None] * heads
        ahead = dot_nt(q[0], keys(0, 0, chunk))
        for i, (g, c) in enumerate(items):
            s = ahead
            if i + 1 < len(items):
                ng, nc = items[i + 1]
                ahead = dot_nt(q[ng], keys(ng, nc * chunk, chunk))
            if c == count - 1:
                here = lax.broadcasted_iota(jnp.int32, s.shape, 1) + c * chunk
                s = jnp.where(here < valid, s, NEG)
            if c == 0:
                peaks[g] = jnp.max(s, axis=1, keepdims=True)
            p = jnp.exp2((s - peaks[g]) * c2).astype(jnp.bfloat16)
            part = sums(p, vals(g, c * chunk, chunk))
            accs[g] = part if c == 0 else accs[g] + part
        for g in range(heads):
            put(g, used, accs[g], peaks[g])

    for count in range(1, tile_len // chunk + 1):
        for used in range(ROUND, bl + 1, ROUND):
            some_keys = (valid > (count - 1) * chunk) & (valid <= count * chunk)
            some_rows = (length > used - ROUND) & (length <= used)
            pl.when(some_keys & some_rows)(functools.partial(single_pass, used, count))

    top = jnp.where(acc_ref[:, :, HD:] < BIG, 0.0, 1.0)

    @pl.when(jnp.max(top) > 0.5)
    def _():
        exact()

    if kx == 0:
        @pl.when(step == 0)
        def _():
            for g in range(heads):
                base = (first + g) * 2 * HD
                s = dot_nt(group(g, bl), own_ref[0, :, base:base + HD])
                row = lax.broadcasted_iota(jnp.int32, s.shape, 0) % bl
                col = lax.broadcasted_iota(jnp.int32, s.shape, 1)
                update(g, s, col <= row, own_ref[0, :, base + HD:base + 2 * HD])

    lane = lax.broadcasted_iota(jnp.int32, (bl, EXTRA), 1)
    total_tile = jnp.zeros((bl, EXTRA), jnp.float32)
    m_tile = jnp.zeros((bl, EXTRA), jnp.float32)
    for g in range(heads):
        total = acc_ref[g][:, HD:]
        out = (acc_ref[g][:, :HD] / jnp.where(total > 0.0, total, 1.0)).astype(jnp.bfloat16)
        for r in range(GR):
            h = g * GR + r
            at = slice(r * bl, (r + 1) * bl)
            out_ref[step, :, h * HD:(h + 1) * HD] = out[at]
            total_tile = jnp.where(lane == h, total[at], total_tile)
            m_tile = jnp.where(lane == h, m_ref[g, at], m_tile)
    some = total_tile > 0.0
    lse = m_tile * c2 + jnp.log2(jnp.where(some, total_tile, 1.0))
    out_ref[step, :, width:] = encode(jnp.where(some, lse, NEG))


def attend(grid, kx, meta, near, fars, cache, own, first, heads):
    zs, share, cols = near.shape
    bl = own.shape[1]
    tile_len = cache.shape[1]
    width = heads * GR * HD + EXTRA
    whole = pl.BlockSpec(memory_space=pltpu.VMEM)
    return pl.pallas_call(
        functools.partial(attend_kernel, grid, kx, bl, share, first, heads, tile_len),
        grid_spec=pltpu.PrefetchScalarGridSpec(
            num_scalar_prefetch=1,
            grid=(1,),
            in_specs=[whole] * (grid.xs + 2),
            out_specs=whole,
            scratch_shapes=[
                pltpu.VMEM((grid.n * share + bl + 8, cols), jnp.float32),
                pltpu.VMEM((heads, GR * bl, 2 * HD), jnp.float32),
                pltpu.VMEM((heads, GR * bl, HD), jnp.float32),
            ],
        ),
        out_shape=jax.ShapeDtypeStruct((zs, bl, width), jnp.bfloat16),
        compiler_params=pltpu.CompilerParams(vmem_limit_bytes=20 * MIB),
        cost_estimate=pl.CostEstimate(
            flops=8 * zs * bl * cols * tile_len,
            bytes_accessed=2 * zs * tile_len * heads * 2 * HD,
            transcendentals=zs * bl * heads * GR * tile_len,
        ),
        name="attend",
    )(meta, near, *fars, cache, own)


def finish_kernel(n, heads, bl, done, meta, *refs):
    sources, out_ref = refs[:-1], refs[-1]
    pieces = sources[done:]
    facts = Facts(n, meta)
    length = facts.length(facts.shard)
    row = lax.broadcasted_iota(jnp.int32, (bl, HD), 0)
    width = heads * GR * HD
    for c in range(done):
        out_ref[0, :, c * width:(c + 1) * width] = sources[c][0]
    parts, _ = merge(pieces, heads * GR)
    for h in range(heads * GR):
        at = done * width + h * HD
        out_ref[0, :, at:at + HD] = jnp.where(row < length, parts[h], 0.0).astype(jnp.bfloat16)


def finish(n, meta, done, pieces, heads):
    bl = pieces[0].shape[0]
    whole = pl.BlockSpec(memory_space=pltpu.VMEM)
    sources = list(done) + list(pieces)
    return pl.pallas_call(
        functools.partial(finish_kernel, n, heads, bl, len(done)),
        grid_spec=pltpu.PrefetchScalarGridSpec(
            num_scalar_prefetch=1,
            grid=(1,),
            in_specs=[whole] * len(sources),
            out_specs=whole,
        ),
        out_shape=jax.ShapeDtypeStruct((1, bl, (len(done) + 1) * heads * GR * HD), jnp.bfloat16),
        compiler_params=pltpu.CompilerParams(vmem_limit_bytes=16 * MIB),
        name="finish",
    )(meta, *sources)


def shards(
    hidden_rows,
    carried,
    query_weight,
    response_cache,
    prompt_cache,
    prompt_lengths,
    response_lengths,
    block_prompts,
):
    grid = Grid(lax.axis_size("seq"))
    bl = hidden_rows.shape[1]
    local_kv = response_cache.shape[2] // (2 * HD)
    share = bl * 5 // 8
    chunks = 2 if local_kv % 2 == 0 else 1
    heads = local_kv // chunks
    part_cols = heads * GR * HD
    place = jnp.stack([lax.axis_index("sec"), lax.axis_index("seq")]).astype(jnp.int32)
    meta = jnp.concatenate(
        [place, response_lengths.reshape(-1), block_prompts.reshape(-1), prompt_lengths]
    )

    def after(value, done):
        return lax.optimization_barrier((value, done))[0]

    def fetched(c):
        return fetch_cache(grid.n, meta, prompt_cache, heads * 2 * HD, c)

    handed = lax.ppermute(carried, "sec", [(0, 1)])
    depth = query_weight.shape[1]
    hidden = hidden_rows if depth % HD else fetch([hidden_rows])[0]
    slices = split(grid, meta, hidden, handed, depth)
    weight, own = fetch([query_weight, response_cache])
    x = [slices[0]] + [None] * (grid.n - 1)
    for kz in reversed(range(grid.zs)):
        for kx in reversed(range(grid.xs)):
            k = kx * grid.zs + kz
            if k:
                x[k] = grid.swap(slices[k], kx, kz)
    part = project(grid, meta, x, weight, bl, share, chunks)
    part = [piece.reshape(grid.zs, share, part_cols) for piece in part]
    part = [part[c * grid.xs:(c + 1) * grid.xs] for c in range(chunks)]

    def narrow(value):
        return (value * 0.125).astype(jnp.float16)

    def widen(value):
        return value.astype(jnp.float32) * 8.0

    def sum_x(c, done):
        parts = part[c]
        got = [grid.swap(after(narrow(parts[kx]), done), kx, 0) for kx in range(1, grid.xs)]
        return functools.reduce(jnp.add, [parts[0]] + [widen(value) for value in got]), got

    def sum_z(held, done):
        got = [grid.swap(after(narrow(held[kz]), done), 0, kz) for kz in range(1, grid.zs)]
        total = functools.reduce(jnp.add, [held[0]] + [widen(value) for value in got])
        return total.astype(jnp.bfloat16)

    def gather_z(mine):
        return [mine] + [grid.swap(mine, 0, kz) for kz in range(1, grid.zs)]

    def gather_x(near):
        return [near] + [grid.swap(near, kx, 0) for kx in range(1, grid.xs)]

    def call(c, kx, queries):
        return attend(
            grid, kx, meta, queries[0], queries[1:], caches[c], own, c * heads, heads,
        )

    def call_far(c, queries):
        outs = [call(c, kx, queries) for kx in range(1, grid.xs)]
        return outs, [grid.swap(out, kx + 1, 0) for kx, out in enumerate(outs)]

    def send_z(merged):
        return [merged[0]] + [grid.swap(merged[kz], 0, kz) for kz in range(1, grid.zs)]

    caches = [None] * chunks
    if chunks > 1:
        caches[1] = fetched(1)
        part[0][0] = after(part[0][0], caches[1])
    held, got = sum_x(0, ())
    mine = sum_z(held, ())
    column = gather_z(mine)
    caches[0] = fetched(0)
    near = jnp.stack(after(column, caches[0]))
    if chunks > 1:
        held, _ = sum_x(1, got)
        mine = sum_z(held, column)
    queries = gather_x(near)
    if chunks > 1:
        column = gather_z(mine)
        queries[0] = after(queries[0], mine)
    outs, mets = call_far(0, queries)
    if chunks > 1:
        near = jnp.stack(after(column, outs))
        later = gather_x(near)
        queries[0] = after(queries[0], near)
    held = call(0, 0, queries)
    if chunks > 1:
        later[0] = after(later[0], held)
        outs, later_mets = call_far(1, later)
        held = after(held, outs)
    merged = merge_column([held] + mets, heads * GR)
    pieces = send_z(merged)
    if chunks == 1:
        return finish(grid.n, meta, [], pieces, heads)
    later[0] = after(later[0], merged)
    held = call(1, 0, later)
    done = finish(grid.n, meta, [], pieces, heads)
    pieces = send_z(merge_column([held] + later_mets, heads * GR))
    return finish(grid.n, meta, [done], pieces, heads)


def solution(mesh):
    placed = (
        P("sec", "seq", None),
        P("sec", "seq", None),
        P("sec", "seq", "tp"),
        P("sec", "seq", "tp"),
        P("sec", None, "seq", "tp"),
        P(),
        P(),
        P(),
    )
    return jax.shard_map(
        shards, mesh=mesh, in_specs=placed, out_specs=P("sec", "seq", "tp"), check_vma=False
    )
```

```python
import functools
import math

import jax
import jax.numpy as jnp
from jax import lax
from jax.experimental import pallas as pl
from jax.experimental.pallas import tpu as pltpu
from jax.sharding import PartitionSpec as P

HD = 128
GR = 4
NEG = -1e30
LOG2E = 1.4426950408889634
CHUNK = 512
ROUND = 32
EXTRA = 128
SLOT = 16
BIG = 2.0 ** 100
MIB = 1024 * 1024


def dot_nt(a, b):
    return lax.dot_general(a, b, (((1,), (1,)), ((), ())), preferred_element_type=jnp.float32)


class Grid:
    def __init__(self, count):
        self.n = count
        self.xs = 1 << ((count.bit_length() - 1) // 2)
        self.zs = count // self.xs

    def owner(self, shard, kx, kz):
        z, x = shard // self.xs, shard % self.xs
        return (z ^ kz) * self.xs + (x ^ kx)

    def swap(self, value, kx, kz):
        pairs = [(s, self.owner(s, kx, kz)) for s in range(self.n)]
        return lax.ppermute(value, "seq", pairs)


class Facts:
    def __init__(self, n, meta):
        self.n, self.meta = n, meta
        self.section, self.shard = meta[0], meta[1]

    def length(self, block):
        return self.meta[2 + self.section * self.n + block]

    def prompt(self, block):
        return self.meta[2 + (2 + self.section) * self.n + block]

    def prompt_length(self, prompt):
        return self.meta[2 + 4 * self.n + prompt]


def split_kernel(grid, depth, meta, hidden_ref, handed_ref, *out_refs):
    for kx in range(grid.xs):
        for kz in range(grid.zs):
            at = pl.multiple_of(grid.owner(meta[1], kx, kz) * depth, HD)
            total = hidden_ref[0, :, pl.ds(at, depth)].astype(jnp.float32) + handed_ref[
                0, :, pl.ds(at, depth)
            ].astype(jnp.float32)
            out_refs[kx * grid.zs + kz][...] = total.astype(jnp.bfloat16)


def split(grid, meta, hidden, handed, depth):
    bl = hidden.shape[1]
    if depth % HD:
        total = (hidden[0].astype(jnp.float32) + handed[0].astype(jnp.float32)).astype(jnp.bfloat16)
        return [
            lax.dynamic_slice_in_dim(total, grid.owner(meta[1], kx, kz) * depth, depth, 1)
            for kx in range(grid.xs) for kz in range(grid.zs)
        ]
    whole = pl.BlockSpec(hidden.shape, lambda i, *m: (0, 0, 0))
    return pl.pallas_call(
        functools.partial(split_kernel, grid, depth),
        grid_spec=pltpu.PrefetchScalarGridSpec(
            num_scalar_prefetch=1,
            grid=(1,),
            in_specs=[whole, whole],
            out_specs=[pl.BlockSpec((bl, depth), lambda i, *m: (0, 0))] * grid.n,
        ),
        out_shape=[jax.ShapeDtypeStruct((bl, depth), jnp.bfloat16)] * grid.n,
        compiler_params=pltpu.CompilerParams(vmem_limit_bytes=16 * MIB),
        name="split",
    )(meta, hidden, handed)


def run_moves(moves):
    for needed, move in moves:
        if needed is None:
            move.start()
        else:
            pl.when(needed)(move.start)
    for needed, move in moves:
        if needed is None:
            move.wait()
        else:
            pl.when(needed)(move.wait)


def fetch_kernel(*refs):
    count = len(refs) // 2
    run_moves([
        (None, pltpu.make_async_copy(refs[i], refs[count + i], refs[-1].at[i]))
        for i in range(count)
    ])


def fetch(arrays):
    anywhere, near = pl.BlockSpec(memory_space=pltpu.HBM), pl.BlockSpec(memory_space=pltpu.VMEM)
    size = sum(math.prod(array.shape) for array in arrays)
    out = pl.pallas_call(
        fetch_kernel,
        in_specs=[anywhere] * len(arrays),
        out_specs=[near] * len(arrays),
        scratch_shapes=[pltpu.SemaphoreType.DMA((len(arrays),))],
        out_shape=[pltpu.VMEM(array.shape, array.dtype) for array in arrays],
        compiler_params=pltpu.CompilerParams(vmem_limit_bytes=4 * MIB),
        cost_estimate=pl.CostEstimate(flops=0, bytes_accessed=2 * size, transcendentals=0),
        name="fetch",
    )(*[pltpu.with_memory_space_constraint(array, pltpu.HBM) for array in arrays])
    return [pltpu.with_memory_space_constraint(array, pltpu.VMEM) for array in out]


def fetch_cache_kernel(n, chunk, width, first, meta, cache_ref, kv_ref, sem):
    count, tile_len = kv_ref.shape[:2]
    facts = Facts(n, meta)
    moves = []
    for p in range(count):
        asked = facts.prompt(0) == p
        for b in range(1, n):
            asked = asked | (facts.prompt(b) == p)
        for c in range(tile_len // chunk):
            at = pl.ds(c * chunk, chunk)
            needed = asked & (facts.prompt_length(p) > facts.shard * tile_len + c * chunk)
            moves.append((needed, pltpu.make_async_copy(
                cache_ref.at[0, p, at, pl.ds(first * width, width)], kv_ref.at[p, at],
                sem.at[p, c],
            )))
    run_moves(moves)


def fetch_cache(n, meta, cache, width, first):
    count, tile_len = cache.shape[1:3]
    chunk = min(CHUNK, tile_len)
    shape = (count, tile_len, width)
    out = pl.pallas_call(
        functools.partial(fetch_cache_kernel, n, chunk, width, first),
        grid_spec=pltpu.PrefetchScalarGridSpec(
            num_scalar_prefetch=1,
            grid=(1,),
            in_specs=[pl.BlockSpec(memory_space=pltpu.HBM)],
            out_specs=pl.BlockSpec(memory_space=pltpu.VMEM),
            scratch_shapes=[pltpu.SemaphoreType.DMA((count, tile_len // chunk))],
        ),
        out_shape=pltpu.VMEM(shape, cache.dtype),
        compiler_params=pltpu.CompilerParams(vmem_limit_bytes=4 * MIB),
        cost_estimate=pl.CostEstimate(
            flops=0, bytes_accessed=2 * math.prod(shape), transcendentals=0
        ),
        name="fetch_cache",
    )(meta, pltpu.with_memory_space_constraint(cache, pltpu.HBM))
    return pltpu.with_memory_space_constraint(out, pltpu.VMEM)


def project_kernel(grid, bl, share, meta, *refs):
    x_refs, w_ref, refs = refs[:grid.n], refs[grid.n], refs[grid.n + 1:]
    out_refs, (xp_ref, starts) = refs[:-2], refs[-2:]

    @pl.when(pl.program_id(0) == 0)
    def _():
        facts = Facts(grid.n, meta)
        shard = facts.shard
        offset = jnp.int32(0)
        for b in range(grid.n):
            starts[b] = offset
            offset = offset + facts.length(b)
        lane = lax.broadcasted_iota(jnp.int32, (8, grid.n * bl), 1)
        target = jnp.full(lane.shape, -1, jnp.int32)
        owners = [
            grid.owner(shard, kx, kz) for kx in range(grid.xs) for kz in range(grid.zs)
        ]
        for k, b in enumerate(owners):
            order = lane - k * bl
            used = (order >= 0) & (order < facts.length(b))
            target = jnp.where(used, order + starts[b], target)
        row = lax.broadcasted_iota(jnp.int32, (share, grid.n * bl), 0)
        target = jnp.broadcast_to(target[:1], row.shape)
        picks = [jnp.where(row + b * share == target, 1.0, 0.0) for b in owners]
        pick = jnp.concatenate(picks, axis=0).astype(jnp.bfloat16)
        x = jnp.concatenate([ref[...] for ref in x_refs], axis=0)
        chosen = jnp.dot(pick, x, preferred_element_type=jnp.float32)
        xp_ref[...] = chosen.astype(jnp.bfloat16)

    result = jnp.dot(xp_ref[...], w_ref[0], preferred_element_type=jnp.float32)
    rows = grid.zs * share
    for i, out_ref in enumerate(out_refs):
        chunk, kx = i // grid.xs, i % grid.xs

        @pl.when(pl.program_id(0) == chunk)
        def _(out_ref=out_ref, kx=kx):
            out_ref[...] = result[kx * rows:(kx + 1) * rows]


def project(grid, meta, xs, w, bl, share, chunks):
    k, cols = w.shape[1:]
    rows = grid.n * share
    tile = cols // chunks
    piece = (grid.zs * share, tile)
    return pl.pallas_call(
        functools.partial(project_kernel, grid, bl, share),
        grid_spec=pltpu.PrefetchScalarGridSpec(
            num_scalar_prefetch=1,
            grid=(chunks,),
            in_specs=[pl.BlockSpec((bl, k), lambda j, *m: (0, 0))] * grid.n
            + [pl.BlockSpec((1, k, tile), lambda j, *m: (0, 0, j))],
            out_specs=[pl.BlockSpec(piece, lambda j, *m: (0, 0))] * (chunks * grid.xs),
            scratch_shapes=[
                pltpu.VMEM((rows, k), jnp.bfloat16), pltpu.SMEM((grid.n,), jnp.int32)
            ],
        ),
        out_shape=[jax.ShapeDtypeStruct(piece, jnp.float32)] * (chunks * grid.xs),
        compiler_params=pltpu.CompilerParams(vmem_limit_bytes=20 * MIB),
        cost_estimate=pl.CostEstimate(
            flops=2 * rows * k * cols, bytes_accessed=2 * k * cols + 4 * rows * cols,
            transcendentals=0,
        ),
        name="project",
    )(meta, *xs, w)


def three_terms(value):
    high = value.astype(jnp.bfloat16).astype(jnp.float32)
    mid = (value - high).astype(jnp.bfloat16).astype(jnp.float32)
    return [high, mid, value - high - mid]


def encode(peak, total):
    lane = lax.broadcasted_iota(jnp.int32, peak.shape, 1)
    out = jnp.zeros(peak.shape, jnp.float32)
    for i, term in enumerate(three_terms(peak) + three_terms(total)):
        term = jnp.where(lane < SLOT, term, 0.0)
        out = out + (pltpu.roll(term, i * SLOT, 1) if i else term)
    return out.astype(jnp.bfloat16)


def decode(tile):
    terms = tile.astype(jnp.float32)
    parts = [terms] + [pltpu.roll(terms, EXTRA - i * SLOT, 1) for i in range(1, 6)]
    return parts[0] + parts[1] + parts[2], parts[3] + parts[4] + parts[5]


def merge(refs, heads):
    width = heads * HD
    peaks, totals = zip(*[decode(ref[:, width:]) for ref in refs])
    rows = peaks[0].shape[0]
    peak = functools.reduce(jnp.maximum, peaks)
    weights = [jnp.exp2(one - peak) for one in peaks]
    total = functools.reduce(jnp.add, [w * one for w, one in zip(weights, totals)])
    out = []
    for h in range(heads):
        terms = [
            jnp.broadcast_to(weight[:, h:h + 1], (rows, HD))
            * ref[:, h * HD:(h + 1) * HD].astype(jnp.float32)
            for weight, ref in zip(weights, refs)
        ]
        out.append(functools.reduce(jnp.add, terms))
    return out, peak, total


def merge_kernel(zs, heads, *refs):
    sources, outs = refs[:-zs], refs[-zs:]
    for kz in range(zs):
        parts, peak, total = merge([ref.at[kz] for ref in sources], heads)
        for h in range(heads):
            outs[kz][:, h * HD:(h + 1) * HD] = parts[h].astype(jnp.bfloat16)
        outs[kz][:, heads * HD:] = encode(peak, total)


def merge_column(sources, heads):
    zs, bl, width = sources[0].shape
    return pl.pallas_call(
        functools.partial(merge_kernel, zs, heads),
        out_shape=[jax.ShapeDtypeStruct((bl, width), jnp.bfloat16)] * zs,
        compiler_params=pltpu.CompilerParams(vmem_limit_bytes=16 * MIB),
        name="merge",
    )(*sources)


def attend_kernel(grid, kx, bl, share, first, heads, tile_len, meta, *refs):
    near_ref, far_refs = refs[0], refs[1:grid.xs]
    kv_refs, refs = refs[grid.xs:grid.xs + heads], refs[grid.xs + heads:]
    own_ref, out_ref, q32_ref, acc_ref, m_ref = refs
    facts = Facts(grid.n, meta)
    shard = facts.shard
    rows = grid.n * share
    for fx in range(grid.xs):
        for fz in range(grid.zs):
            source = near_ref if fx == 0 else far_refs[fx - 1]
            at = pl.multiple_of(grid.owner(shard, fx, fz) * share, 8)
            q32_ref[pl.ds(at, share), :] = source[fz].astype(jnp.float32)
    q32_ref[rows:, :] = jnp.zeros((bl + 8, q32_ref.shape[1]), jnp.float32)
    acc_ref[...] = jnp.zeros_like(acc_ref)
    m_ref[...] = jnp.full_like(m_ref, NEG)

    def one(kz, carry):
        attend_block(
            grid, kx, bl, first, heads, tile_len, kz, facts,
            kv_refs, own_ref, out_ref, q32_ref, acc_ref, m_ref,
        )
        return carry

    lax.fori_loop(0, grid.zs, one, 0)


def attend_block(grid, kx, bl, first, heads, tile_len, step, facts,
                 kv_refs, own_ref, out_ref, q32_ref, acc_ref, m_ref):
    block = grid.owner(facts.shard, kx, step)
    offset = jnp.int32(0)
    for b in range(grid.n):
        offset = offset + jnp.where(b < block, facts.length(b), 0)
    prompt = facts.prompt(block)
    valid = jnp.clip(facts.prompt_length(prompt) - facts.shard * tile_len, 0, tile_len)
    c2 = LOG2E / math.sqrt(HD)
    chunk = min(CHUNK, tile_len)
    width = heads * GR * HD

    rest = offset % 8
    window = q32_ref[pl.ds(pl.multiple_of(offset - rest, 8), bl + 8), :]
    window = pltpu.roll(window, jnp.where(rest == 0, 0, bl + 8 - rest), 0)
    queries = window[:bl].astype(jnp.bfloat16)

    def group(g, used):
        return jnp.concatenate(
            [queries[:used, (g * GR + r) * HD:(g * GR + r + 1) * HD] for r in range(GR)], axis=0
        )

    def with_ones(v):
        return jnp.concatenate([v, jnp.ones(v.shape, jnp.bfloat16)], axis=1)

    def sums(p, v):
        return jnp.dot(p, with_ones(v), preferred_element_type=jnp.float32)

    def keys(g, at, size):
        return kv_refs[g][prompt, pl.ds(at, size), :HD]

    def vals(g, at, size):
        return kv_refs[g][prompt, pl.ds(at, size), HD:]

    def put(g, used, acc, m):
        m = jnp.broadcast_to(m, (GR * used, HD))
        for r in range(GR):
            acc_ref[g, r * bl:r * bl + used] = acc[r * used:(r + 1) * used]
            m_ref[g, r * bl:r * bl + used] = m[r * used:(r + 1) * used]

    def update(g, s, seen, v):
        s = jnp.where(seen, s, NEG)
        before = m_ref[g][:, :1]
        m = jnp.maximum(before, jnp.max(s, axis=1, keepdims=True))
        p = jnp.where(seen, jnp.exp2((s - m) * c2), 0.0).astype(jnp.bfloat16)
        acc_ref[g] = acc_ref[g] * jnp.exp2((before - m) * c2) + sums(p, v)
        m_ref[g] = jnp.broadcast_to(m, m_ref.shape[1:])

    def exact():
        acc_ref[...] = jnp.zeros_like(acc_ref)
        m_ref[...] = jnp.full_like(m_ref, NEG)

        def one(c, carry):
            at = pl.multiple_of(c * chunk, chunk)
            for g in range(heads):
                s = dot_nt(group(g, bl), keys(g, at, chunk))
                here = lax.broadcasted_iota(jnp.int32, s.shape, 1) + at
                update(g, s, here < valid, vals(g, at, chunk))
            return carry

        lax.fori_loop(0, (valid + chunk - 1) // chunk, one, 0)

    length = facts.length(block)

    @pl.when(valid == 0)
    def _():
        acc_ref[...] = jnp.zeros_like(acc_ref)
        m_ref[...] = jnp.full_like(m_ref, NEG)

    def single_pass(used, count):
        items = [(g, c) for c in range(count) for g in range(heads)]
        q = [group(g, used) for g in range(heads)]
        peaks = [None] * heads
        accs = [None] * heads
        ahead = dot_nt(q[0], keys(0, 0, chunk))
        for i, (g, c) in enumerate(items):
            s = ahead
            if i + 1 < len(items):
                ng, nc = items[i + 1]
                ahead = dot_nt(q[ng], keys(ng, nc * chunk, chunk))
            if c == count - 1:
                here = lax.broadcasted_iota(jnp.int32, s.shape, 1) + c * chunk
                s = jnp.where(here < valid, s, NEG)
            if c == 0:
                peaks[g] = jnp.max(s, axis=1, keepdims=True)
            p = jnp.exp2((s - peaks[g]) * c2).astype(jnp.bfloat16)
            part = sums(p, vals(g, c * chunk, chunk))
            accs[g] = part if c == 0 else accs[g] + part
        for g in range(heads):
            put(g, used, accs[g], peaks[g])

    for count in range(1, tile_len // chunk + 1):
        for used in range(ROUND, bl + 1, ROUND):
            some_keys = (valid > (count - 1) * chunk) & (valid <= count * chunk)
            some_rows = (length > used - ROUND) & (length <= used)
            pl.when(some_keys & some_rows)(functools.partial(single_pass, used, count))

    def own_part():
        @pl.when(step == 0)
        def _():
            for g in range(heads):
                base = (first + g) * 2 * HD
                s = dot_nt(group(g, bl), own_ref[0, :, base:base + HD])
                row = lax.broadcasted_iota(jnp.int32, s.shape, 0) % bl
                col = lax.broadcasted_iota(jnp.int32, s.shape, 1)
                update(g, s, col <= row, own_ref[0, :, base + HD:base + 2 * HD])

    def write():
        lane = lax.broadcasted_iota(jnp.int32, (bl, EXTRA), 1)
        total = jnp.zeros((bl, EXTRA), jnp.float32)
        peak = jnp.zeros((bl, EXTRA), jnp.float32)
        for g in range(heads):
            for r in range(GR):
                h = g * GR + r
                at = slice(r * bl, (r + 1) * bl)
                out_ref[step, :, h * HD:(h + 1) * HD] = acc_ref[g, at, :HD].astype(jnp.bfloat16)
                total = jnp.where(lane == h, acc_ref[g, at, HD:], total)
                peak = jnp.where(lane == h, m_ref[g, at], peak)
        out_ref[step, :, width:] = encode(peak * c2, total)
        return total

    if kx == 0:
        own_part()
    total = write()

    @pl.when(jnp.max(jnp.where(total < BIG, 0.0, 1.0)) > 0.5)
    def _():
        exact()
        if kx == 0:
            own_part()
        write()


def attend(grid, kx, meta, near, fars, caches, own, first, heads):
    zs, share, cols = near.shape
    bl = own.shape[1]
    tile_len = caches[0].shape[1]
    width = heads * GR * HD + EXTRA
    whole = pl.BlockSpec(memory_space=pltpu.VMEM)
    return pl.pallas_call(
        functools.partial(attend_kernel, grid, kx, bl, share, first, heads, tile_len),
        grid_spec=pltpu.PrefetchScalarGridSpec(
            num_scalar_prefetch=1,
            grid=(1,),
            in_specs=[whole] * (grid.xs + heads + 1),
            out_specs=whole,
            scratch_shapes=[
                pltpu.VMEM((grid.n * share + bl + 8, cols), jnp.float32),
                pltpu.VMEM((heads, GR * bl, 2 * HD), jnp.float32),
                pltpu.VMEM((heads, GR * bl, HD), jnp.float32),
            ],
        ),
        out_shape=jax.ShapeDtypeStruct((zs, bl, width), jnp.bfloat16),
        compiler_params=pltpu.CompilerParams(vmem_limit_bytes=20 * MIB),
        cost_estimate=pl.CostEstimate(
            flops=8 * zs * bl * cols * tile_len,
            bytes_accessed=2 * zs * tile_len * heads * 2 * HD,
            transcendentals=zs * bl * heads * GR * tile_len,
        ),
        name="attend",
    )(meta, near, *fars, *caches, own)


def finish_kernel(n, heads, bl, done, meta, *refs):
    sources, out_ref = refs[:-1], refs[-1]
    pieces = sources[done:]
    facts = Facts(n, meta)
    length = facts.length(facts.shard)
    row = lax.broadcasted_iota(jnp.int32, (bl, HD), 0)
    width = heads * GR * HD
    for c in range(done):
        out_ref[0, :, c * width:(c + 1) * width] = sources[c][0]
    parts, _, total = merge(pieces, heads * GR)
    for h in range(heads * GR):
        at = done * width + h * HD
        value = parts[h] / jnp.broadcast_to(total[:, h:h + 1], (bl, HD))
        out_ref[0, :, at:at + HD] = jnp.where(row < length, value, 0.0).astype(jnp.bfloat16)


def finish(n, meta, done, pieces, heads):
    bl = pieces[0].shape[0]
    whole = pl.BlockSpec(memory_space=pltpu.VMEM)
    sources = list(done) + list(pieces)
    return pl.pallas_call(
        functools.partial(finish_kernel, n, heads, bl, len(done)),
        grid_spec=pltpu.PrefetchScalarGridSpec(
            num_scalar_prefetch=1,
            grid=(1,),
            in_specs=[whole] * len(sources),
            out_specs=whole,
        ),
        out_shape=jax.ShapeDtypeStruct((1, bl, (len(done) + 1) * heads * GR * HD), jnp.bfloat16),
        compiler_params=pltpu.CompilerParams(vmem_limit_bytes=16 * MIB),
        name="finish",
    )(meta, *sources)


def shards(
    hidden_rows,
    carried,
    query_weight,
    response_cache,
    prompt_cache,
    prompt_lengths,
    response_lengths,
    block_prompts,
):
    grid = Grid(lax.axis_size("seq"))
    bl = hidden_rows.shape[1]
    local_kv = response_cache.shape[2] // (2 * HD)
    share = bl * 5 // 8
    chunks = 2 if local_kv % 2 == 0 else 1
    heads = local_kv // chunks
    part_cols = heads * GR * HD
    place = jnp.stack([lax.axis_index("sec"), lax.axis_index("seq")]).astype(jnp.int32)

    def after(value, done):
        return lax.optimization_barrier((value, done))[0]

    def fetched(head, done=()):
        return fetch_cache(grid.n, after(meta, done), prompt_cache, 2 * HD, head)

    handed = lax.ppermute(carried, "sec", [(0, 1)])
    depth = query_weight.shape[1]
    hidden = hidden_rows if depth % HD else fetch([hidden_rows])[0]
    slices = split(grid, place, hidden, handed, depth)
    later_place = after(place, slices[0])
    prompts = block_prompts[:, :, 0]
    meta = jnp.concatenate(
        [later_place] + [a[i] for a in (response_lengths, prompts) for i in range(2)]
        + [prompt_lengths]
    )
    weight, own = fetch([query_weight, response_cache])
    x = [slices[0]] + [None] * (grid.n - 1)
    for kz in reversed(range(grid.zs)):
        for kx in reversed(range(grid.xs)):
            k = kx * grid.zs + kz
            if k:
                x[k] = grid.swap(slices[k], kx, kz)
    part = project(grid, meta, x, weight, bl, share, chunks)
    part = [piece.reshape(grid.zs, share, part_cols) for piece in part]
    part = [part[c * grid.xs:(c + 1) * grid.xs] for c in range(chunks)]

    def narrow(value):
        return (value * 0.125).astype(jnp.float16)

    def widen(value):
        return value.astype(jnp.float32) * 8.0

    def sum_x(c, done):
        parts = part[c]
        got = [grid.swap(after(narrow(parts[kx]), done), kx, 0) for kx in range(1, grid.xs)]
        return functools.reduce(jnp.add, [parts[0]] + [widen(value) for value in got]), got

    def narrow_z(held, done):
        return [after(narrow(held[kz]), done) for kz in range(1, grid.zs)]

    def sum_z(held, sends, beside):
        got = [grid.swap(send, 0, kz + 1) for kz, send in enumerate(sends)]
        parts = [after(held[0], beside)] + [widen(value) for value in got]
        return functools.reduce(jnp.add, parts).astype(jnp.bfloat16)

    def gather_z(mine):
        return [mine] + [grid.swap(mine, 0, kz) for kz in range(1, grid.zs)]

    def gather_x(near):
        return [near] + [grid.swap(near, kx, 0) for kx in range(1, grid.xs)]

    def call(c, kx, queries):
        return attend(
            grid, kx, meta, queries[0], queries[1:], caches[c * heads:(c + 1) * heads], own,
            c * heads, heads,
        )

    def call_far(c, queries):
        outs = [call(c, kx, queries) for kx in range(1, grid.xs)]
        return outs, [grid.swap(out, kx + 1, 0) for kx, out in enumerate(outs)]

    def send_z(merged):
        return [merged[0]] + [grid.swap(merged[kz], 0, kz) for kz in range(1, grid.zs)]

    half = (local_kv + 1) // 4
    caches = [fetched(head) for head in range(half)]
    part[0][0] = after(part[0][0], caches)
    held, got = sum_x(0, ())
    caches += [fetched(head) for head in range(half, heads)]
    mine = sum_z(held, narrow_z(held, ()), caches)
    column = gather_z(mine)
    if chunks > 1:
        later_held, _ = sum_x(1, got)
        sends = narrow_z(later_held, mine)
        caches += [fetched(head, mine) for head in range(heads, local_kv)]
        column = after(column, (caches[:heads + half], sends))
    queries = gather_x(jnp.stack(column))
    outs, mets = call_far(0, queries)
    if chunks > 1:
        mine = sum_z(later_held, sends, (caches, outs))
        column = gather_z(mine)
        queries[0] = after(queries[0], mine)
    held = call(0, 0, queries)
    if chunks > 1:
        near = jnp.stack(after(column, held))
        later = gather_x(near)
        held = after(held, near)
    merged = merge_column([held] + mets, heads * GR)
    pieces = send_z(merged)
    if chunks == 1:
        return finish(grid.n, meta, [], pieces, heads)
    later[0] = after(later[0], merged)
    outs, mets = call_far(1, later)
    later[0] = after(later[0], outs)
    held = call(1, 0, later)
    done = finish(grid.n, meta, [], pieces, heads)
    pieces = send_z(merge_column([held] + mets, heads * GR))
    return finish(grid.n, meta, [done], pieces, heads)


def solution(mesh):
    placed = (
        P("sec", "seq", None),
        P("sec", "seq", None),
        P("sec", "seq", "tp"),
        P("sec", "seq", "tp"),
        P("sec", None, "seq", "tp"),
        P(),
        P(),
        P(),
    )
    return jax.shard_map(
        shards, mesh=mesh, in_specs=placed, out_specs=P("sec", "seq", "tp"), check_vma=False
    )
```

```python
import functools
import math

import jax
import jax.numpy as jnp
from jax import lax
from jax.experimental import pallas as pl
from jax.experimental.pallas import tpu as pltpu
from jax.sharding import PartitionSpec as P

HD = 128
GR = 4
NEG = -1e30
LOG2E = 1.4426950408889634
CHUNK = 512
ROUND = 32
EXTRA = 128
SLOT = 16
BIG = 2.0 ** 100
MIB = 1024 * 1024


def dot_nt(a, b):
    return lax.dot_general(a, b, (((1,), (1,)), ((), ())), preferred_element_type=jnp.float32)


class Grid:
    def __init__(self, count):
        self.n = count
        self.xs = 1 << ((count.bit_length() - 1) // 2)
        self.zs = count // self.xs

    def owner(self, shard, kx, kz):
        z, x = shard // self.xs, shard % self.xs
        return (z ^ kz) * self.xs + (x ^ kx)

    def swap(self, value, kx, kz):
        pairs = [(s, self.owner(s, kx, kz)) for s in range(self.n)]
        return lax.ppermute(value, "seq", pairs)


class Facts:
    def __init__(self, n, meta):
        self.n, self.meta = n, meta
        self.section, self.shard = meta[0], meta[1]

    def length(self, block):
        return self.meta[2 + self.section * self.n + block]

    def prompt(self, block):
        return self.meta[2 + (2 + self.section) * self.n + block]

    def prompt_length(self, prompt):
        return self.meta[2 + 4 * self.n + prompt]


def split_kernel(grid, depth, meta, hidden_ref, handed_ref, *out_refs):
    for kx in range(grid.xs):
        for kz in range(grid.zs):
            at = pl.multiple_of(grid.owner(meta[1], kx, kz) * depth, HD)
            total = hidden_ref[0, :, pl.ds(at, depth)].astype(jnp.float32) + handed_ref[
                0, :, pl.ds(at, depth)
            ].astype(jnp.float32)
            out_refs[kx * grid.zs + kz][...] = total.astype(jnp.bfloat16)


def split(grid, meta, hidden, handed, depth):
    bl = hidden.shape[1]
    if depth % HD:
        total = (hidden[0].astype(jnp.float32) + handed[0].astype(jnp.float32)).astype(jnp.bfloat16)
        return [
            lax.dynamic_slice_in_dim(total, grid.owner(meta[1], kx, kz) * depth, depth, 1)
            for kx in range(grid.xs) for kz in range(grid.zs)
        ]
    whole = pl.BlockSpec(hidden.shape, lambda i, *m: (0, 0, 0))
    return pl.pallas_call(
        functools.partial(split_kernel, grid, depth),
        grid_spec=pltpu.PrefetchScalarGridSpec(
            num_scalar_prefetch=1,
            grid=(1,),
            in_specs=[whole, whole],
            out_specs=[pl.BlockSpec((bl, depth), lambda i, *m: (0, 0))] * grid.n,
        ),
        out_shape=[jax.ShapeDtypeStruct((bl, depth), jnp.bfloat16)] * grid.n,
        compiler_params=pltpu.CompilerParams(vmem_limit_bytes=16 * MIB),
        name="split",
    )(meta, hidden, handed)


def run_moves(moves):
    for needed, move in moves:
        if needed is None:
            move.start()
        else:
            pl.when(needed)(move.start)
    for needed, move in moves:
        if needed is None:
            move.wait()
        else:
            pl.when(needed)(move.wait)


def fetch_kernel(*refs):
    count = len(refs) // 2
    run_moves([
        (None, pltpu.make_async_copy(refs[i], refs[count + i], refs[-1].at[i]))
        for i in range(count)
    ])


def fetch(arrays):
    anywhere, near = pl.BlockSpec(memory_space=pltpu.HBM), pl.BlockSpec(memory_space=pltpu.VMEM)
    size = sum(math.prod(array.shape) for array in arrays)
    out = pl.pallas_call(
        fetch_kernel,
        in_specs=[anywhere] * len(arrays),
        out_specs=[near] * len(arrays),
        scratch_shapes=[pltpu.SemaphoreType.DMA((len(arrays),))],
        out_shape=[pltpu.VMEM(array.shape, array.dtype) for array in arrays],
        compiler_params=pltpu.CompilerParams(vmem_limit_bytes=4 * MIB),
        cost_estimate=pl.CostEstimate(flops=0, bytes_accessed=2 * size, transcendentals=0),
        name="fetch",
    )(*[pltpu.with_memory_space_constraint(array, pltpu.HBM) for array in arrays])
    return [pltpu.with_memory_space_constraint(array, pltpu.VMEM) for array in out]


def fetch_cache_kernel(n, chunk, width, first, meta, cache_ref, kv_ref, sem):
    count, tile_len = kv_ref.shape[:2]
    facts = Facts(n, meta)
    moves = []
    for p in range(count):
        asked = facts.prompt(0) == p
        for b in range(1, n):
            asked = asked | (facts.prompt(b) == p)
        for c in range(tile_len // chunk):
            at = pl.ds(c * chunk, chunk)
            needed = asked & (facts.prompt_length(p) > facts.shard * tile_len + c * chunk)
            moves.append((needed, pltpu.make_async_copy(
                cache_ref.at[0, p, at, pl.ds(first * width, width)], kv_ref.at[p, at],
                sem.at[p, c],
            )))
    run_moves(moves)


def fetch_cache(n, meta, cache, width, first):
    count, tile_len = cache.shape[1:3]
    chunk = min(CHUNK, tile_len)
    shape = (count, tile_len, width)
    out = pl.pallas_call(
        functools.partial(fetch_cache_kernel, n, chunk, width, first),
        grid_spec=pltpu.PrefetchScalarGridSpec(
            num_scalar_prefetch=1,
            grid=(1,),
            in_specs=[pl.BlockSpec(memory_space=pltpu.HBM)],
            out_specs=pl.BlockSpec(memory_space=pltpu.VMEM),
            scratch_shapes=[pltpu.SemaphoreType.DMA((count, tile_len // chunk))],
        ),
        out_shape=pltpu.VMEM(shape, cache.dtype),
        compiler_params=pltpu.CompilerParams(vmem_limit_bytes=4 * MIB),
        cost_estimate=pl.CostEstimate(
            flops=0, bytes_accessed=2 * math.prod(shape), transcendentals=0
        ),
        name="fetch_cache",
    )(meta, pltpu.with_memory_space_constraint(cache, pltpu.HBM))
    return pltpu.with_memory_space_constraint(out, pltpu.VMEM)


def project_kernel(grid, bl, share, meta, *refs):
    x_refs, w_ref, refs = refs[:grid.n], refs[grid.n], refs[grid.n + 1:]
    out_refs, (xp_ref, starts) = refs[:-2], refs[-2:]

    @pl.when(pl.program_id(0) == 0)
    def _():
        facts = Facts(grid.n, meta)
        shard = facts.shard
        offset = jnp.int32(0)
        for b in range(grid.n):
            starts[b] = offset
            offset = offset + facts.length(b)
        lane = lax.broadcasted_iota(jnp.int32, (8, grid.n * bl), 1)
        target = jnp.full(lane.shape, -1, jnp.int32)
        owners = [
            grid.owner(shard, kx, kz) for kx in range(grid.xs) for kz in range(grid.zs)
        ]
        for k, b in enumerate(owners):
            order = lane - k * bl
            used = (order >= 0) & (order < facts.length(b))
            target = jnp.where(used, order + starts[b], target)
        row = lax.broadcasted_iota(jnp.int32, (share, grid.n * bl), 0)
        target = jnp.broadcast_to(target[:1], row.shape)
        picks = [jnp.where(row + b * share == target, 1.0, 0.0) for b in owners]
        pick = jnp.concatenate(picks, axis=0).astype(jnp.bfloat16)
        x = jnp.concatenate([ref[...] for ref in x_refs], axis=0)
        chosen = jnp.dot(pick, x, preferred_element_type=jnp.float32)
        xp_ref[...] = chosen.astype(jnp.bfloat16)

    result = jnp.dot(xp_ref[...], w_ref[0], preferred_element_type=jnp.float32)
    rows = grid.zs * share
    for i, out_ref in enumerate(out_refs):
        chunk, kx = i // grid.xs, i % grid.xs

        @pl.when(pl.program_id(0) == chunk)
        def _(out_ref=out_ref, kx=kx):
            out_ref[...] = result[kx * rows:(kx + 1) * rows]


def project(grid, meta, xs, w, bl, share, chunks):
    k, cols = w.shape[1:]
    rows = grid.n * share
    tile = cols // chunks
    piece = (grid.zs * share, tile)
    return pl.pallas_call(
        functools.partial(project_kernel, grid, bl, share),
        grid_spec=pltpu.PrefetchScalarGridSpec(
            num_scalar_prefetch=1,
            grid=(chunks,),
            in_specs=[pl.BlockSpec((bl, k), lambda j, *m: (0, 0))] * grid.n
            + [pl.BlockSpec((1, k, tile), lambda j, *m: (0, 0, j))],
            out_specs=[pl.BlockSpec(piece, lambda j, *m: (0, 0))] * (chunks * grid.xs),
            scratch_shapes=[
                pltpu.VMEM((rows, k), jnp.bfloat16), pltpu.SMEM((grid.n,), jnp.int32)
            ],
        ),
        out_shape=[jax.ShapeDtypeStruct(piece, jnp.float32)] * (chunks * grid.xs),
        compiler_params=pltpu.CompilerParams(vmem_limit_bytes=20 * MIB),
        cost_estimate=pl.CostEstimate(
            flops=2 * rows * k * cols, bytes_accessed=2 * k * cols + 4 * rows * cols,
            transcendentals=0,
        ),
        name="project",
    )(meta, *xs, w)


def three_terms(value):
    high = value.astype(jnp.bfloat16).astype(jnp.float32)
    mid = (value - high).astype(jnp.bfloat16).astype(jnp.float32)
    return [high, mid, value - high - mid]


def encode(peak, total):
    lane = lax.broadcasted_iota(jnp.int32, peak.shape, 1)
    out = jnp.zeros(peak.shape, jnp.float32)
    for i, term in enumerate(three_terms(peak) + three_terms(total)):
        term = jnp.where(lane < SLOT, term, 0.0)
        out = out + (pltpu.roll(term, i * SLOT, 1) if i else term)
    return out.astype(jnp.bfloat16)


def decode(tile):
    terms = tile.astype(jnp.float32)
    parts = [terms] + [pltpu.roll(terms, EXTRA - i * SLOT, 1) for i in range(1, 6)]
    return parts[0] + parts[1] + parts[2], parts[3] + parts[4] + parts[5]


def merge(refs, heads):
    width = heads * HD
    peaks, totals = zip(*[decode(ref[:, width:]) for ref in refs])
    rows = peaks[0].shape[0]
    peak = functools.reduce(jnp.maximum, peaks)
    weights = [jnp.exp2(one - peak) for one in peaks]
    total = functools.reduce(jnp.add, [w * one for w, one in zip(weights, totals)])
    out = []
    for h in range(heads):
        terms = [
            jnp.broadcast_to(weight[:, h:h + 1], (rows, HD))
            * ref[:, h * HD:(h + 1) * HD].astype(jnp.float32)
            for weight, ref in zip(weights, refs)
        ]
        out.append(functools.reduce(jnp.add, terms))
    return out, peak, total


def merge_kernel(zs, heads, *refs):
    sources, outs = refs[:-zs], refs[-zs:]
    for kz in range(zs):
        parts, peak, total = merge([ref.at[kz] for ref in sources], heads)
        for h in range(heads):
            outs[kz][:, h * HD:(h + 1) * HD] = parts[h].astype(jnp.bfloat16)
        outs[kz][:, heads * HD:] = encode(peak, total)


def merge_column(sources, heads):
    zs, bl, width = sources[0].shape
    return pl.pallas_call(
        functools.partial(merge_kernel, zs, heads),
        out_shape=[jax.ShapeDtypeStruct((bl, width), jnp.bfloat16)] * zs,
        compiler_params=pltpu.CompilerParams(vmem_limit_bytes=16 * MIB),
        name="merge",
    )(*sources)


def attend_kernel(grid, kx, bl, share, first, heads, tile_len, meta, *refs):
    near_ref, far_refs = refs[0], refs[1:grid.xs]
    kv_refs, refs = refs[grid.xs:grid.xs + heads], refs[grid.xs + heads:]
    own_ref, out_ref, q32_ref, acc_ref, m_ref = refs
    facts = Facts(grid.n, meta)
    shard = facts.shard
    rows = grid.n * share
    for fx in range(grid.xs):
        for fz in range(grid.zs):
            source = near_ref if fx == 0 else far_refs[fx - 1]
            at = pl.multiple_of(grid.owner(shard, fx, fz) * share, 8)
            q32_ref[pl.ds(at, share), :] = source[fz].astype(jnp.float32)
    q32_ref[rows:, :] = jnp.zeros((bl + 8, q32_ref.shape[1]), jnp.float32)
    acc_ref[...] = jnp.zeros_like(acc_ref)
    m_ref[...] = jnp.full_like(m_ref, NEG)

    def one(kz, carry):
        attend_block(
            grid, kx, bl, first, heads, tile_len, kz, facts,
            kv_refs, own_ref, out_ref, q32_ref, acc_ref, m_ref,
        )
        return carry

    lax.fori_loop(0, grid.zs, one, 0)


def attend_block(grid, kx, bl, first, heads, tile_len, step, facts,
                 kv_refs, own_ref, out_ref, q32_ref, acc_ref, m_ref):
    block = grid.owner(facts.shard, kx, step)
    offset = jnp.int32(0)
    for b in range(grid.n):
        offset = offset + jnp.where(b < block, facts.length(b), 0)
    prompt = facts.prompt(block)
    valid = jnp.clip(facts.prompt_length(prompt) - facts.shard * tile_len, 0, tile_len)
    c2 = LOG2E / math.sqrt(HD)
    chunk = min(CHUNK, tile_len)
    width = heads * GR * HD

    rest = offset % 8
    window = q32_ref[pl.ds(pl.multiple_of(offset - rest, 8), bl + 8), :]
    window = pltpu.roll(window, jnp.where(rest == 0, 0, bl + 8 - rest), 0)
    queries = window[:bl].astype(jnp.bfloat16)

    def group(g, used):
        return jnp.concatenate(
            [queries[:used, (g * GR + r) * HD:(g * GR + r + 1) * HD] for r in range(GR)], axis=0
        )

    def with_ones(v):
        return jnp.concatenate([v, jnp.ones(v.shape, jnp.bfloat16)], axis=1)

    def sums(p, v):
        return jnp.dot(p, with_ones(v), preferred_element_type=jnp.float32)

    def keys(g, at, size):
        return kv_refs[g][prompt, pl.ds(at, size), :HD]

    def vals(g, at, size):
        return kv_refs[g][prompt, pl.ds(at, size), HD:]

    def put(g, used, acc, m):
        m = jnp.broadcast_to(m, (GR * used, HD))
        for r in range(GR):
            acc_ref[g, r * bl:r * bl + used] = acc[r * used:(r + 1) * used]
            m_ref[g, r * bl:r * bl + used] = m[r * used:(r + 1) * used]

    def update(g, s, seen, v):
        s = jnp.where(seen, s, NEG)
        before = m_ref[g][:, :1]
        m = jnp.maximum(before, jnp.max(s, axis=1, keepdims=True))
        p = jnp.where(seen, jnp.exp2((s - m) * c2), 0.0).astype(jnp.bfloat16)
        acc_ref[g] = acc_ref[g] * jnp.exp2((before - m) * c2) + sums(p, v)
        m_ref[g] = jnp.broadcast_to(m, m_ref.shape[1:])

    def exact():
        acc_ref[...] = jnp.zeros_like(acc_ref)
        m_ref[...] = jnp.full_like(m_ref, NEG)

        def one(c, carry):
            at = pl.multiple_of(c * chunk, chunk)
            for g in range(heads):
                s = dot_nt(group(g, bl), keys(g, at, chunk))
                here = lax.broadcasted_iota(jnp.int32, s.shape, 1) + at
                update(g, s, here < valid, vals(g, at, chunk))
            return carry

        lax.fori_loop(0, (valid + chunk - 1) // chunk, one, 0)

    length = facts.length(block)

    @pl.when(valid == 0)
    def _():
        acc_ref[...] = jnp.zeros_like(acc_ref)
        m_ref[...] = jnp.full_like(m_ref, NEG)

    def single_pass(used, count):
        items = [(g, c) for c in range(count) for g in range(heads)]
        q = [group(g, used) for g in range(heads)]
        peaks = [None] * heads
        accs = [None] * heads
        ahead = dot_nt(q[0], keys(0, 0, chunk))
        for i, (g, c) in enumerate(items):
            s = ahead
            if i + 1 < len(items):
                ng, nc = items[i + 1]
                ahead = dot_nt(q[ng], keys(ng, nc * chunk, chunk))
            if c == count - 1:
                here = lax.broadcasted_iota(jnp.int32, s.shape, 1) + c * chunk
                s = jnp.where(here < valid, s, NEG)
            if c == 0:
                peaks[g] = jnp.max(s, axis=1, keepdims=True)
            p = jnp.exp2((s - peaks[g]) * c2).astype(jnp.bfloat16)
            part = sums(p, vals(g, c * chunk, chunk))
            accs[g] = part if c == 0 else accs[g] + part
        for g in range(heads):
            put(g, used, accs[g], peaks[g])

    for count in range(1, tile_len // chunk + 1):
        for used in range(ROUND, bl + 1, ROUND):
            some_keys = (valid > (count - 1) * chunk) & (valid <= count * chunk)
            some_rows = (length > used - ROUND) & (length <= used)
            pl.when(some_keys & some_rows)(functools.partial(single_pass, used, count))

    def own_part():
        @pl.when(step == 0)
        def _():
            for g in range(heads):
                base = (first + g) * 2 * HD
                s = dot_nt(group(g, bl), own_ref[0, :, base:base + HD])
                row = lax.broadcasted_iota(jnp.int32, s.shape, 0) % bl
                col = lax.broadcasted_iota(jnp.int32, s.shape, 1)
                update(g, s, col <= row, own_ref[0, :, base + HD:base + 2 * HD])

    def write():
        lane = lax.broadcasted_iota(jnp.int32, (bl, EXTRA), 1)
        total = jnp.zeros((bl, EXTRA), jnp.float32)
        peak = jnp.zeros((bl, EXTRA), jnp.float32)
        for g in range(heads):
            for r in range(GR):
                h = g * GR + r
                at = slice(r * bl, (r + 1) * bl)
                out_ref[step, :, h * HD:(h + 1) * HD] = acc_ref[g, at, :HD].astype(jnp.bfloat16)
                total = jnp.where(lane == h, acc_ref[g, at, HD:], total)
                peak = jnp.where(lane == h, m_ref[g, at], peak)
        out_ref[step, :, width:] = encode(peak * c2, total)
        return total

    if kx == 0:
        own_part()
    total = write()

    @pl.when(jnp.max(jnp.where(total < BIG, 0.0, 1.0)) > 0.5)
    def _():
        exact()
        if kx == 0:
            own_part()
        write()


def attend(grid, kx, meta, near, fars, caches, own, first, heads):
    zs, share, cols = near.shape
    bl = own.shape[1]
    tile_len = caches[0].shape[1]
    width = heads * GR * HD + EXTRA
    whole = pl.BlockSpec(memory_space=pltpu.VMEM)
    return pl.pallas_call(
        functools.partial(attend_kernel, grid, kx, bl, share, first, heads, tile_len),
        grid_spec=pltpu.PrefetchScalarGridSpec(
            num_scalar_prefetch=1,
            grid=(1,),
            in_specs=[whole] * (grid.xs + heads + 1),
            out_specs=whole,
            scratch_shapes=[
                pltpu.VMEM((grid.n * share + bl + 8, cols), jnp.float32),
                pltpu.VMEM((heads, GR * bl, 2 * HD), jnp.float32),
                pltpu.VMEM((heads, GR * bl, HD), jnp.float32),
            ],
        ),
        out_shape=jax.ShapeDtypeStruct((zs, bl, width), jnp.bfloat16),
        compiler_params=pltpu.CompilerParams(vmem_limit_bytes=20 * MIB),
        cost_estimate=pl.CostEstimate(
            flops=8 * zs * bl * cols * tile_len,
            bytes_accessed=2 * zs * tile_len * heads * 2 * HD,
            transcendentals=zs * bl * heads * GR * tile_len,
        ),
        name="attend",
    )(meta, near, *fars, *caches, own)


def finish_kernel(n, heads, bl, done, meta, *refs):
    sources, out_ref = refs[:-1], refs[-1]
    pieces = sources[done:]
    facts = Facts(n, meta)
    length = facts.length(facts.shard)
    row = lax.broadcasted_iota(jnp.int32, (bl, HD), 0)
    width = heads * GR * HD
    for c in range(done):
        out_ref[0, :, c * width:(c + 1) * width] = sources[c][0]
    parts, _, total = merge(pieces, heads * GR)
    for h in range(heads * GR):
        at = done * width + h * HD
        value = parts[h] / jnp.broadcast_to(total[:, h:h + 1], (bl, HD))
        out_ref[0, :, at:at + HD] = jnp.where(row < length, value, 0.0).astype(jnp.bfloat16)


def finish(n, meta, done, pieces, heads):
    bl = pieces[0].shape[0]
    whole = pl.BlockSpec(memory_space=pltpu.VMEM)
    sources = list(done) + list(pieces)
    return pl.pallas_call(
        functools.partial(finish_kernel, n, heads, bl, len(done)),
        grid_spec=pltpu.PrefetchScalarGridSpec(
            num_scalar_prefetch=1,
            grid=(1,),
            in_specs=[whole] * len(sources),
            out_specs=whole,
        ),
        out_shape=jax.ShapeDtypeStruct((1, bl, (len(done) + 1) * heads * GR * HD), jnp.bfloat16),
        compiler_params=pltpu.CompilerParams(vmem_limit_bytes=16 * MIB),
        name="finish",
    )(meta, *sources)


def shards(
    hidden_rows,
    carried,
    query_weight,
    response_cache,
    prompt_cache,
    prompt_lengths,
    response_lengths,
    block_prompts,
):
    grid = Grid(lax.axis_size("seq"))
    bl = hidden_rows.shape[1]
    local_kv = response_cache.shape[2] // (2 * HD)
    share = bl * 5 // 8
    chunks = 2 if local_kv % 2 == 0 else 1
    heads = local_kv // chunks
    part_cols = heads * GR * HD
    place = jnp.stack([lax.axis_index("sec"), lax.axis_index("seq")]).astype(jnp.int32)

    def after(value, done):
        return lax.optimization_barrier((value, done))[0]

    def fetched(head, done=()):
        return fetch_cache(grid.n, after(meta, done), prompt_cache, 2 * HD, head)

    handed = lax.ppermute(carried, "sec", [(0, 1)])
    depth = query_weight.shape[1]
    hidden = hidden_rows if depth % HD else fetch([hidden_rows])[0]
    slices = split(grid, place, hidden, handed, depth)
    later_place = after(place, slices[0])
    prompts = block_prompts[:, :, 0]
    meta = jnp.concatenate(
        [later_place] + [a[i] for a in (response_lengths, prompts) for i in range(2)]
        + [prompt_lengths]
    )
    weight, own = fetch([query_weight, response_cache])
    x = [slices[0]] + [None] * (grid.n - 1)
    for kz in reversed(range(grid.zs)):
        for kx in reversed(range(grid.xs)):
            k = kx * grid.zs + kz
            if k:
                x[k] = grid.swap(slices[k], kx, kz)
    part = project(grid, meta, x, weight, bl, share, chunks)
    part = [piece.reshape(grid.zs, share, part_cols) for piece in part]
    part = [part[c * grid.xs:(c + 1) * grid.xs] for c in range(chunks)]

    def narrow(value):
        return (value * 0.125).astype(jnp.float16)

    def widen(value):
        return value.astype(jnp.float32) * 8.0

    def sum_x(c, done):
        parts = part[c]
        got = [grid.swap(after(narrow(parts[kx]), done), kx, 0) for kx in range(1, grid.xs)]
        return functools.reduce(jnp.add, [parts[0]] + [widen(value) for value in got]), got

    def narrow_z(held, done):
        return [after(narrow(held[kz]), done) for kz in range(1, grid.zs)]

    def sum_z(held, sends, beside):
        got = [grid.swap(send, 0, kz + 1) for kz, send in enumerate(sends)]
        parts = [after(held[0], beside)] + [widen(value) for value in got]
        return functools.reduce(jnp.add, parts).astype(jnp.bfloat16)

    def gather_z(mine):
        return [mine] + [grid.swap(mine, 0, kz) for kz in range(1, grid.zs)]

    def gather_x(near):
        return [near] + [grid.swap(near, kx, 0) for kx in range(1, grid.xs)]

    def call(c, kx, queries):
        return attend(
            grid, kx, meta, queries[0], queries[1:], caches[c * heads:(c + 1) * heads], own,
            c * heads, heads,
        )

    def call_far(c, queries):
        outs = [call(c, kx, queries) for kx in range(1, grid.xs)]
        return outs, [grid.swap(out, kx + 1, 0) for kx, out in enumerate(outs)]

    def send_z(merged):
        return [merged[0]] + [grid.swap(merged[kz], 0, kz) for kz in range(1, grid.zs)]

    half = (local_kv + 1) // 4
    caches = [fetched(head) for head in range(half)]
    part[0][0] = after(part[0][0], caches)
    held, got = sum_x(0, ())
    caches += [fetched(head) for head in range(half, heads)]
    mine = sum_z(held, narrow_z(held, ()), caches)
    column = gather_z(mine)
    if chunks > 1:
        later_held, _ = sum_x(1, got)
        sends = narrow_z(later_held, mine)
        caches += [fetched(head, mine) for head in range(heads, local_kv)]
        column = after(column, (caches[:heads + half], sends))
    queries = gather_x(jnp.stack(column))
    if chunks > 1:
        mine = sum_z(later_held, sends, caches)
        column = gather_z(mine)
        queries[0] = after(queries[0], mine)
    outs, mets = call_far(0, queries)
    if chunks > 1:
        near = jnp.stack(after(column, outs))
        later = gather_x(near)
        queries[0] = after(queries[0], near)
    held = call(0, 0, queries)
    if chunks == 1:
        return finish(grid.n, meta, [], send_z(merge_column([held] + mets, heads * GR)), heads)
    later[0] = after(later[0], held)
    outs, later_mets = call_far(1, later)
    merged = merge_column([after(held, outs)] + mets, heads * GR)
    pieces = send_z(merged)
    later[0] = after(later[0], merged)
    held = call(1, 0, later)
    done = finish(grid.n, meta, [], pieces, heads)
    pieces = send_z(merge_column([held] + later_mets, heads * GR))
    return finish(grid.n, meta, [done], pieces, heads)


def solution(mesh):
    placed = (
        P("sec", "seq", None),
        P("sec", "seq", None),
        P("sec", "seq", "tp"),
        P("sec", "seq", "tp"),
        P("sec", None, "seq", "tp"),
        P(),
        P(),
        P(),
    )
    return jax.shard_map(
        shards, mesh=mesh, in_specs=placed, out_specs=P("sec", "seq", "tp"), check_vma=False
    )
```

```python
import functools
import math

import jax
import jax.numpy as jnp
from jax import lax
from jax.experimental import pallas as pl
from jax.experimental.pallas import tpu as pltpu
from jax.sharding import PartitionSpec as P

HD = 128
GR = 4
NEG = -1e30
LOG2E = 1.4426950408889634
CHUNK = 512
PIECE = 1024
ROUND = 32
EXTRA = 128
SLOT = 16
BIG = 2.0 ** 100
MIB = 1024 * 1024


def dot_nt(a, b):
    return lax.dot_general(a, b, (((1,), (1,)), ((), ())), preferred_element_type=jnp.float32)


class Grid:
    def __init__(self, count):
        self.n = count
        self.xs = 1 << ((count.bit_length() - 1) // 2)
        self.zs = count // self.xs
        self.masks = [2 ** (i + 1) - 1 for i in range(self.zs.bit_length() - 1)]
        self.zorder = [0]
        for mask in reversed(self.masks):
            self.zorder = self.zorder + [kz ^ mask for kz in self.zorder]

    def owner(self, shard, kx, kz):
        z, x = shard // self.xs, shard % self.xs
        return (z ^ kz) * self.xs + (x ^ kx)

    def swap(self, value, kx, kz):
        pairs = [(s, self.owner(s, kx, kz)) for s in range(self.n)]
        return lax.ppermute(value, "seq", pairs)


class Facts:
    def __init__(self, n, meta):
        self.n, self.meta = n, meta
        self.section, self.shard = meta[0], meta[1]

    def length(self, block):
        return self.meta[2 + self.section * self.n + block]

    def prompt(self, block):
        return self.meta[2 + (2 + self.section) * self.n + block]

    def prompt_length(self, prompt):
        return self.meta[2 + 4 * self.n + prompt]


def split_kernel(grid, depth, meta, hidden_ref, handed_ref, *out_refs):
    for kx in range(grid.xs):
        for i, kz in enumerate(grid.zorder):
            at = pl.multiple_of(grid.owner(meta[1], kx, kz) * depth, HD)
            total = hidden_ref[0, :, pl.ds(at, depth)].astype(jnp.float32) + handed_ref[
                0, :, pl.ds(at, depth)
            ].astype(jnp.float32)
            out_refs[kx * grid.zs + i][...] = total.astype(jnp.bfloat16)


def split(grid, meta, hidden, handed, depth):
    bl = hidden.shape[1]
    if depth % HD:
        total = (hidden[0].astype(jnp.float32) + handed[0].astype(jnp.float32)).astype(jnp.bfloat16)
        return [
            lax.dynamic_slice_in_dim(total, grid.owner(meta[1], kx, kz) * depth, depth, 1)
            for kx in range(grid.xs) for kz in grid.zorder
        ]
    whole = pl.BlockSpec(hidden.shape, lambda i, *m: (0, 0, 0))
    return pl.pallas_call(
        functools.partial(split_kernel, grid, depth),
        grid_spec=pltpu.PrefetchScalarGridSpec(
            num_scalar_prefetch=1,
            grid=(1,),
            in_specs=[whole, whole],
            out_specs=[pl.BlockSpec((bl, depth), lambda i, *m: (0, 0))] * grid.n,
        ),
        out_shape=[jax.ShapeDtypeStruct((bl, depth), jnp.bfloat16)] * grid.n,
        compiler_params=pltpu.CompilerParams(vmem_limit_bytes=16 * MIB),
        name="split",
    )(meta, hidden, handed)


def run_moves(moves):
    for needed, move in moves:
        if needed is None:
            move.start()
        else:
            pl.when(needed)(move.start)
    for needed, move in moves:
        if needed is None:
            move.wait()
        else:
            pl.when(needed)(move.wait)


def fetch_kernel(*refs):
    count = len(refs) // 2
    run_moves([
        (None, pltpu.make_async_copy(refs[i], refs[count + i], refs[-1].at[i]))
        for i in range(count)
    ])


def fetch(arrays):
    anywhere, near = pl.BlockSpec(memory_space=pltpu.HBM), pl.BlockSpec(memory_space=pltpu.VMEM)
    size = sum(math.prod(array.shape) for array in arrays)
    out = pl.pallas_call(
        fetch_kernel,
        in_specs=[anywhere] * len(arrays),
        out_specs=[near] * len(arrays),
        scratch_shapes=[pltpu.SemaphoreType.DMA((len(arrays),))],
        out_shape=[pltpu.VMEM(array.shape, array.dtype) for array in arrays],
        compiler_params=pltpu.CompilerParams(vmem_limit_bytes=4 * MIB),
        cost_estimate=pl.CostEstimate(flops=0, bytes_accessed=2 * size, transcendentals=0),
        name="fetch",
    )(*[pltpu.with_memory_space_constraint(array, pltpu.HBM) for array in arrays])
    return [pltpu.with_memory_space_constraint(array, pltpu.VMEM) for array in out]


def fetch_cache_kernel(n, chunk, width, first, meta, cache_ref, kv_ref, sem):
    count, tile_len = kv_ref.shape[:2]
    facts = Facts(n, meta)
    moves = []
    for p in range(count):
        asked = facts.prompt(0) == p
        for b in range(1, n):
            asked = asked | (facts.prompt(b) == p)
        for c in range(tile_len // chunk):
            at = pl.ds(c * chunk, chunk)
            needed = asked & (facts.prompt_length(p) > facts.shard * tile_len + c * chunk)
            moves.append((needed, pltpu.make_async_copy(
                cache_ref.at[0, p, at, pl.ds(first * width, width)], kv_ref.at[p, at],
                sem.at[p, c],
            )))
    run_moves(moves)


def fetch_cache(n, meta, cache, width, first):
    count, tile_len = cache.shape[1:3]
    chunk = min(PIECE, tile_len)
    shape = (count, tile_len, width)
    out = pl.pallas_call(
        functools.partial(fetch_cache_kernel, n, chunk, width, first),
        grid_spec=pltpu.PrefetchScalarGridSpec(
            num_scalar_prefetch=1,
            grid=(1,),
            in_specs=[pl.BlockSpec(memory_space=pltpu.HBM)],
            out_specs=pl.BlockSpec(memory_space=pltpu.VMEM),
            scratch_shapes=[pltpu.SemaphoreType.DMA((count, tile_len // chunk))],
        ),
        out_shape=pltpu.VMEM(shape, cache.dtype),
        compiler_params=pltpu.CompilerParams(vmem_limit_bytes=4 * MIB),
        cost_estimate=pl.CostEstimate(
            flops=0, bytes_accessed=2 * math.prod(shape), transcendentals=0
        ),
        name="fetch_cache",
    )(meta, pltpu.with_memory_space_constraint(cache, pltpu.HBM))
    return pltpu.with_memory_space_constraint(out, pltpu.VMEM)


def project_kernel(grid, bl, share, meta, *refs):
    x_refs, w_ref, refs = refs[:grid.n], refs[grid.n], refs[grid.n + 1:]
    out_refs, (xp_ref, starts) = refs[:-2], refs[-2:]

    @pl.when(pl.program_id(0) == 0)
    def _():
        facts = Facts(grid.n, meta)
        shard = facts.shard
        offset = jnp.int32(0)
        for b in range(grid.n):
            starts[b] = offset
            offset = offset + facts.length(b)
        lane = lax.broadcasted_iota(jnp.int32, (8, grid.n * bl), 1)
        target = jnp.full(lane.shape, -1, jnp.int32)
        owners = [
            grid.owner(shard, kx, kz) for kx in range(grid.xs) for kz in grid.zorder
        ]
        for k, b in enumerate(owners):
            order = lane - k * bl
            used = (order >= 0) & (order < facts.length(b))
            target = jnp.where(used, order + starts[b], target)
        row = lax.broadcasted_iota(jnp.int32, (share, grid.n * bl), 0)
        target = jnp.broadcast_to(target[:1], row.shape)
        picks = [jnp.where(row + b * share == target, 1.0, 0.0) for b in owners]
        pick = jnp.concatenate(picks, axis=0).astype(jnp.bfloat16)
        x = jnp.concatenate([ref[...] for ref in x_refs], axis=0)
        chosen = jnp.dot(pick, x, preferred_element_type=jnp.float32)
        xp_ref[...] = chosen.astype(jnp.bfloat16)

    result = jnp.dot(xp_ref[...], w_ref[0], preferred_element_type=jnp.float32)
    rows = grid.zs * share
    for i, out_ref in enumerate(out_refs):
        chunk, kx = i // grid.xs, i % grid.xs

        @pl.when(pl.program_id(0) == chunk)
        def _(out_ref=out_ref, kx=kx):
            out_ref[...] = result[kx * rows:(kx + 1) * rows]


def project(grid, meta, xs, w, bl, share, chunks):
    k, cols = w.shape[1:]
    rows = grid.n * share
    tile = cols // chunks
    piece = (grid.zs * share, tile)
    return pl.pallas_call(
        functools.partial(project_kernel, grid, bl, share),
        grid_spec=pltpu.PrefetchScalarGridSpec(
            num_scalar_prefetch=1,
            grid=(chunks,),
            in_specs=[pl.BlockSpec((bl, k), lambda j, *m: (0, 0))] * grid.n
            + [pl.BlockSpec((1, k, tile), lambda j, *m: (0, 0, j))],
            out_specs=[pl.BlockSpec(piece, lambda j, *m: (0, 0))] * (chunks * grid.xs),
            scratch_shapes=[
                pltpu.VMEM((rows, k), jnp.bfloat16), pltpu.SMEM((grid.n,), jnp.int32)
            ],
        ),
        out_shape=[jax.ShapeDtypeStruct(piece, jnp.float32)] * (chunks * grid.xs),
        compiler_params=pltpu.CompilerParams(vmem_limit_bytes=20 * MIB),
        cost_estimate=pl.CostEstimate(
            flops=2 * rows * k * cols, bytes_accessed=2 * k * cols + 4 * rows * cols,
            transcendentals=0,
        ),
        name="project",
    )(meta, *xs, w)


def three_terms(value):
    high = value.astype(jnp.bfloat16).astype(jnp.float32)
    mid = (value - high).astype(jnp.bfloat16).astype(jnp.float32)
    return [high, mid, value - high - mid]


def encode(peak, total):
    lane = lax.broadcasted_iota(jnp.int32, peak.shape, 1)
    out = jnp.zeros(peak.shape, jnp.float32)
    for i, term in enumerate(three_terms(peak) + three_terms(total)):
        term = jnp.where(lane < SLOT, term, 0.0)
        out = out + (pltpu.roll(term, i * SLOT, 1) if i else term)
    return out.astype(jnp.bfloat16)


def decode(tile):
    terms = tile.astype(jnp.float32)
    parts = [terms] + [pltpu.roll(terms, EXTRA - i * SLOT, 1) for i in range(1, 6)]
    return parts[0] + parts[1] + parts[2], parts[3] + parts[4] + parts[5]


def merge(refs, heads):
    width = heads * HD
    peaks, totals = zip(*[decode(ref[:, width:]) for ref in refs])
    rows = peaks[0].shape[0]
    peak = functools.reduce(jnp.maximum, peaks)
    weights = [jnp.exp2(one - peak) for one in peaks]
    total = functools.reduce(jnp.add, [w * one for w, one in zip(weights, totals)])
    out = []
    for h in range(heads):
        terms = [
            jnp.broadcast_to(weight[:, h:h + 1], (rows, HD))
            * ref[:, h * HD:(h + 1) * HD].astype(jnp.float32)
            for weight, ref in zip(weights, refs)
        ]
        out.append(functools.reduce(jnp.add, terms))
    return out, peak, total


def merge_kernel(zs, heads, *refs):
    sources, outs = refs[:-zs], refs[-zs:]
    for kz in range(zs):
        parts, peak, total = merge([ref.at[kz] for ref in sources], heads)
        for h in range(heads):
            outs[kz][:, h * HD:(h + 1) * HD] = parts[h].astype(jnp.bfloat16)
        outs[kz][:, heads * HD:] = encode(peak, total)


def merge_column(sources, heads):
    zs, bl, width = sources[0].shape
    return pl.pallas_call(
        functools.partial(merge_kernel, zs, heads),
        out_shape=[jax.ShapeDtypeStruct((bl, width), jnp.bfloat16)] * zs,
        compiler_params=pltpu.CompilerParams(vmem_limit_bytes=16 * MIB),
        name="merge",
    )(*sources)


def attend_kernel(grid, kx, bl, share, first, heads, tile_len, meta, *refs):
    near_ref, far_refs = refs[0], refs[1:grid.xs]
    kv_refs, refs = refs[grid.xs:grid.xs + heads], refs[grid.xs + heads:]
    own_ref, out_ref, q32_ref, acc_ref, m_ref = refs
    facts = Facts(grid.n, meta)
    shard = facts.shard
    rows = grid.n * share
    for fx in range(grid.xs):
        for fz in range(grid.zs):
            source = near_ref if fx == 0 else far_refs[fx - 1]
            at = pl.multiple_of(grid.owner(shard, fx, grid.zorder[fz]) * share, 8)
            q32_ref[pl.ds(at, share), :] = source[fz].astype(jnp.float32)
    q32_ref[rows:, :] = jnp.zeros((bl + 8, q32_ref.shape[1]), jnp.float32)
    acc_ref[...] = jnp.zeros_like(acc_ref)
    m_ref[...] = jnp.full_like(m_ref, NEG)

    def one(kz, carry):
        attend_block(
            grid, kx, bl, first, heads, tile_len, kz, facts,
            kv_refs, own_ref, out_ref, q32_ref, acc_ref, m_ref,
        )
        return carry

    lax.fori_loop(0, grid.zs, one, 0)


def attend_block(grid, kx, bl, first, heads, tile_len, step, facts,
                 kv_refs, own_ref, out_ref, q32_ref, acc_ref, m_ref):
    block = grid.owner(facts.shard, kx, step)
    offset = jnp.int32(0)
    for b in range(grid.n):
        offset = offset + jnp.where(b < block, facts.length(b), 0)
    prompt = facts.prompt(block)
    valid = jnp.clip(facts.prompt_length(prompt) - facts.shard * tile_len, 0, tile_len)
    c2 = LOG2E / math.sqrt(HD)
    chunk = min(CHUNK, tile_len)
    width = heads * GR * HD

    rest = offset % 8
    window = q32_ref[pl.ds(pl.multiple_of(offset - rest, 8), bl + 8), :]
    window = pltpu.roll(window, jnp.where(rest == 0, 0, bl + 8 - rest), 0)
    queries = window[:bl].astype(jnp.bfloat16)

    def group(g, used):
        return jnp.concatenate(
            [queries[:used, (g * GR + r) * HD:(g * GR + r + 1) * HD] for r in range(GR)], axis=0
        )

    def with_ones(v):
        return jnp.concatenate([v, jnp.ones(v.shape, jnp.bfloat16)], axis=1)

    def sums(p, v):
        return jnp.dot(p, with_ones(v), preferred_element_type=jnp.float32)

    def keys(g, at, size):
        return kv_refs[g][prompt, pl.ds(at, size), :HD]

    def vals(g, at, size):
        return kv_refs[g][prompt, pl.ds(at, size), HD:]

    def put(g, used, acc, m):
        m = jnp.broadcast_to(m, (GR * used, HD))
        for r in range(GR):
            acc_ref[g, r * bl:r * bl + used] = acc[r * used:(r + 1) * used]
            m_ref[g, r * bl:r * bl + used] = m[r * used:(r + 1) * used]

    def update(g, s, seen, v):
        s = jnp.where(seen, s, NEG)
        before = m_ref[g][:, :1]
        m = jnp.maximum(before, jnp.max(s, axis=1, keepdims=True))
        p = jnp.where(seen, jnp.exp2((s - m) * c2), 0.0).astype(jnp.bfloat16)
        acc_ref[g] = acc_ref[g] * jnp.exp2((before - m) * c2) + sums(p, v)
        m_ref[g] = jnp.broadcast_to(m, m_ref.shape[1:])

    def exact():
        acc_ref[...] = jnp.zeros_like(acc_ref)
        m_ref[...] = jnp.full_like(m_ref, NEG)

        def one(c, carry):
            at = pl.multiple_of(c * chunk, chunk)
            for g in range(heads):
                s = dot_nt(group(g, bl), keys(g, at, chunk))
                here = lax.broadcasted_iota(jnp.int32, s.shape, 1) + at
                update(g, s, here < valid, vals(g, at, chunk))
            return carry

        lax.fori_loop(0, (valid + chunk - 1) // chunk, one, 0)

    length = facts.length(block)

    @pl.when(valid == 0)
    def _():
        acc_ref[...] = jnp.zeros_like(acc_ref)
        m_ref[...] = jnp.full_like(m_ref, NEG)

    step_of = min(PIECE, tile_len) // chunk

    def single_pass(used, count):
        items = [(g, c) for c in range(count) for g in range(heads)]
        q = [group(g, used) for g in range(heads)]
        peaks = [None] * heads
        accs = [None] * heads
        ahead = dot_nt(q[0], keys(0, 0, chunk))
        for i, (g, c) in enumerate(items):
            s = ahead
            if i + 1 < len(items):
                ng, nc = items[i + 1]
                ahead = dot_nt(q[ng], keys(ng, nc * chunk, chunk))
            if (c + 1) * chunk > (count - step_of) * chunk:
                here = lax.broadcasted_iota(jnp.int32, s.shape, 1) + c * chunk
                s = jnp.where(here < valid, s, NEG)
            if c == 0:
                peaks[g] = jnp.max(s, axis=1, keepdims=True)
            p = jnp.exp2((s - peaks[g]) * c2).astype(jnp.bfloat16)
            part = sums(p, vals(g, c * chunk, chunk))
            accs[g] = part if c == 0 else accs[g] + part
        for g in range(heads):
            put(g, used, accs[g], peaks[g])

    for count in range(step_of, tile_len // chunk + 1, step_of):
        for used in range(ROUND, bl + 1, ROUND):
            some_keys = (valid > (count - step_of) * chunk) & (valid <= count * chunk)
            some_rows = (length > used - ROUND) & (length <= used)
            pl.when(some_keys & some_rows)(functools.partial(single_pass, used, count))

    def own_part():
        @pl.when(step == 0)
        def _():
            for g in range(heads):
                base = (first + g) * 2 * HD
                s = dot_nt(group(g, bl), own_ref[0, :, base:base + HD])
                row = lax.broadcasted_iota(jnp.int32, s.shape, 0) % bl
                col = lax.broadcasted_iota(jnp.int32, s.shape, 1)
                update(g, s, col <= row, own_ref[0, :, base + HD:base + 2 * HD])

    def write():
        lane = lax.broadcasted_iota(jnp.int32, (bl, EXTRA), 1)
        total = jnp.zeros((bl, EXTRA), jnp.float32)
        peak = jnp.zeros((bl, EXTRA), jnp.float32)
        for g in range(heads):
            for r in range(GR):
                h = g * GR + r
                at = slice(r * bl, (r + 1) * bl)
                out_ref[step, :, h * HD:(h + 1) * HD] = acc_ref[g, at, :HD].astype(jnp.bfloat16)
                total = jnp.where(lane == h, acc_ref[g, at, HD:], total)
                peak = jnp.where(lane == h, m_ref[g, at], peak)
        out_ref[step, :, width:] = encode(peak * c2, total)
        return total

    if kx == 0:
        own_part()
    total = write()

    @pl.when(jnp.max(jnp.where(total < BIG, 0.0, 1.0)) > 0.5)
    def _():
        exact()
        if kx == 0:
            own_part()
        write()


def attend(grid, kx, meta, near, fars, caches, own, first, heads):
    zs, share, cols = near.shape
    bl = own.shape[1]
    tile_len = caches[0].shape[1]
    width = heads * GR * HD + EXTRA
    whole = pl.BlockSpec(memory_space=pltpu.VMEM)
    return pl.pallas_call(
        functools.partial(attend_kernel, grid, kx, bl, share, first, heads, tile_len),
        grid_spec=pltpu.PrefetchScalarGridSpec(
            num_scalar_prefetch=1,
            grid=(1,),
            in_specs=[whole] * (grid.xs + heads + 1),
            out_specs=whole,
            scratch_shapes=[
                pltpu.VMEM((grid.n * share + bl + 8, cols), jnp.float32),
                pltpu.VMEM((heads, GR * bl, 2 * HD), jnp.float32),
                pltpu.VMEM((heads, GR * bl, HD), jnp.float32),
            ],
        ),
        out_shape=jax.ShapeDtypeStruct((zs, bl, width), jnp.bfloat16),
        compiler_params=pltpu.CompilerParams(vmem_limit_bytes=20 * MIB),
        cost_estimate=pl.CostEstimate(
            flops=8 * zs * bl * cols * tile_len,
            bytes_accessed=2 * zs * tile_len * heads * 2 * HD,
            transcendentals=zs * bl * heads * GR * tile_len,
        ),
        name="attend",
    )(meta, near, *fars, *caches, own)


def finish_kernel(n, heads, bl, done, meta, *refs):
    sources, out_ref = refs[:-1], refs[-1]
    pieces = sources[done:]
    facts = Facts(n, meta)
    length = facts.length(facts.shard)
    row = lax.broadcasted_iota(jnp.int32, (bl, HD), 0)
    width = heads * GR * HD
    for c in range(done):
        out_ref[0, :, c * width:(c + 1) * width] = sources[c][0]
    parts, _, total = merge(pieces, heads * GR)
    for h in range(heads * GR):
        at = done * width + h * HD
        value = parts[h] / jnp.broadcast_to(total[:, h:h + 1], (bl, HD))
        out_ref[0, :, at:at + HD] = jnp.where(row < length, value, 0.0).astype(jnp.bfloat16)


def finish(n, meta, done, pieces, heads):
    bl = pieces[0].shape[0]
    whole = pl.BlockSpec(memory_space=pltpu.VMEM)
    sources = list(done) + list(pieces)
    return pl.pallas_call(
        functools.partial(finish_kernel, n, heads, bl, len(done)),
        grid_spec=pltpu.PrefetchScalarGridSpec(
            num_scalar_prefetch=1,
            grid=(1,),
            in_specs=[whole] * len(sources),
            out_specs=whole,
        ),
        out_shape=jax.ShapeDtypeStruct((1, bl, (len(done) + 1) * heads * GR * HD), jnp.bfloat16),
        compiler_params=pltpu.CompilerParams(vmem_limit_bytes=16 * MIB),
        name="finish",
    )(meta, *sources)


def shards(
    hidden_rows,
    carried,
    query_weight,
    response_cache,
    prompt_cache,
    prompt_lengths,
    response_lengths,
    block_prompts,
):
    grid = Grid(lax.axis_size("seq"))
    bl = hidden_rows.shape[1]
    local_kv = response_cache.shape[2] // (2 * HD)
    share = bl * 5 // 8
    chunks = 2 if local_kv % 2 == 0 else 1
    heads = local_kv // chunks
    part_cols = heads * GR * HD
    place = jnp.stack([lax.axis_index("sec"), lax.axis_index("seq")]).astype(jnp.int32)

    def after(value, done):
        return lax.optimization_barrier((value, done))[0]

    def fetched(head, done=()):
        return fetch_cache(grid.n, after(meta, done), prompt_cache, 2 * HD, head)

    handed = lax.ppermute(carried, "sec", [(0, 1)])
    depth = query_weight.shape[1]
    hidden = hidden_rows if depth % HD else fetch([hidden_rows])[0]
    slices = split(grid, place, hidden, handed, depth)
    later_place = after(place, slices[0])
    prompts = block_prompts[:, :, 0]
    meta = jnp.concatenate(
        [later_place] + [a[i] for a in (response_lengths, prompts) for i in range(2)]
        + [prompt_lengths]
    )
    weight, own = fetch([query_weight, response_cache])
    x = [slices[0]] + [None] * (grid.n - 1)
    for i in sorted(range(grid.zs), key=lambda i: -grid.zorder[i]):
        for kx in reversed(range(grid.xs)):
            k = kx * grid.zs + i
            if k:
                x[k] = grid.swap(slices[k], kx, grid.zorder[i])
    part = project(grid, meta, x, weight, bl, share, chunks)
    part = [piece.reshape(grid.zs, share, part_cols) for piece in part]
    part = [part[c * grid.xs:(c + 1) * grid.xs] for c in range(chunks)]

    def narrow(value):
        return (value * 0.125).astype(jnp.float16)

    def widen(value):
        return value.astype(jnp.float32) * 8.0

    def both(first, second):
        return lax.optimization_barrier((first, second))

    def reduce_x(parts, done=()):
        got = [grid.swap(after(narrow(parts[kx]), done), kx, 0) for kx in range(1, grid.xs)]
        return functools.reduce(jnp.add, [parts[0]] + [widen(value) for value in got])

    def halve(held, mask, sent):
        return held[:held.shape[0] // 2] + widen(grid.swap(sent, 0, mask))

    def upper(held):
        return narrow(held[held.shape[0] // 2:])

    def double(held, mask):
        return jnp.concatenate([held, grid.swap(held, 0, mask)])

    def gather_x(near):
        return [near] + [grid.swap(near, kx, 0) for kx in range(1, grid.xs)]

    def call(c, kx, queries):
        return attend(
            grid, kx, meta, queries[0], queries[1:], caches[c * heads:(c + 1) * heads], own,
            c * heads, heads,
        )

    def call_far(c, queries):
        outs = [call(c, kx, queries) for kx in range(1, grid.xs)]
        return outs, [grid.swap(out, kx + 1, 0) for kx, out in enumerate(outs)]

    def send_z(merged):
        return [merged[0]] + [grid.swap(merged[kz], 0, kz) for kz in range(1, grid.zs)]

    half = (local_kv + 1) // 4
    caches = [fetched(head) for head in range(half)]
    part[0][0] = after(part[0][0], caches)
    held = reduce_x(part[0])
    if chunks > 1:
        sent, part[1][1] = both(upper(held), part[1][1])
        later = reduce_x(part[1])
    else:
        sent = upper(held)
    caches += [fetched(head, sent) for head in range(half, heads + half)][:local_kv - half]
    for i, mask in enumerate(grid.masks):
        held = halve(held, mask, sent)
        if i + 1 < len(grid.masks):
            sent = upper(held)
    near = after(held, caches).astype(jnp.bfloat16)
    for i, mask in enumerate(reversed(grid.masks)):
        if chunks > 1:
            near, sent = both(near, upper(later))
        near = double(near, mask)
        if chunks > 1:
            later = halve(later, grid.masks[i], sent)
    if chunks > 1:
        near, later = both(near, later.astype(jnp.bfloat16))
    queries = gather_x(near)
    if chunks > 1:
        caches += [fetched(head, later) for head in range(heads + half, local_kv)]
        for mask in reversed(grid.masks):
            later = double(later, mask)
        queries[0], later = both(queries[0], after(later, caches))
        later = gather_x(later)
    outs, mets = call_far(0, queries)
    queries[0] = after(queries[0], outs)
    held = call(0, 0, queries)
    if chunks == 1:
        return finish(grid.n, meta, [], send_z(merge_column([held] + mets, heads * GR)), heads)
    later[0] = after(later[0], held)
    outs, later_mets = call_far(1, later)
    merged = merge_column([after(held, outs)] + mets, heads * GR)
    pieces = send_z(merged)
    later[0] = after(later[0], merged)
    held = call(1, 0, later)
    done = finish(grid.n, meta, [], pieces, heads)
    pieces = send_z(merge_column([held] + later_mets, heads * GR))
    return finish(grid.n, meta, [done], pieces, heads)


def solution(mesh):
    placed = (
        P("sec", "seq", None),
        P("sec", "seq", None),
        P("sec", "seq", "tp"),
        P("sec", "seq", "tp"),
        P("sec", None, "seq", "tp"),
        P(),
        P(),
        P(),
    )
    return jax.shard_map(
        shards, mesh=mesh, in_specs=placed, out_specs=P("sec", "seq", "tp"), check_vma=False
    )
```

```python
import functools
import math

import jax
import jax.numpy as jnp
from jax import lax
from jax.experimental import pallas as pl
from jax.experimental.pallas import tpu as pltpu
from jax.sharding import PartitionSpec as P

HD = 128
GR = 4
NEG = -1e30
LOG2E = 1.4426950408889634
CHUNK = 512
PIECE = 1024
ROUND = 32
EXTRA = 128
SLOT = 16
BIG = 2.0 ** 100
MIB = 1024 * 1024


def dot_nt(a, b):
    return lax.dot_general(a, b, (((1,), (1,)), ((), ())), preferred_element_type=jnp.float32)


class Grid:
    def __init__(self, count):
        self.n = count
        self.xs = 1 << ((count.bit_length() - 1) // 2)
        self.zs = count // self.xs

    def owner(self, shard, kx, kz):
        z, x = shard // self.xs, shard % self.xs
        return (z ^ kz) * self.xs + (x ^ kx)

    def swap(self, value, kx, kz):
        pairs = [(s, self.owner(s, kx, kz)) for s in range(self.n)]
        return lax.ppermute(value, "seq", pairs)


class Facts:
    def __init__(self, n, meta):
        self.n, self.meta = n, meta
        self.section, self.shard = meta[0], meta[1]

    def length(self, block):
        return self.meta[2 + self.section * self.n + block]

    def prompt(self, block):
        return self.meta[2 + (2 + self.section) * self.n + block]

    def prompt_length(self, prompt):
        return self.meta[2 + 4 * self.n + prompt]


def split_kernel(grid, depth, meta, hidden_ref, handed_ref, *out_refs):
    for kx in range(grid.xs):
        for kz in range(grid.zs):
            at = pl.multiple_of(grid.owner(meta[1], kx, kz) * depth, HD)
            total = hidden_ref[0, :, pl.ds(at, depth)].astype(jnp.float32) + handed_ref[
                0, :, pl.ds(at, depth)
            ].astype(jnp.float32)
            out_refs[kx * grid.zs + kz][...] = total.astype(jnp.bfloat16)


def split(grid, meta, hidden, handed, depth):
    bl = hidden.shape[1]
    if depth % HD:
        total = (hidden[0].astype(jnp.float32) + handed[0].astype(jnp.float32)).astype(jnp.bfloat16)
        return [
            lax.dynamic_slice_in_dim(total, grid.owner(meta[1], kx, kz) * depth, depth, 1)
            for kx in range(grid.xs) for kz in range(grid.zs)
        ]
    whole = pl.BlockSpec(hidden.shape, lambda i, *m: (0, 0, 0))
    return pl.pallas_call(
        functools.partial(split_kernel, grid, depth),
        grid_spec=pltpu.PrefetchScalarGridSpec(
            num_scalar_prefetch=1,
            grid=(1,),
            in_specs=[whole, whole],
            out_specs=[pl.BlockSpec((bl, depth), lambda i, *m: (0, 0))] * grid.n,
        ),
        out_shape=[jax.ShapeDtypeStruct((bl, depth), jnp.bfloat16)] * grid.n,
        compiler_params=pltpu.CompilerParams(vmem_limit_bytes=16 * MIB),
        name="split",
    )(meta, hidden, handed)


def run_moves(moves):
    for needed, move in moves:
        if needed is None:
            move.start()
        else:
            pl.when(needed)(move.start)
    for needed, move in moves:
        if needed is None:
            move.wait()
        else:
            pl.when(needed)(move.wait)


def fetch_kernel(*refs):
    count = len(refs) // 2
    run_moves([
        (None, pltpu.make_async_copy(refs[i], refs[count + i], refs[-1].at[i]))
        for i in range(count)
    ])


def fetch(arrays):
    anywhere, near = pl.BlockSpec(memory_space=pltpu.HBM), pl.BlockSpec(memory_space=pltpu.VMEM)
    size = sum(math.prod(array.shape) for array in arrays)
    out = pl.pallas_call(
        fetch_kernel,
        in_specs=[anywhere] * len(arrays),
        out_specs=[near] * len(arrays),
        scratch_shapes=[pltpu.SemaphoreType.DMA((len(arrays),))],
        out_shape=[pltpu.VMEM(array.shape, array.dtype) for array in arrays],
        compiler_params=pltpu.CompilerParams(vmem_limit_bytes=4 * MIB),
        cost_estimate=pl.CostEstimate(flops=0, bytes_accessed=2 * size, transcendentals=0),
        name="fetch",
    )(*[pltpu.with_memory_space_constraint(array, pltpu.HBM) for array in arrays])
    return [pltpu.with_memory_space_constraint(array, pltpu.VMEM) for array in out]


def fetch_cache_kernel(n, chunk, width, first, meta, cache_ref, kv_ref, sem):
    count, tile_len = kv_ref.shape[:2]
    facts = Facts(n, meta)
    moves = []
    for p in range(count):
        asked = facts.prompt(0) == p
        for b in range(1, n):
            asked = asked | (facts.prompt(b) == p)
        for c in range(tile_len // chunk):
            at = pl.ds(c * chunk, chunk)
            needed = asked & (facts.prompt_length(p) > facts.shard * tile_len + c * chunk)
            moves.append((needed, pltpu.make_async_copy(
                cache_ref.at[0, p, at, pl.ds(first * width, width)], kv_ref.at[p, at],
                sem.at[p, c],
            )))
    run_moves(moves)


def fetch_cache(n, meta, cache, width, first):
    count, tile_len = cache.shape[1:3]
    chunk = min(PIECE, tile_len)
    shape = (count, tile_len, width)
    out = pl.pallas_call(
        functools.partial(fetch_cache_kernel, n, chunk, width, first),
        grid_spec=pltpu.PrefetchScalarGridSpec(
            num_scalar_prefetch=1,
            grid=(1,),
            in_specs=[pl.BlockSpec(memory_space=pltpu.HBM)],
            out_specs=pl.BlockSpec(memory_space=pltpu.VMEM),
            scratch_shapes=[pltpu.SemaphoreType.DMA((count, tile_len // chunk))],
        ),
        out_shape=pltpu.VMEM(shape, cache.dtype),
        compiler_params=pltpu.CompilerParams(vmem_limit_bytes=4 * MIB),
        cost_estimate=pl.CostEstimate(
            flops=0, bytes_accessed=2 * math.prod(shape), transcendentals=0
        ),
        name="fetch_cache",
    )(meta, pltpu.with_memory_space_constraint(cache, pltpu.HBM))
    return pltpu.with_memory_space_constraint(out, pltpu.VMEM)


def project_kernel(grid, bl, share, meta, *refs):
    x_refs, w_ref, refs = refs[:grid.n], refs[grid.n], refs[grid.n + 1:]
    out_refs, (xp_ref, starts) = refs[:-2], refs[-2:]

    @pl.when(pl.program_id(0) == 0)
    def _():
        facts = Facts(grid.n, meta)
        shard = facts.shard
        offset = jnp.int32(0)
        for b in range(grid.n):
            starts[b] = offset
            offset = offset + facts.length(b)
        lane = lax.broadcasted_iota(jnp.int32, (8, grid.n * bl), 1)
        target = jnp.full(lane.shape, -1, jnp.int32)
        owners = [
            grid.owner(shard, kx, kz) for kx in range(grid.xs) for kz in range(grid.zs)
        ]
        for k, b in enumerate(owners):
            order = lane - k * bl
            used = (order >= 0) & (order < facts.length(b))
            target = jnp.where(used, order + starts[b], target)
        row = lax.broadcasted_iota(jnp.int32, (share, grid.n * bl), 0)
        target = jnp.broadcast_to(target[:1], row.shape)
        picks = [jnp.where(row + b * share == target, 1.0, 0.0) for b in owners]
        pick = jnp.concatenate(picks, axis=0).astype(jnp.bfloat16)
        x = jnp.concatenate([ref[...] for ref in x_refs], axis=0)
        chosen = jnp.dot(pick, x, preferred_element_type=jnp.float32)
        xp_ref[...] = chosen.astype(jnp.bfloat16)

    result = jnp.dot(xp_ref[...], w_ref[0], preferred_element_type=jnp.float32)
    rows = grid.zs * share
    for i, out_ref in enumerate(out_refs):
        chunk, kx = i // grid.xs, i % grid.xs

        @pl.when(pl.program_id(0) == chunk)
        def _(out_ref=out_ref, kx=kx):
            out_ref[...] = result[kx * rows:(kx + 1) * rows]


def project(grid, meta, xs, w, bl, share, chunks):
    k, cols = w.shape[1:]
    rows = grid.n * share
    tile = cols // chunks
    piece = (grid.zs * share, tile)
    return pl.pallas_call(
        functools.partial(project_kernel, grid, bl, share),
        grid_spec=pltpu.PrefetchScalarGridSpec(
            num_scalar_prefetch=1,
            grid=(chunks,),
            in_specs=[pl.BlockSpec((bl, k), lambda j, *m: (0, 0))] * grid.n
            + [pl.BlockSpec((1, k, tile), lambda j, *m: (0, 0, j))],
            out_specs=[pl.BlockSpec(piece, lambda j, *m: (0, 0))] * (chunks * grid.xs),
            scratch_shapes=[
                pltpu.VMEM((rows, k), jnp.bfloat16), pltpu.SMEM((grid.n,), jnp.int32)
            ],
        ),
        out_shape=[jax.ShapeDtypeStruct(piece, jnp.float32)] * (chunks * grid.xs),
        compiler_params=pltpu.CompilerParams(vmem_limit_bytes=20 * MIB),
        cost_estimate=pl.CostEstimate(
            flops=2 * rows * k * cols, bytes_accessed=2 * k * cols + 4 * rows * cols,
            transcendentals=0,
        ),
        name="project",
    )(meta, *xs, w)


def three_terms(value):
    high = value.astype(jnp.bfloat16).astype(jnp.float32)
    mid = (value - high).astype(jnp.bfloat16).astype(jnp.float32)
    return [high, mid, value - high - mid]


def encode(peak, total):
    lane = lax.broadcasted_iota(jnp.int32, peak.shape, 1)
    out = jnp.zeros(peak.shape, jnp.float32)
    for i, term in enumerate(three_terms(peak) + three_terms(total)):
        term = jnp.where(lane < SLOT, term, 0.0)
        out = out + (pltpu.roll(term, i * SLOT, 1) if i else term)
    return out.astype(jnp.bfloat16)


def decode(tile):
    terms = tile.astype(jnp.float32)
    parts = [terms] + [pltpu.roll(terms, EXTRA - i * SLOT, 1) for i in range(1, 6)]
    return parts[0] + parts[1] + parts[2], parts[3] + parts[4] + parts[5]


def merge(refs, heads):
    width = heads * HD
    peaks, totals = zip(*[decode(ref[:, width:]) for ref in refs])
    rows = peaks[0].shape[0]
    peak = functools.reduce(jnp.maximum, peaks)
    weights = [jnp.exp2(one - peak) for one in peaks]
    total = functools.reduce(jnp.add, [w * one for w, one in zip(weights, totals)])
    out = []
    for h in range(heads):
        terms = [
            jnp.broadcast_to(weight[:, h:h + 1], (rows, HD))
            * ref[:, h * HD:(h + 1) * HD].astype(jnp.float32)
            for weight, ref in zip(weights, refs)
        ]
        out.append(functools.reduce(jnp.add, terms))
    return out, peak, total


def merge_kernel(zs, heads, *refs):
    sources, outs = refs[:-zs], refs[-zs:]
    for kz in range(zs):
        parts, peak, total = merge([ref.at[kz] for ref in sources], heads)
        for h in range(heads):
            outs[kz][:, h * HD:(h + 1) * HD] = parts[h].astype(jnp.bfloat16)
        outs[kz][:, heads * HD:] = encode(peak, total)


def merge_column(sources, heads):
    zs, bl, width = sources[0].shape
    return pl.pallas_call(
        functools.partial(merge_kernel, zs, heads),
        out_shape=[jax.ShapeDtypeStruct((bl, width), jnp.bfloat16)] * zs,
        compiler_params=pltpu.CompilerParams(vmem_limit_bytes=16 * MIB),
        name="merge",
    )(*sources)


def attend_kernel(grid, kx, bl, share, first, heads, tile_len, coords, meta, *refs):
    q_refs, refs = refs[:len(coords)], refs[len(coords):]
    kv_refs, refs = refs[:heads], refs[heads:]
    own_ref, out_ref, q32_ref, acc_ref, m_ref = refs
    facts = Facts(grid.n, meta)
    shard = facts.shard
    rows = grid.n * share
    for q_ref, places in zip(q_refs, coords):
        for i, (fx, fz) in enumerate(places):
            at = pl.multiple_of(grid.owner(shard, fx, fz) * share, 8)
            q32_ref[pl.ds(at, share), :] = q_ref[i].astype(jnp.float32)
    q32_ref[rows:, :] = jnp.zeros((bl + 8, q32_ref.shape[1]), jnp.float32)
    acc_ref[...] = jnp.zeros_like(acc_ref)
    m_ref[...] = jnp.full_like(m_ref, NEG)

    def one(kz, carry):
        attend_block(
            grid, kx, bl, first, heads, tile_len, kz, facts,
            kv_refs, own_ref, out_ref, q32_ref, acc_ref, m_ref,
        )
        return carry

    lax.fori_loop(0, grid.zs, one, 0)


def attend_block(grid, kx, bl, first, heads, tile_len, step, facts,
                 kv_refs, own_ref, out_ref, q32_ref, acc_ref, m_ref):
    block = grid.owner(facts.shard, kx, step)
    offset = jnp.int32(0)
    for b in range(grid.n):
        offset = offset + jnp.where(b < block, facts.length(b), 0)
    prompt = facts.prompt(block)
    valid = jnp.clip(facts.prompt_length(prompt) - facts.shard * tile_len, 0, tile_len)
    c2 = LOG2E / math.sqrt(HD)
    chunk = min(CHUNK, tile_len)
    width = heads * GR * HD

    rest = offset % 8
    window = q32_ref[pl.ds(pl.multiple_of(offset - rest, 8), bl + 8), :]
    window = pltpu.roll(window, jnp.where(rest == 0, 0, bl + 8 - rest), 0)
    queries = window[:bl].astype(jnp.bfloat16)

    def group(g, used):
        return jnp.concatenate(
            [queries[:used, (g * GR + r) * HD:(g * GR + r + 1) * HD] for r in range(GR)], axis=0
        )

    def with_ones(v):
        return jnp.concatenate([v, jnp.ones(v.shape, jnp.bfloat16)], axis=1)

    def sums(p, v):
        return jnp.dot(p, with_ones(v), preferred_element_type=jnp.float32)

    def keys(g, at, size):
        return kv_refs[g][prompt, pl.ds(at, size), :HD]

    def vals(g, at, size):
        return kv_refs[g][prompt, pl.ds(at, size), HD:]

    def put(g, used, acc, m):
        m = jnp.broadcast_to(m, (GR * used, HD))
        for r in range(GR):
            acc_ref[g, r * bl:r * bl + used] = acc[r * used:(r + 1) * used]
            m_ref[g, r * bl:r * bl + used] = m[r * used:(r + 1) * used]

    def update(g, s, seen, v):
        s = jnp.where(seen, s, NEG)
        before = m_ref[g][:, :1]
        m = jnp.maximum(before, jnp.max(s, axis=1, keepdims=True))
        p = jnp.where(seen, jnp.exp2((s - m) * c2), 0.0).astype(jnp.bfloat16)
        acc_ref[g] = acc_ref[g] * jnp.exp2((before - m) * c2) + sums(p, v)
        m_ref[g] = jnp.broadcast_to(m, m_ref.shape[1:])

    def exact():
        acc_ref[...] = jnp.zeros_like(acc_ref)
        m_ref[...] = jnp.full_like(m_ref, NEG)

        def one(c, carry):
            at = pl.multiple_of(c * chunk, chunk)
            for g in range(heads):
                s = dot_nt(group(g, bl), keys(g, at, chunk))
                here = lax.broadcasted_iota(jnp.int32, s.shape, 1) + at
                update(g, s, here < valid, vals(g, at, chunk))
            return carry

        lax.fori_loop(0, (valid + chunk - 1) // chunk, one, 0)

    length = facts.length(block)

    @pl.when(valid == 0)
    def _():
        acc_ref[...] = jnp.zeros_like(acc_ref)
        m_ref[...] = jnp.full_like(m_ref, NEG)

    step_of = min(PIECE, tile_len) // chunk

    def single_pass(used, count):
        items = [(g, c) for c in range(count) for g in range(heads)]
        q = [group(g, used) for g in range(heads)]
        peaks = [None] * heads
        accs = [None] * heads
        ahead = dot_nt(q[0], keys(0, 0, chunk))
        for i, (g, c) in enumerate(items):
            s = ahead
            if i + 1 < len(items):
                ng, nc = items[i + 1]
                ahead = dot_nt(q[ng], keys(ng, nc * chunk, chunk))
            if (c + 1) * chunk > (count - step_of) * chunk:
                here = lax.broadcasted_iota(jnp.int32, s.shape, 1) + c * chunk
                s = jnp.where(here < valid, s, NEG)
            if c == 0:
                peaks[g] = jnp.max(s, axis=1, keepdims=True)
            p = jnp.exp2((s - peaks[g]) * c2).astype(jnp.bfloat16)
            part = sums(p, vals(g, c * chunk, chunk))
            accs[g] = part if c == 0 else accs[g] + part
        for g in range(heads):
            put(g, used, accs[g], peaks[g])

    for count in range(step_of, tile_len // chunk + 1, step_of):
        for used in range(ROUND, bl + 1, ROUND):
            some_keys = (valid > (count - step_of) * chunk) & (valid <= count * chunk)
            some_rows = (length > used - ROUND) & (length <= used)
            pl.when(some_keys & some_rows)(functools.partial(single_pass, used, count))

    def own_part():
        @pl.when(step == 0)
        def _():
            for g in range(heads):
                base = (first + g) * 2 * HD
                s = dot_nt(group(g, bl), own_ref[0, :, base:base + HD])
                row = lax.broadcasted_iota(jnp.int32, s.shape, 0) % bl
                col = lax.broadcasted_iota(jnp.int32, s.shape, 1)
                update(g, s, col <= row, own_ref[0, :, base + HD:base + 2 * HD])

    def write():
        lane = lax.broadcasted_iota(jnp.int32, (bl, EXTRA), 1)
        total = jnp.zeros((bl, EXTRA), jnp.float32)
        peak = jnp.zeros((bl, EXTRA), jnp.float32)
        for g in range(heads):
            for r in range(GR):
                h = g * GR + r
                at = slice(r * bl, (r + 1) * bl)
                out_ref[step, :, h * HD:(h + 1) * HD] = acc_ref[g, at, :HD].astype(jnp.bfloat16)
                total = jnp.where(lane == h, acc_ref[g, at, HD:], total)
                peak = jnp.where(lane == h, m_ref[g, at], peak)
        out_ref[step, :, width:] = encode(peak * c2, total)
        return total

    if kx == 0:
        own_part()
    total = write()

    @pl.when(jnp.max(jnp.where(total < BIG, 0.0, 1.0)) > 0.5)
    def _():
        exact()
        if kx == 0:
            own_part()
        write()


def attend(grid, kx, meta, queries, coords, caches, own, first, heads):
    zs = grid.zs
    _, share, cols = queries[0].shape
    bl = own.shape[1]
    tile_len = caches[0].shape[1]
    width = heads * GR * HD + EXTRA
    whole = pl.BlockSpec(memory_space=pltpu.VMEM)
    return pl.pallas_call(
        functools.partial(attend_kernel, grid, kx, bl, share, first, heads, tile_len, coords),
        grid_spec=pltpu.PrefetchScalarGridSpec(
            num_scalar_prefetch=1,
            grid=(1,),
            in_specs=[whole] * (len(queries) + heads + 1),
            out_specs=whole,
            scratch_shapes=[
                pltpu.VMEM((grid.n * share + bl + 8, cols), jnp.float32),
                pltpu.VMEM((heads, GR * bl, 2 * HD), jnp.float32),
                pltpu.VMEM((heads, GR * bl, HD), jnp.float32),
            ],
        ),
        out_shape=jax.ShapeDtypeStruct((zs, bl, width), jnp.bfloat16),
        compiler_params=pltpu.CompilerParams(vmem_limit_bytes=20 * MIB),
        cost_estimate=pl.CostEstimate(
            flops=8 * zs * bl * cols * tile_len,
            bytes_accessed=2 * zs * tile_len * heads * 2 * HD,
            transcendentals=zs * bl * heads * GR * tile_len,
        ),
        name="attend",
    )(meta, *queries, *caches, own)


def finish_kernel(n, heads, bl, done, meta, *refs):
    sources, out_ref = refs[:-1], refs[-1]
    pieces = sources[done:]
    facts = Facts(n, meta)
    length = facts.length(facts.shard)
    row = lax.broadcasted_iota(jnp.int32, (bl, HD), 0)
    width = heads * GR * HD
    for c in range(done):
        out_ref[0, :, c * width:(c + 1) * width] = sources[c][0]
    parts, _, total = merge(pieces, heads * GR)
    for h in range(heads * GR):
        at = done * width + h * HD
        value = parts[h] / jnp.broadcast_to(total[:, h:h + 1], (bl, HD))
        out_ref[0, :, at:at + HD] = jnp.where(row < length, value, 0.0).astype(jnp.bfloat16)


def finish(n, meta, done, pieces, heads):
    bl = pieces[0].shape[0]
    whole = pl.BlockSpec(memory_space=pltpu.VMEM)
    sources = list(done) + list(pieces)
    return pl.pallas_call(
        functools.partial(finish_kernel, n, heads, bl, len(done)),
        grid_spec=pltpu.PrefetchScalarGridSpec(
            num_scalar_prefetch=1,
            grid=(1,),
            in_specs=[whole] * len(sources),
            out_specs=whole,
        ),
        out_shape=jax.ShapeDtypeStruct((1, bl, (len(done) + 1) * heads * GR * HD), jnp.bfloat16),
        compiler_params=pltpu.CompilerParams(vmem_limit_bytes=16 * MIB),
        name="finish",
    )(meta, *sources)


def shards(
    hidden_rows,
    carried,
    query_weight,
    response_cache,
    prompt_cache,
    prompt_lengths,
    response_lengths,
    block_prompts,
):
    grid = Grid(lax.axis_size("seq"))
    bl = hidden_rows.shape[1]
    local_kv = response_cache.shape[2] // (2 * HD)
    share = bl * 5 // 8
    chunks = 2 if local_kv % 2 == 0 else 1
    heads = local_kv // chunks
    part_cols = heads * GR * HD
    place = jnp.stack([lax.axis_index("sec"), lax.axis_index("seq")]).astype(jnp.int32)

    def after(value, done):
        return lax.optimization_barrier((value, done))[0]

    def fetched(head, done=()):
        return fetch_cache(grid.n, after(meta, done), prompt_cache, 2 * HD, head)

    handed = lax.ppermute(carried, "sec", [(0, 1)])
    depth = query_weight.shape[1]
    hidden = hidden_rows if depth % HD else fetch([hidden_rows])[0]
    slices = split(grid, place, hidden, handed, depth)
    later_place = after(place, slices[0])
    prompts = block_prompts[:, :, 0]
    meta = jnp.concatenate(
        [later_place] + [a[i] for a in (response_lengths, prompts) for i in range(2)]
        + [prompt_lengths]
    )
    weight, own = fetch([query_weight, response_cache])
    x = [slices[0]] + [None] * (grid.n - 1)
    for kz in reversed(range(grid.zs)):
        for kx in reversed(range(grid.xs)):
            k = kx * grid.zs + kz
            if k:
                x[k] = grid.swap(slices[k], kx, kz)
    part = project(grid, meta, x, weight, bl, share, chunks)
    part = [piece.reshape(grid.zs, share, part_cols) for piece in part]
    part = [part[c * grid.xs:(c + 1) * grid.xs] for c in range(chunks)]

    def narrow(value):
        return (value * 0.125).astype(jnp.float16)

    def widen(value):
        return value.astype(jnp.float32) * 8.0

    def both(first, second):
        return lax.optimization_barrier((first, second))

    def reduce_x(parts, done=()):
        got = [grid.swap(after(narrow(parts[kx]), done), kx, 0) for kx in range(1, grid.xs)]
        return functools.reduce(jnp.add, [parts[0]] + [widen(value) for value in got])

    def narrow_z(held):
        return [narrow(held[kz]) for kz in range(1, grid.zs)]

    def sum_z(held, sends, beside):
        got = [grid.swap(send, 0, kz + 1) for kz, send in enumerate(sends)]
        parts = [after(held[0], beside)] + [widen(value) for value in got]
        return functools.reduce(jnp.add, parts).astype(jnp.bfloat16)

    def gather_z(value):
        return [value] + [grid.swap(value, 0, kz) for kz in range(1, grid.zs)]

    def gather_x(value):
        return [value] + [grid.swap(value, kx, 0) for kx in range(1, grid.xs)]

    z_then_x = [[(kx, kz) for kz in range(grid.zs)] for kx in range(grid.xs)]
    x_then_z = [[(kx, kz) for kx in range(grid.xs)] for kz in range(grid.zs)]

    def call(c, kx, queries):
        return attend(
            grid, kx, meta, queries, x_then_z if c else z_then_x,
            caches[c * heads:(c + 1) * heads], own, c * heads, heads,
        )

    def call_far(c, queries):
        outs = [call(c, kx, queries) for kx in range(1, grid.xs)]
        return outs, [grid.swap(out, kx + 1, 0) for kx, out in enumerate(outs)]

    def send_z(merged):
        return [merged[0]] + [grid.swap(merged[kz], 0, kz) for kz in range(1, grid.zs)]

    half = (local_kv + 1) // 4
    caches = [fetched(head) for head in range(half)]
    part[0][0] = after(part[0][0], caches)
    held = reduce_x(part[0])
    sends = narrow_z(held)
    if chunks > 1:
        sends, part[1][1] = both(sends, part[1][1])
        later = reduce_x(part[1])
    caches += [fetched(head, sends) for head in range(half, heads)]
    mine = sum_z(held, sends, caches)
    column = gather_z(mine)
    if chunks > 1:
        caches += [fetched(head, mine) for head in range(heads, heads + half)]
        sends = narrow_z(after(later, mine))
        column = after(column, (caches, sends))
    queries = gather_x(jnp.stack(column))
    if chunks == 1:
        outs, mets = call_far(0, queries)
        queries[0] = after(queries[0], outs)
        pieces = send_z(merge_column([call(0, 0, queries)] + mets, heads * GR))
        return finish(grid.n, meta, [], pieces, heads)
    caches += [fetched(head, sends) for head in range(heads + half, local_kv)]
    mine = sum_z(later, sends, caches)
    queries[0] = after(queries[0], mine)
    near = jnp.stack(gather_x(mine))
    outs, mets = call_far(0, queries)
    near = after(near, outs)
    queries[0] = after(queries[0], near)
    later = gather_z(near)
    held = call(0, 0, queries)
    merged = merge_column([held] + mets, heads * GR)
    later[0] = after(later[0], merged)
    outs, mets = call_far(1, later)
    merged, later[0] = both(after(merged, outs), later[0])
    pieces = send_z(merged)
    held = call(1, 0, later)
    done = finish(grid.n, meta, [], pieces, heads)
    pieces = send_z(merge_column([held] + mets, heads * GR))
    return finish(grid.n, meta, [done], pieces, heads)


def solution(mesh):
    placed = (
        P("sec", "seq", None),
        P("sec", "seq", None),
        P("sec", "seq", "tp"),
        P("sec", "seq", "tp"),
        P("sec", None, "seq", "tp"),
        P(),
        P(),
        P(),
    )
    return jax.shard_map(
        shards, mesh=mesh, in_specs=placed, out_specs=P("sec", "seq", "tp"), check_vma=False
    )
```

```python
import functools
import math

import jax
import jax.numpy as jnp
from jax import lax
from jax.experimental import pallas as pl
from jax.experimental.pallas import tpu as pltpu
from jax.sharding import PartitionSpec as P

HD = 128
GR = 4
NEG = -1e30
LOG2E = 1.4426950408889634
CHUNK = 512
PIECE = 1024
ROUND = 32
EXTRA = 128
SLOT = 16
BIG = 2.0 ** 100
MIB = 1024 * 1024


def dot_nt(a, b):
    return lax.dot_general(a, b, (((1,), (1,)), ((), ())), preferred_element_type=jnp.float32)


class Grid:
    def __init__(self, count):
        self.n = count
        self.xs = 1 << ((count.bit_length() - 1) // 2)
        self.zs = count // self.xs

    def owner(self, shard, kx, kz):
        z, x = shard // self.xs, shard % self.xs
        return (z ^ kz) * self.xs + (x ^ kx)

    def swap(self, value, kx, kz):
        pairs = [(s, self.owner(s, kx, kz)) for s in range(self.n)]
        return lax.ppermute(value, "seq", pairs)


class Facts:
    def __init__(self, meta):
        self.meta = meta
        self.section, self.shard = meta[5, 0], meta[5, 1]

    def length(self, block):
        return self.meta[self.section, block]

    def prompt(self, block):
        return self.meta[2 + self.section, block]

    def prompt_length(self, prompt):
        return self.meta[4, prompt]


def split_kernel(grid, depth, meta, hidden_ref, handed_ref, *out_refs):
    for kx in range(grid.xs):
        for kz in range(grid.zs):
            at = pl.multiple_of(grid.owner(meta[1], kx, kz) * depth, HD)
            total = hidden_ref[0, :, pl.ds(at, depth)].astype(jnp.float32) + handed_ref[
                0, :, pl.ds(at, depth)
            ].astype(jnp.float32)
            out_refs[kx * grid.zs + kz][...] = total.astype(jnp.bfloat16)


def split(grid, meta, hidden, handed, depth):
    bl = hidden.shape[1]
    if depth % HD:
        total = (hidden[0].astype(jnp.float32) + handed[0].astype(jnp.float32)).astype(jnp.bfloat16)
        return [
            lax.dynamic_slice_in_dim(total, grid.owner(meta[1], kx, kz) * depth, depth, 1)
            for kx in range(grid.xs) for kz in range(grid.zs)
        ]
    whole = pl.BlockSpec(hidden.shape, lambda i, *m: (0, 0, 0))
    return pl.pallas_call(
        functools.partial(split_kernel, grid, depth),
        grid_spec=pltpu.PrefetchScalarGridSpec(
            num_scalar_prefetch=1,
            grid=(1,),
            in_specs=[whole, whole],
            out_specs=[pl.BlockSpec((bl, depth), lambda i, *m: (0, 0))] * grid.n,
        ),
        out_shape=[jax.ShapeDtypeStruct((bl, depth), jnp.bfloat16)] * grid.n,
        compiler_params=pltpu.CompilerParams(vmem_limit_bytes=16 * MIB),
        name="split",
    )(meta, hidden, handed)


def run_moves(moves):
    for needed, move in moves:
        if needed is None:
            move.start()
        else:
            pl.when(needed)(move.start)
    for needed, move in moves:
        if needed is None:
            move.wait()
        else:
            pl.when(needed)(move.wait)


def fetch_kernel(*refs):
    count = len(refs) // 2
    run_moves([
        (None, pltpu.make_async_copy(refs[i], refs[count + i], refs[-1].at[i]))
        for i in range(count)
    ])


def fetch(arrays):
    anywhere, near = pl.BlockSpec(memory_space=pltpu.HBM), pl.BlockSpec(memory_space=pltpu.VMEM)
    size = sum(math.prod(array.shape) for array in arrays)
    out = pl.pallas_call(
        fetch_kernel,
        in_specs=[anywhere] * len(arrays),
        out_specs=[near] * len(arrays),
        scratch_shapes=[pltpu.SemaphoreType.DMA((len(arrays),))],
        out_shape=[pltpu.VMEM(array.shape, array.dtype) for array in arrays],
        compiler_params=pltpu.CompilerParams(vmem_limit_bytes=4 * MIB),
        cost_estimate=pl.CostEstimate(flops=0, bytes_accessed=2 * size, transcendentals=0),
        name="fetch",
    )(*[pltpu.with_memory_space_constraint(array, pltpu.HBM) for array in arrays])
    return [pltpu.with_memory_space_constraint(array, pltpu.VMEM) for array in out]


def fetch_cache_kernel(n, chunk, width, first, meta, cache_ref, kv_ref, sem):
    count, tile_len = kv_ref.shape[:2]
    facts = Facts(meta)
    moves = []
    for p in range(count):
        asked = facts.prompt(0) == p
        for b in range(1, n):
            asked = asked | (facts.prompt(b) == p)
        for c in range(tile_len // chunk):
            at = pl.ds(c * chunk, chunk)
            needed = asked & (facts.prompt_length(p) > facts.shard * tile_len + c * chunk)
            moves.append((needed, pltpu.make_async_copy(
                cache_ref.at[0, p, at, pl.ds(first * width, width)], kv_ref.at[p, at],
                sem.at[p, c],
            )))
    run_moves(moves)


def fetch_cache(n, meta, cache, width, first):
    count, tile_len = cache.shape[1:3]
    chunk = min(PIECE, tile_len)
    shape = (count, tile_len, width)
    out = pl.pallas_call(
        functools.partial(fetch_cache_kernel, n, chunk, width, first),
        grid_spec=pltpu.PrefetchScalarGridSpec(
            num_scalar_prefetch=1,
            grid=(1,),
            in_specs=[pl.BlockSpec(memory_space=pltpu.HBM)],
            out_specs=pl.BlockSpec(memory_space=pltpu.VMEM),
            scratch_shapes=[pltpu.SemaphoreType.DMA((count, tile_len // chunk))],
        ),
        out_shape=pltpu.VMEM(shape, cache.dtype),
        compiler_params=pltpu.CompilerParams(vmem_limit_bytes=4 * MIB),
        cost_estimate=pl.CostEstimate(
            flops=0, bytes_accessed=2 * math.prod(shape), transcendentals=0
        ),
        name="fetch_cache",
    )(meta, pltpu.with_memory_space_constraint(cache, pltpu.HBM))
    return pltpu.with_memory_space_constraint(out, pltpu.VMEM)


def project_kernel(grid, bl, share, meta, *refs):
    x_refs, w_ref, refs = refs[:grid.n], refs[grid.n], refs[grid.n + 1:]
    out_refs, (xp_ref, starts) = refs[:-2], refs[-2:]

    @pl.when(pl.program_id(0) == 0)
    def _():
        facts = Facts(meta)
        shard = facts.shard
        offset = jnp.int32(0)
        for b in range(grid.n):
            starts[b] = offset
            offset = offset + facts.length(b)
        lane = lax.broadcasted_iota(jnp.int32, (8, grid.n * bl), 1)
        target = jnp.full(lane.shape, -1, jnp.int32)
        owners = [
            grid.owner(shard, kx, kz) for kx in range(grid.xs) for kz in range(grid.zs)
        ]
        for k, b in enumerate(owners):
            order = lane - k * bl
            used = (order >= 0) & (order < facts.length(b))
            target = jnp.where(used, order + starts[b], target)
        row = lax.broadcasted_iota(jnp.int32, (share, grid.n * bl), 0)
        target = jnp.broadcast_to(target[:1], row.shape)
        picks = [jnp.where(row + b * share == target, 1.0, 0.0) for b in owners]
        pick = jnp.concatenate(picks, axis=0).astype(jnp.bfloat16)
        x = jnp.concatenate([ref[...] for ref in x_refs], axis=0)
        chosen = jnp.dot(pick, x, preferred_element_type=jnp.float32)
        xp_ref[...] = chosen.astype(jnp.bfloat16)

    result = jnp.dot(xp_ref[...], w_ref[0], preferred_element_type=jnp.float32)
    rows = grid.zs * share
    for i, out_ref in enumerate(out_refs):
        chunk, kx = i // grid.xs, i % grid.xs

        @pl.when(pl.program_id(0) == chunk)
        def _(out_ref=out_ref, kx=kx):
            out_ref[...] = result[kx * rows:(kx + 1) * rows]


def project(grid, meta, xs, w, bl, share, chunks):
    k, cols = w.shape[1:]
    rows = grid.n * share
    tile = cols // chunks
    piece = (grid.zs * share, tile)
    return pl.pallas_call(
        functools.partial(project_kernel, grid, bl, share),
        grid_spec=pltpu.PrefetchScalarGridSpec(
            num_scalar_prefetch=1,
            grid=(chunks,),
            in_specs=[pl.BlockSpec((bl, k), lambda j, *m: (0, 0))] * grid.n
            + [pl.BlockSpec((1, k, tile), lambda j, *m: (0, 0, j))],
            out_specs=[pl.BlockSpec(piece, lambda j, *m: (0, 0))] * (chunks * grid.xs),
            scratch_shapes=[
                pltpu.VMEM((rows, k), jnp.bfloat16), pltpu.SMEM((grid.n,), jnp.int32)
            ],
        ),
        out_shape=[jax.ShapeDtypeStruct(piece, jnp.float32)] * (chunks * grid.xs),
        compiler_params=pltpu.CompilerParams(vmem_limit_bytes=20 * MIB),
        cost_estimate=pl.CostEstimate(
            flops=2 * rows * k * cols, bytes_accessed=2 * k * cols + 4 * rows * cols,
            transcendentals=0,
        ),
        name="project",
    )(meta, *xs, w)


def three_terms(value):
    high = value.astype(jnp.bfloat16).astype(jnp.float32)
    mid = (value - high).astype(jnp.bfloat16).astype(jnp.float32)
    return [high, mid, value - high - mid]


def encode(peak, total):
    lane = lax.broadcasted_iota(jnp.int32, peak.shape, 1)
    out = jnp.zeros(peak.shape, jnp.float32)
    for i, term in enumerate(three_terms(peak) + three_terms(total)):
        term = jnp.where(lane < SLOT, term, 0.0)
        out = out + (pltpu.roll(term, i * SLOT, 1) if i else term)
    return out.astype(jnp.bfloat16)


def decode(tile):
    terms = tile.astype(jnp.float32)
    parts = [terms] + [pltpu.roll(terms, EXTRA - i * SLOT, 1) for i in range(1, 6)]
    return parts[0] + parts[1] + parts[2], parts[3] + parts[4] + parts[5]


def merge(refs, heads):
    width = heads * HD
    peaks, totals = zip(*[decode(ref[:, width:]) for ref in refs])
    rows = peaks[0].shape[0]
    peak = functools.reduce(jnp.maximum, peaks)
    weights = [jnp.exp2(one - peak) for one in peaks]
    total = functools.reduce(jnp.add, [w * one for w, one in zip(weights, totals)])
    out = []
    for h in range(heads):
        terms = [
            jnp.broadcast_to(weight[:, h:h + 1], (rows, HD))
            * ref[:, h * HD:(h + 1) * HD].astype(jnp.float32)
            for weight, ref in zip(weights, refs)
        ]
        out.append(functools.reduce(jnp.add, terms))
    return out, peak, total


def merge_kernel(zs, heads, *refs):
    sources, outs = refs[:-zs], refs[-zs:]
    for kz in range(zs):
        parts, peak, total = merge([ref.at[kz] for ref in sources], heads)
        for h in range(heads):
            outs[kz][:, h * HD:(h + 1) * HD] = parts[h].astype(jnp.bfloat16)
        outs[kz][:, heads * HD:] = encode(peak, total)


def merge_column(sources, heads):
    zs, bl, width = sources[0].shape
    return pl.pallas_call(
        functools.partial(merge_kernel, zs, heads),
        out_shape=[jax.ShapeDtypeStruct((bl, width), jnp.bfloat16)] * zs,
        compiler_params=pltpu.CompilerParams(vmem_limit_bytes=16 * MIB),
        name="merge",
    )(*sources)


def attend_kernel(grid, kx, bl, share, heads, tile_len, coords, meta, *refs):
    q_refs, refs = refs[:len(coords)], refs[len(coords):]
    kv_refs, refs = refs[:heads], refs[heads:]
    out_ref, own_q_ref = refs[0], refs[1] if kx == 0 else None
    q32_ref, acc_ref, m_ref, over_ref = refs[-4:]
    facts = Facts(meta)
    shard = facts.shard
    rows = grid.n * share
    for q_ref, places in zip(q_refs, coords):
        for i, (fx, fz) in enumerate(places):
            at = pl.multiple_of(grid.owner(shard, fx, fz) * share, 8)
            q32_ref[pl.ds(at, share), :] = q_ref[i].astype(jnp.float32)
    q32_ref[rows:, :] = jnp.zeros((bl + 8, q32_ref.shape[1]), jnp.float32)

    def one(kz, carry):
        attend_block(
            grid, kx, bl, heads, tile_len, kz, facts,
            kv_refs, out_ref, own_q_ref, q32_ref, acc_ref, m_ref, over_ref,
        )
        return carry

    lax.fori_loop(0, grid.zs, one, 0)


def group_rows(queries, g, used):
    return jnp.concatenate(
        [queries[:used, (g * GR + r) * HD:(g * GR + r + 1) * HD] for r in range(GR)], axis=0
    )


def sums(p, v):
    v = jnp.concatenate([v, jnp.ones(v.shape, jnp.bfloat16)], axis=1)
    return jnp.dot(p, v, preferred_element_type=jnp.float32)


def write_partial(accs, peaks, store, c2):
    used = accs[0].shape[0] // GR
    lane = lax.broadcasted_iota(jnp.int32, (used, EXTRA), 1)
    total = jnp.zeros((used, EXTRA), jnp.float32)
    peak = jnp.zeros((used, EXTRA), jnp.float32)
    for g, (acc, m) in enumerate(zip(accs, peaks)):
        for r in range(GR):
            h = g * GR + r
            at = slice(r * used, (r + 1) * used)
            store(slice(h * HD, (h + 1) * HD), acc[at, :HD].astype(jnp.bfloat16))
            total = jnp.where(lane == h, acc[at, HD:], total)
            peak = jnp.where(lane == h, m[at], peak)
    width = len(accs) * GR * HD
    store(slice(width, width + EXTRA), encode(peak * c2, total))
    return total


def attend_block(grid, kx, bl, heads, tile_len, step, facts,
                 kv_refs, out_ref, own_q_ref, q32_ref, acc_ref, m_ref, over_ref):
    block = grid.owner(facts.shard, kx, step)
    offset = jnp.int32(0)
    for b in range(grid.n):
        offset = offset + jnp.where(b < block, facts.length(b), 0)
    prompt = facts.prompt(block)
    valid = jnp.clip(facts.prompt_length(prompt) - facts.shard * tile_len, 0, tile_len)
    c2 = LOG2E / math.sqrt(HD)
    chunk = min(CHUNK, tile_len)
    width = heads * GR * HD

    rest = offset % 8
    window = q32_ref[pl.ds(pl.multiple_of(offset - rest, 8), bl + 8), :]
    window = pltpu.roll(window, jnp.where(rest == 0, 0, bl + 8 - rest), 0)
    queries = window[:bl].astype(jnp.bfloat16)

    group = functools.partial(group_rows, queries)
    if kx == 0:
        @pl.when(step == 0)
        def _():
            own_q_ref[...] = queries

    def keys(g, at, size):
        return kv_refs[g][prompt, pl.ds(at, size), :HD]

    def vals(g, at, size):
        return kv_refs[g][prompt, pl.ds(at, size), HD:]

    def store(used, columns, value):
        out_ref[step, :used, columns] = value

    def update(g, s, seen, v):
        s = jnp.where(seen, s, NEG)
        before = m_ref[g][:, :1]
        m = jnp.maximum(before, jnp.max(s, axis=1, keepdims=True))
        p = jnp.where(seen, jnp.exp2((s - m) * c2), 0.0).astype(jnp.bfloat16)
        acc_ref[g] = acc_ref[g] * jnp.exp2((before - m) * c2) + sums(p, v)
        m_ref[g] = jnp.broadcast_to(m, m_ref.shape[1:])

    def exact():
        acc_ref[...] = jnp.zeros_like(acc_ref)
        m_ref[...] = jnp.full_like(m_ref, NEG)

        def one(c, carry):
            at = pl.multiple_of(c * chunk, chunk)
            for g in range(heads):
                s = dot_nt(group(g, bl), keys(g, at, chunk))
                here = lax.broadcasted_iota(jnp.int32, s.shape, 1) + at
                update(g, s, here < valid, vals(g, at, chunk))
            return carry

        lax.fori_loop(0, (valid + chunk - 1) // chunk, one, 0)
        write_partial(
            [acc_ref[g] for g in range(heads)], [m_ref[g] for g in range(heads)],
            functools.partial(store, bl), c2,
        )

    length = facts.length(block)

    @pl.when(valid == 0)
    def _():
        over_ref[0] = 0
        out_ref[step, :, :width] = jnp.zeros((bl, width), jnp.bfloat16)
        none = jnp.zeros((bl, EXTRA), jnp.float32)
        out_ref[step, :, width:] = encode(none + NEG, none)

    step_of = min(PIECE, tile_len) // chunk

    def single_pass(used, count):
        items = [(g, c) for c in range(count) for g in range(heads)]
        q = [group(g, used) for g in range(heads)]
        peaks = [None] * heads
        accs = [None] * heads
        ahead = dot_nt(q[0], keys(0, 0, chunk))
        for i, (g, c) in enumerate(items):
            s = ahead
            if i + 1 < len(items):
                ng, nc = items[i + 1]
                ahead = dot_nt(q[ng], keys(ng, nc * chunk, chunk))
            if (c + 1) * chunk > (count - step_of) * chunk:
                here = lax.broadcasted_iota(jnp.int32, s.shape, 1) + c * chunk
                s = jnp.where(here < valid, s, NEG)
            if c == 0:
                peaks[g] = jnp.max(s, axis=1, keepdims=True)
            p = jnp.exp2((s - peaks[g]) * c2).astype(jnp.bfloat16)
            part = sums(p, vals(g, c * chunk, chunk))
            accs[g] = part if c == 0 else accs[g] + part
        total = write_partial(
            accs, [jnp.broadcast_to(m, (GR * used, EXTRA)) for m in peaks],
            functools.partial(store, used), c2,
        )

        over_ref[0] = (jnp.max(jnp.where(total < BIG, 0.0, 1.0)) > 0.5).astype(jnp.int32)

    for count in range(step_of, tile_len // chunk + 1, step_of):
        for used in range(ROUND, bl + 1, ROUND):
            some_keys = (valid > (count - step_of) * chunk) & (valid <= count * chunk)
            some_rows = (length > used - ROUND) & (length <= used)
            pl.when(some_keys & some_rows)(functools.partial(single_pass, used, count))

    pl.when(over_ref[0] > 0)(exact)


def own_kernel(first, heads, bl, q_ref, own_ref, out_ref):
    c2 = LOG2E / math.sqrt(HD)
    queries = q_ref[...]
    accs, peaks = [], []
    for g in range(heads):
        base = (first + g) * 2 * HD
        s = dot_nt(group_rows(queries, g, bl), own_ref[0, :, base:base + HD])
        row = lax.broadcasted_iota(jnp.int32, s.shape, 0) % bl
        seen = lax.broadcasted_iota(jnp.int32, s.shape, 1) <= row
        s = jnp.where(seen, s, NEG)
        m = jnp.max(s, axis=1, keepdims=True)
        p = jnp.where(seen, jnp.exp2((s - m) * c2), 0.0).astype(jnp.bfloat16)
        accs.append(sums(p, own_ref[0, :, base + HD:base + 2 * HD]))
        peaks.append(jnp.broadcast_to(m, (GR * bl, EXTRA)))

    def store(columns, value):
        out_ref[:, columns] = value

    write_partial(accs, peaks, store, c2)


def attend_own(queries, own, first, heads):
    bl = own.shape[1]
    return pl.pallas_call(
        functools.partial(own_kernel, first, heads, bl),
        out_shape=jax.ShapeDtypeStruct((bl, heads * GR * HD + EXTRA), jnp.bfloat16),
        compiler_params=pltpu.CompilerParams(vmem_limit_bytes=16 * MIB),
        name="attend_own",
    )(queries, own)


def attend(grid, kx, meta, queries, coords, caches, bl, heads):
    zs = grid.zs
    _, share, cols = queries[0].shape
    tile_len = caches[0].shape[1]
    width = heads * GR * HD + EXTRA
    whole = pl.BlockSpec(memory_space=pltpu.VMEM)
    shapes = [(zs, bl, width)] + [(bl, cols)] * (kx == 0)
    outs = [jax.ShapeDtypeStruct(shape, jnp.bfloat16) for shape in shapes]
    return pl.pallas_call(
        functools.partial(attend_kernel, grid, kx, bl, share, heads, tile_len, coords),
        grid_spec=pltpu.PrefetchScalarGridSpec(
            num_scalar_prefetch=1,
            grid=(1,),
            in_specs=[whole] * (len(queries) + heads),
            out_specs=[whole] * len(outs),
            scratch_shapes=[
                pltpu.VMEM((grid.n * share + bl + 8, cols), jnp.float32),
                pltpu.VMEM((heads, GR * bl, 2 * HD), jnp.float32),
                pltpu.VMEM((heads, GR * bl, HD), jnp.float32),
                pltpu.SMEM((1,), jnp.int32),
            ],
        ),
        out_shape=outs,
        compiler_params=pltpu.CompilerParams(vmem_limit_bytes=20 * MIB),
        cost_estimate=pl.CostEstimate(
            flops=8 * zs * bl * cols * tile_len,
            bytes_accessed=2 * zs * tile_len * heads * 2 * HD,
            transcendentals=zs * bl * heads * GR * tile_len,
        ),
        name="attend",
    )(meta, *queries, *caches)


def finish_kernel(heads, bl, done, meta, *refs):
    sources, out_ref = refs[:-1], refs[-1]
    pieces = sources[done:]
    facts = Facts(meta)
    length = facts.length(facts.shard)
    row = lax.broadcasted_iota(jnp.int32, (bl, HD), 0)
    width = heads * GR * HD
    for c in range(done):
        out_ref[0, :, c * width:(c + 1) * width] = sources[c][0]
    parts, _, total = merge(pieces, heads * GR)
    for h in range(heads * GR):
        at = done * width + h * HD
        value = parts[h] / jnp.broadcast_to(total[:, h:h + 1], (bl, HD))
        out_ref[0, :, at:at + HD] = jnp.where(row < length, value, 0.0).astype(jnp.bfloat16)


def finish(meta, done, pieces, heads):
    bl = pieces[0].shape[0]
    whole = pl.BlockSpec(memory_space=pltpu.VMEM)
    sources = list(done) + list(pieces)
    return pl.pallas_call(
        functools.partial(finish_kernel, heads, bl, len(done)),
        grid_spec=pltpu.PrefetchScalarGridSpec(
            num_scalar_prefetch=1,
            grid=(1,),
            in_specs=[whole] * len(sources),
            out_specs=whole,
        ),
        out_shape=jax.ShapeDtypeStruct((1, bl, (len(done) + 1) * heads * GR * HD), jnp.bfloat16),
        compiler_params=pltpu.CompilerParams(vmem_limit_bytes=16 * MIB),
        name="finish",
    )(meta, *sources)


def shards(
    hidden_rows,
    carried,
    query_weight,
    response_cache,
    prompt_cache,
    prompt_lengths,
    response_lengths,
    block_prompts,
):
    grid = Grid(lax.axis_size("seq"))
    bl = hidden_rows.shape[1]
    local_kv = response_cache.shape[2] // (2 * HD)
    share = bl * 5 // 8
    chunks = 2 if local_kv % 2 == 0 else 1
    heads = local_kv // chunks
    part_cols = heads * GR * HD
    place = jnp.stack([lax.axis_index("sec"), lax.axis_index("seq")]).astype(jnp.int32)

    def after(value, done):
        return lax.optimization_barrier((value, done))[0]

    def fetched(head, done=()):
        return fetch_cache(grid.n, after(meta, done), prompt_cache, 2 * HD, head)

    handed = lax.ppermute(carried, "sec", [(0, 1)])
    depth = query_weight.shape[1]
    hidden = hidden_rows if depth % HD else fetch([hidden_rows])[0]
    slices = split(grid, place, hidden, handed, depth)
    n = grid.n
    lane = lax.broadcasted_iota(jnp.int32, (1, n), 1)
    section, shard = after((lax.axis_index("sec"), lax.axis_index("seq")), handed)
    meta = jnp.concatenate([
        response_lengths, block_prompts[:, :, 0],
        jnp.pad(prompt_lengths, (0, n - prompt_lengths.shape[0]))[None],
        jnp.where(lane == 0, section, shard).astype(jnp.int32),
    ])
    weight, own = fetch([query_weight, after(response_cache, handed)])
    x = [slices[0]] + [None] * (grid.n - 1)
    for kz in reversed(range(grid.zs)):
        for kx in reversed(range(grid.xs)):
            k = kx * grid.zs + kz
            if k:
                x[k] = grid.swap(slices[k], kx, kz)
    part = project(grid, meta, x, weight, bl, share, chunks)
    part = [piece.reshape(grid.zs, share, part_cols) for piece in part]
    part = [part[c * grid.xs:(c + 1) * grid.xs] for c in range(chunks)]

    def narrow(value):
        return (value * 0.125).astype(jnp.float16)

    def widen(value):
        return value.astype(jnp.float32) * 8.0

    def both(first, second):
        return lax.optimization_barrier((first, second))

    def reduce_x(parts, done=()):
        got = [grid.swap(after(narrow(parts[kx]), done), kx, 0) for kx in range(1, grid.xs)]
        return functools.reduce(jnp.add, [parts[0]] + [widen(value) for value in got])

    def narrow_z(held):
        return [narrow(held[kz]) for kz in range(1, grid.zs)]

    def sum_z(held, sends, beside):
        got = [grid.swap(send, 0, kz + 1) for kz, send in enumerate(sends)]
        parts = [after(held[0], beside)] + [widen(value) for value in got]
        return functools.reduce(jnp.add, parts).astype(jnp.bfloat16)

    def gather_z(value):
        return [value] + [grid.swap(value, 0, kz) for kz in range(1, grid.zs)]

    def gather_x(value):
        return [value] + [grid.swap(value, kx, 0) for kx in range(1, grid.xs)]

    z_then_x = [[(kx, kz) for kz in range(grid.zs)] for kx in range(grid.xs)]
    x_then_z = [[(kx, kz) for kx in range(grid.xs)] for kz in range(grid.zs)]

    def call(c, kx, queries):
        return attend(
            grid, kx, meta, queries, x_then_z if c else z_then_x,
            caches[c * heads:(c + 1) * heads], bl, heads,
        )

    def call_far(c, queries):
        outs = [call(c, kx, queries)[0] for kx in range(1, grid.xs)]
        return outs, [grid.swap(out, kx + 1, 0) for kx, out in enumerate(outs)]

    def send_z(merged):
        return [merged[0]] + [grid.swap(merged[kz], 0, kz) for kz in range(1, grid.zs)]

    half = (local_kv + 1) // 4
    caches = [fetched(head) for head in range(half)]
    part[0][0] = after(part[0][0], caches)
    held = reduce_x(part[0])
    sends = narrow_z(held)
    if chunks > 1:
        sends, part[1][1] = both(sends, part[1][1])
        later = reduce_x(part[1])
    caches += [fetched(head, sends) for head in range(half, heads)]
    mine = sum_z(held, sends, caches)
    column = gather_z(mine)
    if chunks > 1:
        caches += [fetched(head, mine) for head in range(heads, heads + half)]
        sends = narrow_z(after(later, mine))
        column = after(column, (caches, sends))
    queries = gather_x(jnp.stack(column))
    if chunks == 1:
        outs, mets = call_far(0, queries)
        queries[0] = after(queries[0], outs)
        held, own_q = call(0, 0, queries)
        pieces = send_z(merge_column([held] + mets, heads * GR))
        pieces.append(attend_own(own_q, own, 0, heads))
        return finish(meta, [], pieces, heads)
    caches += [fetched(head, sends) for head in range(heads + half, local_kv)]
    mine = sum_z(later, sends, caches)
    queries[0] = after(queries[0], mine)
    near = jnp.stack(gather_x(mine))
    outs, mets = call_far(0, queries)
    near = after(near, outs)
    queries[0] = after(queries[0], near)
    later = gather_z(near)
    held, own_q = call(0, 0, queries)
    merged = merge_column([held] + mets, heads * GR)
    later[0] = after(later[0], merged)
    outs, mets = call_far(1, later)
    merged, later[0] = both(after(merged, outs), later[0])
    pieces = send_z(merged)
    held, later_q = call(1, 0, later)
    merged = merge_column([held] + mets, heads * GR)
    own_q, later_q = after((own_q, later_q), merged)
    done = finish(meta, [], pieces + [attend_own(own_q, own, 0, heads)], heads)
    pieces = send_z(merged) + [attend_own(later_q, own, heads, heads)]
    return finish(meta, [done], pieces, heads)


def solution(mesh):
    placed = (
        P("sec", "seq", None),
        P("sec", "seq", None),
        P("sec", "seq", "tp"),
        P("sec", "seq", "tp"),
        P("sec", None, "seq", "tp"),
        P(),
        P(),
        P(),
    )
    return jax.shard_map(
        shards, mesh=mesh, in_specs=placed, out_specs=P("sec", "seq", "tp"), check_vma=False
    )
```

```python
import functools
import math

import jax
import jax.numpy as jnp
from jax import lax
from jax.experimental import pallas as pl
from jax.experimental.pallas import tpu as pltpu
from jax.sharding import PartitionSpec as P

HD = 128
GR = 4
NEG = -1e30
LOG2E = 1.4426950408889634
CHUNK = 512
PIECE = 1024
ROUND = 32
EXTRA = 128
SLOT = 16
BIG = 2.0 ** 100
MIB = 1024 * 1024


def dot_nt(a, b):
    return lax.dot_general(a, b, (((1,), (1,)), ((), ())), preferred_element_type=jnp.float32)


class Grid:
    def __init__(self, count):
        self.n = count
        self.xs = 1 << ((count.bit_length() - 1) // 2)
        self.zs = count // self.xs

    def owner(self, shard, kx, kz):
        z, x = shard // self.xs, shard % self.xs
        return (z ^ kz) * self.xs + (x ^ kx)

    def swap(self, value, kx, kz):
        pairs = [(s, self.owner(s, kx, kz)) for s in range(self.n)]
        return lax.ppermute(value, "seq", pairs)


class Facts:
    def __init__(self, meta):
        self.meta = meta
        self.section, self.shard = meta[5, 0], meta[5, 1]

    def length(self, block):
        return self.meta[self.section, block]

    def prompt(self, block):
        return self.meta[2 + self.section, block]

    def prompt_length(self, prompt):
        return self.meta[4, prompt]


def split_kernel(grid, depth, meta, hidden_ref, handed_ref, *out_refs):
    for kx in range(grid.xs):
        for kz in range(grid.zs):
            at = pl.multiple_of(grid.owner(meta[1], kx, kz) * depth, HD)
            total = hidden_ref[0, :, pl.ds(at, depth)].astype(jnp.float32) + handed_ref[
                0, :, pl.ds(at, depth)
            ].astype(jnp.float32)
            out_refs[kx * grid.zs + kz][...] = total.astype(jnp.bfloat16)


def split(grid, meta, hidden, handed, depth):
    bl = hidden.shape[1]
    if depth % HD:
        total = (hidden[0].astype(jnp.float32) + handed[0].astype(jnp.float32)).astype(jnp.bfloat16)
        return [
            lax.dynamic_slice_in_dim(total, grid.owner(meta[1], kx, kz) * depth, depth, 1)
            for kx in range(grid.xs) for kz in range(grid.zs)
        ]
    whole = pl.BlockSpec(memory_space=pltpu.VMEM)
    return pl.pallas_call(
        functools.partial(split_kernel, grid, depth),
        grid_spec=pltpu.PrefetchScalarGridSpec(
            num_scalar_prefetch=1,
            grid=(1,),
            in_specs=[whole, whole],
            out_specs=[whole] * grid.n,
        ),
        out_shape=[jax.ShapeDtypeStruct((bl, depth), jnp.bfloat16)] * grid.n,
        compiler_params=pltpu.CompilerParams(vmem_limit_bytes=16 * MIB),
        name="split",
    )(meta, hidden, handed)


def run_moves(moves):
    for needed, move in moves:
        if needed is None:
            move.start()
        else:
            pl.when(needed)(move.start)
    for needed, move in moves:
        if needed is None:
            move.wait()
        else:
            pl.when(needed)(move.wait)


def fetch_kernel(*refs):
    count = len(refs) // 2
    run_moves([
        (None, pltpu.make_async_copy(refs[i], refs[count + i], refs[-1].at[i]))
        for i in range(count)
    ])


def fetch(arrays):
    anywhere, near = pl.BlockSpec(memory_space=pltpu.HBM), pl.BlockSpec(memory_space=pltpu.VMEM)
    size = sum(math.prod(array.shape) for array in arrays)
    out = pl.pallas_call(
        fetch_kernel,
        in_specs=[anywhere] * len(arrays),
        out_specs=[near] * len(arrays),
        scratch_shapes=[pltpu.SemaphoreType.DMA((len(arrays),))],
        out_shape=[pltpu.VMEM(array.shape, array.dtype) for array in arrays],
        compiler_params=pltpu.CompilerParams(vmem_limit_bytes=4 * MIB),
        cost_estimate=pl.CostEstimate(flops=0, bytes_accessed=2 * size, transcendentals=0),
        name="fetch",
    )(*[pltpu.with_memory_space_constraint(array, pltpu.HBM) for array in arrays])
    return [pltpu.with_memory_space_constraint(array, pltpu.VMEM) for array in out]


def fetch_cache_kernel(n, chunk, width, first, meta, cache_ref, kv_ref, sem):
    count, tile_len = kv_ref.shape[:2]
    facts = Facts(meta)
    moves = []
    for p in range(count):
        asked = facts.prompt(0) == p
        for b in range(1, n):
            asked = asked | (facts.prompt(b) == p)
        for c in range(tile_len // chunk):
            at = pl.ds(c * chunk, chunk)
            needed = asked & (facts.prompt_length(p) > facts.shard * tile_len + c * chunk)
            moves.append((needed, pltpu.make_async_copy(
                cache_ref.at[0, p, at, pl.ds(first * width, width)], kv_ref.at[p, at],
                sem.at[p, c],
            )))
    run_moves(moves)


def fetch_cache(n, meta, cache, width, first):
    count, tile_len = cache.shape[1:3]
    chunk = min(PIECE, tile_len)
    shape = (count, tile_len, width)
    out = pl.pallas_call(
        functools.partial(fetch_cache_kernel, n, chunk, width, first),
        grid_spec=pltpu.PrefetchScalarGridSpec(
            num_scalar_prefetch=1,
            grid=(1,),
            in_specs=[pl.BlockSpec(memory_space=pltpu.HBM)],
            out_specs=pl.BlockSpec(memory_space=pltpu.VMEM),
            scratch_shapes=[pltpu.SemaphoreType.DMA((count, tile_len // chunk))],
        ),
        out_shape=pltpu.VMEM(shape, cache.dtype),
        compiler_params=pltpu.CompilerParams(vmem_limit_bytes=4 * MIB),
        cost_estimate=pl.CostEstimate(
            flops=0, bytes_accessed=2 * math.prod(shape), transcendentals=0
        ),
        name="fetch_cache",
    )(meta, pltpu.with_memory_space_constraint(cache, pltpu.HBM))
    return pltpu.with_memory_space_constraint(out, pltpu.VMEM)


def project_kernel(grid, bl, share, meta, *refs):
    x_refs, w_ref, refs = refs[:grid.n], refs[grid.n], refs[grid.n + 1:]
    out_refs, (xp_ref, starts) = refs[:-2], refs[-2:]

    facts = Facts(meta)
    shard = facts.shard
    offset = jnp.int32(0)
    for b in range(grid.n):
        starts[b] = offset
        offset = offset + facts.length(b)
    lane = lax.broadcasted_iota(jnp.int32, (8, grid.n * bl), 1)
    target = jnp.full(lane.shape, -1, jnp.int32)
    owners = [
        grid.owner(shard, kx, kz) for kx in range(grid.xs) for kz in range(grid.zs)
    ]
    for k, b in enumerate(owners):
        order = lane - k * bl
        used = (order >= 0) & (order < facts.length(b))
        target = jnp.where(used, order + starts[b], target)
    row = lax.broadcasted_iota(jnp.int32, (share, grid.n * bl), 0)
    target = jnp.broadcast_to(target[:1], row.shape)
    picks = [jnp.where(row + b * share == target, 1.0, 0.0) for b in owners]
    pick = jnp.concatenate(picks, axis=0).astype(jnp.bfloat16)
    x = jnp.concatenate([ref[...] for ref in x_refs], axis=0)
    chosen = jnp.dot(pick, x, preferred_element_type=jnp.float32)
    xp_ref[...] = chosen.astype(jnp.bfloat16)

    rows = grid.zs * share
    tile = out_refs[0].shape[1]
    for i, out_ref in enumerate(out_refs):
        chunk, kx = i // grid.xs, i % grid.xs
        out_ref[...] = jnp.dot(
            xp_ref[kx * rows:(kx + 1) * rows], w_ref[0, :, chunk * tile:(chunk + 1) * tile],
            preferred_element_type=jnp.float32,
        )


def project(grid, meta, xs, w, bl, share, chunks):
    k, cols = w.shape[1:]
    rows = grid.n * share
    tile = cols // chunks
    piece = (grid.zs * share, tile)
    whole = pl.BlockSpec(memory_space=pltpu.VMEM)
    return pl.pallas_call(
        functools.partial(project_kernel, grid, bl, share),
        grid_spec=pltpu.PrefetchScalarGridSpec(
            num_scalar_prefetch=1,
            grid=(1,),
            in_specs=[whole] * (grid.n + 1),
            out_specs=[whole] * (chunks * grid.xs),
            scratch_shapes=[
                pltpu.VMEM((rows, k), jnp.bfloat16), pltpu.SMEM((grid.n,), jnp.int32)
            ],
        ),
        out_shape=[jax.ShapeDtypeStruct(piece, jnp.float32)] * (chunks * grid.xs),
        compiler_params=pltpu.CompilerParams(vmem_limit_bytes=20 * MIB),
        cost_estimate=pl.CostEstimate(
            flops=2 * rows * k * cols, bytes_accessed=2 * k * cols + 4 * rows * cols,
            transcendentals=0,
        ),
        name="project",
    )(meta, *xs, w)


def three_terms(value):
    high = value.astype(jnp.bfloat16).astype(jnp.float32)
    mid = (value - high).astype(jnp.bfloat16).astype(jnp.float32)
    return [high, mid, value - high - mid]


def encode(peak, total):
    lane = lax.broadcasted_iota(jnp.int32, peak.shape, 1)
    out = jnp.zeros(peak.shape, jnp.float32)
    for i, term in enumerate(three_terms(peak) + three_terms(total)):
        term = jnp.where(lane < SLOT, term, 0.0)
        out = out + (pltpu.roll(term, i * SLOT, 1) if i else term)
    return out.astype(jnp.bfloat16)


def decode(tile):
    terms = tile.astype(jnp.float32)
    parts = [terms] + [pltpu.roll(terms, EXTRA - i * SLOT, 1) for i in range(1, 6)]
    return parts[0] + parts[1] + parts[2], parts[3] + parts[4] + parts[5]


def merge(refs, heads):
    width = heads * HD
    peaks, totals = zip(*[decode(ref[:, width:]) for ref in refs])
    rows = peaks[0].shape[0]
    peak = functools.reduce(jnp.maximum, peaks)
    weights = [jnp.exp2(one - peak) for one in peaks]
    total = functools.reduce(jnp.add, [w * one for w, one in zip(weights, totals)])
    out = []
    for h in range(heads):
        terms = [
            jnp.broadcast_to(weight[:, h:h + 1], (rows, HD))
            * ref[:, h * HD:(h + 1) * HD].astype(jnp.float32)
            for weight, ref in zip(weights, refs)
        ]
        out.append(functools.reduce(jnp.add, terms))
    return out, peak, total


def merge_kernel(zs, heads, *refs):
    sources, outs = refs[:-zs], refs[-zs:]
    for kz in range(zs):
        parts, peak, total = merge([ref.at[kz] for ref in sources], heads)
        for h in range(heads):
            outs[kz][:, h * HD:(h + 1) * HD] = parts[h].astype(jnp.bfloat16)
        outs[kz][:, heads * HD:] = encode(peak, total)


def merge_column(sources, heads):
    zs, bl, width = sources[0].shape
    return pl.pallas_call(
        functools.partial(merge_kernel, zs, heads),
        out_shape=[jax.ShapeDtypeStruct((bl, width), jnp.bfloat16)] * zs,
        compiler_params=pltpu.CompilerParams(vmem_limit_bytes=16 * MIB),
        name="merge",
    )(*sources)


def attend_kernel(grid, kx, bl, share, heads, tile_len, coords, meta, *refs):
    q_refs, refs = refs[:len(coords)], refs[len(coords):]
    kv_refs, refs = refs[:heads], refs[heads:]
    out_ref, own_q_ref = refs[0], refs[1] if kx == 0 else None
    q32_ref, acc_ref, m_ref, over_ref = refs[-4:]
    facts = Facts(meta)
    shard = facts.shard
    rows = grid.n * share
    for q_ref, places in zip(q_refs, coords):
        for i, (fx, fz) in enumerate(places):
            at = pl.multiple_of(grid.owner(shard, fx, fz) * share, 8)
            q32_ref[pl.ds(at, share), :] = q_ref[i].astype(jnp.float32)
    q32_ref[rows:, :] = jnp.zeros((bl + 8, q32_ref.shape[1]), jnp.float32)

    def one(kz, carry):
        attend_block(
            grid, kx, bl, heads, tile_len, kz, facts,
            kv_refs, out_ref, own_q_ref, q32_ref, acc_ref, m_ref, over_ref,
        )
        return carry

    lax.fori_loop(0, grid.zs, one, 0)


def group_rows(queries, g, used):
    return jnp.concatenate(
        [queries[:used, (g * GR + r) * HD:(g * GR + r + 1) * HD] for r in range(GR)], axis=0
    )


def sums(p, v):
    v = jnp.concatenate([v, jnp.ones(v.shape, jnp.bfloat16)], axis=1)
    return jnp.dot(p, v, preferred_element_type=jnp.float32)


def write_partial(accs, peaks, store, c2):
    used = accs[0].shape[0] // GR
    lane = lax.broadcasted_iota(jnp.int32, (used, EXTRA), 1)
    total = jnp.zeros((used, EXTRA), jnp.float32)
    peak = jnp.zeros((used, EXTRA), jnp.float32)
    for g, (acc, m) in enumerate(zip(accs, peaks)):
        for r in range(GR):
            h = g * GR + r
            at = slice(r * used, (r + 1) * used)
            store(slice(h * HD, (h + 1) * HD), acc[at, :HD].astype(jnp.bfloat16))
            total = jnp.where(lane == h, acc[at, HD:], total)
            peak = jnp.where(lane == h, m[at], peak)
    width = len(accs) * GR * HD
    store(slice(width, width + EXTRA), encode(peak * c2, total))
    return total


def attend_block(grid, kx, bl, heads, tile_len, step, facts,
                 kv_refs, out_ref, own_q_ref, q32_ref, acc_ref, m_ref, over_ref):
    block = grid.owner(facts.shard, kx, step)
    offset = jnp.int32(0)
    for b in range(grid.n):
        offset = offset + jnp.where(b < block, facts.length(b), 0)
    prompt = facts.prompt(block)
    valid = jnp.clip(facts.prompt_length(prompt) - facts.shard * tile_len, 0, tile_len)
    c2 = LOG2E / math.sqrt(HD)
    chunk = min(CHUNK, tile_len)
    width = heads * GR * HD

    rest = offset % 8
    window = q32_ref[pl.ds(pl.multiple_of(offset - rest, 8), bl + 8), :]
    window = pltpu.roll(window, jnp.where(rest == 0, 0, bl + 8 - rest), 0)
    queries = window[:bl].astype(jnp.bfloat16)

    group = functools.partial(group_rows, queries)
    if kx == 0:
        @pl.when(step == 0)
        def _():
            own_q_ref[...] = queries

    def keys(g, at, size):
        return kv_refs[g][prompt, pl.ds(at, size), :HD]

    def vals(g, at, size):
        return kv_refs[g][prompt, pl.ds(at, size), HD:]

    def store(used, columns, value):
        out_ref[step, :used, columns] = value

    def update(g, s, seen, v):
        s = jnp.where(seen, s, NEG)
        before = m_ref[g][:, :1]
        m = jnp.maximum(before, jnp.max(s, axis=1, keepdims=True))
        p = jnp.where(seen, jnp.exp2((s - m) * c2), 0.0).astype(jnp.bfloat16)
        acc_ref[g] = acc_ref[g] * jnp.exp2((before - m) * c2) + sums(p, v)
        m_ref[g] = jnp.broadcast_to(m, m_ref.shape[1:])

    def exact():
        acc_ref[...] = jnp.zeros_like(acc_ref)
        m_ref[...] = jnp.full_like(m_ref, NEG)

        def one(c, carry):
            at = pl.multiple_of(c * chunk, chunk)
            for g in range(heads):
                s = dot_nt(group(g, bl), keys(g, at, chunk))
                here = lax.broadcasted_iota(jnp.int32, s.shape, 1) + at
                update(g, s, here < valid, vals(g, at, chunk))
            return carry

        lax.fori_loop(0, (valid + chunk - 1) // chunk, one, 0)
        write_partial(
            [acc_ref[g] for g in range(heads)], [m_ref[g] for g in range(heads)],
            functools.partial(store, bl), c2,
        )

    length = facts.length(block)

    @pl.when(valid == 0)
    def _():
        over_ref[0] = 0
        out_ref[step, :, :width] = jnp.zeros((bl, width), jnp.bfloat16)
        none = jnp.zeros((bl, EXTRA), jnp.float32)
        out_ref[step, :, width:] = encode(none + NEG, none)

    step_of = min(PIECE, tile_len) // chunk

    def single_pass(used, count):
        items = [(g, c) for c in range(count) for g in range(heads)]
        q = [group(g, used) for g in range(heads)]
        peaks = [None] * heads
        accs = [None] * heads
        ahead = dot_nt(q[0], keys(0, 0, chunk))
        for i, (g, c) in enumerate(items):
            s = ahead
            if i + 1 < len(items):
                ng, nc = items[i + 1]
                ahead = dot_nt(q[ng], keys(ng, nc * chunk, chunk))
            if (c + 1) * chunk > (count - step_of) * chunk:
                here = lax.broadcasted_iota(jnp.int32, s.shape, 1) + c * chunk
                s = jnp.where(here < valid, s, NEG)
            if c == 0:
                peaks[g] = jnp.max(s, axis=1, keepdims=True)
            p = jnp.exp2((s - peaks[g]) * c2).astype(jnp.bfloat16)
            part = sums(p, vals(g, c * chunk, chunk))
            accs[g] = part if c == 0 else accs[g] + part
        total = write_partial(
            accs, [jnp.broadcast_to(m, (GR * used, EXTRA)) for m in peaks],
            functools.partial(store, used), c2,
        )

        over_ref[0] = (jnp.max(jnp.where(total < BIG, 0.0, 1.0)) > 0.5).astype(jnp.int32)

    for count in range(step_of, tile_len // chunk + 1, step_of):
        for used in range(ROUND, bl + 1, ROUND):
            some_keys = (valid > (count - step_of) * chunk) & (valid <= count * chunk)
            some_rows = (length > used - ROUND) & (length <= used)
            pl.when(some_keys & some_rows)(functools.partial(single_pass, used, count))

    pl.when(over_ref[0] > 0)(exact)


def own_kernel(first, heads, bl, q_ref, own_ref, out_ref):
    c2 = LOG2E / math.sqrt(HD)
    queries = q_ref[...]
    accs, peaks = [], []
    for g in range(heads):
        base = (first + g) * 2 * HD
        s = dot_nt(group_rows(queries, g, bl), own_ref[0, :, base:base + HD])
        row = lax.broadcasted_iota(jnp.int32, s.shape, 0) % bl
        seen = lax.broadcasted_iota(jnp.int32, s.shape, 1) <= row
        s = jnp.where(seen, s, NEG)
        m = jnp.max(s, axis=1, keepdims=True)
        p = jnp.where(seen, jnp.exp2((s - m) * c2), 0.0).astype(jnp.bfloat16)
        accs.append(sums(p, own_ref[0, :, base + HD:base + 2 * HD]))
        peaks.append(jnp.broadcast_to(m, (GR * bl, EXTRA)))

    def store(columns, value):
        out_ref[:, columns] = value

    write_partial(accs, peaks, store, c2)


def attend_own(queries, own, first, heads):
    bl = own.shape[1]
    return pl.pallas_call(
        functools.partial(own_kernel, first, heads, bl),
        out_shape=jax.ShapeDtypeStruct((bl, heads * GR * HD + EXTRA), jnp.bfloat16),
        compiler_params=pltpu.CompilerParams(vmem_limit_bytes=16 * MIB),
        name="attend_own",
    )(queries, own)


def attend(grid, kx, meta, queries, coords, caches, bl, heads):
    zs = grid.zs
    _, share, cols = queries[0].shape
    tile_len = caches[0].shape[1]
    width = heads * GR * HD + EXTRA
    whole = pl.BlockSpec(memory_space=pltpu.VMEM)
    shapes = [(zs, bl, width)] + [(bl, cols)] * (kx == 0)
    outs = [jax.ShapeDtypeStruct(shape, jnp.bfloat16) for shape in shapes]
    return pl.pallas_call(
        functools.partial(attend_kernel, grid, kx, bl, share, heads, tile_len, coords),
        grid_spec=pltpu.PrefetchScalarGridSpec(
            num_scalar_prefetch=1,
            grid=(1,),
            in_specs=[whole] * (len(queries) + heads),
            out_specs=[whole] * len(outs),
            scratch_shapes=[
                pltpu.VMEM((grid.n * share + bl + 8, cols), jnp.float32),
                pltpu.VMEM((heads, GR * bl, 2 * HD), jnp.float32),
                pltpu.VMEM((heads, GR * bl, HD), jnp.float32),
                pltpu.SMEM((1,), jnp.int32),
            ],
        ),
        out_shape=outs,
        compiler_params=pltpu.CompilerParams(vmem_limit_bytes=20 * MIB),
        cost_estimate=pl.CostEstimate(
            flops=8 * zs * bl * cols * tile_len,
            bytes_accessed=2 * zs * tile_len * heads * 2 * HD,
            transcendentals=zs * bl * heads * GR * tile_len,
        ),
        name="attend",
    )(meta, *queries, *caches)


def finish_kernel(heads, bl, done, meta, *refs):
    sources, out_ref = refs[:-1], refs[-1]
    pieces = sources[done:]
    facts = Facts(meta)
    length = facts.length(facts.shard)
    row = lax.broadcasted_iota(jnp.int32, (bl, HD), 0)
    width = heads * GR * HD
    for c in range(done):
        out_ref[0, :, c * width:(c + 1) * width] = sources[c][0]
    parts, _, total = merge(pieces, heads * GR)
    for h in range(heads * GR):
        at = done * width + h * HD
        value = parts[h] / jnp.broadcast_to(total[:, h:h + 1], (bl, HD))
        out_ref[0, :, at:at + HD] = jnp.where(row < length, value, 0.0).astype(jnp.bfloat16)


def finish(meta, done, pieces, heads):
    bl = pieces[0].shape[0]
    whole = pl.BlockSpec(memory_space=pltpu.VMEM)
    sources = list(done) + list(pieces)
    return pl.pallas_call(
        functools.partial(finish_kernel, heads, bl, len(done)),
        grid_spec=pltpu.PrefetchScalarGridSpec(
            num_scalar_prefetch=1,
            grid=(1,),
            in_specs=[whole] * len(sources),
            out_specs=whole,
        ),
        out_shape=jax.ShapeDtypeStruct((1, bl, (len(done) + 1) * heads * GR * HD), jnp.bfloat16),
        compiler_params=pltpu.CompilerParams(vmem_limit_bytes=16 * MIB),
        name="finish",
    )(meta, *sources)


def shards(
    hidden_rows,
    carried,
    query_weight,
    response_cache,
    prompt_cache,
    prompt_lengths,
    response_lengths,
    block_prompts,
):
    grid = Grid(lax.axis_size("seq"))
    bl = hidden_rows.shape[1]
    local_kv = response_cache.shape[2] // (2 * HD)
    share = bl * 5 // 8
    chunks = 2 if local_kv % 2 == 0 else 1
    heads = local_kv // chunks
    part_cols = heads * GR * HD
    place = jnp.stack([lax.axis_index("sec"), lax.axis_index("seq")]).astype(jnp.int32)

    def after(value, done):
        return lax.optimization_barrier((value, done))[0]

    def fetched(head, done=()):
        return fetch_cache(grid.n, after(meta, done), prompt_cache, 2 * HD, head)

    handed = lax.ppermute(carried, "sec", [(0, 1)])
    depth = query_weight.shape[1]
    hidden = hidden_rows if depth % HD else fetch([hidden_rows])[0]
    slices = split(grid, place, hidden, handed, depth)
    weight, own = fetch([query_weight, after(response_cache, handed)])
    x = [slices[0]] + [None] * (grid.n - 1)
    order = sorted(range(1, grid.n), key=lambda k: (k % grid.zs, k), reverse=True)
    for k in order:
        x[k] = grid.swap(slices[k], k // grid.zs, k % grid.zs)
    n = grid.n
    lane = lax.broadcasted_iota(jnp.int32, (1, n), 1)
    section, shard = after((lax.axis_index("sec"), lax.axis_index("seq")), x[order[2]])
    meta = jnp.concatenate([
        response_lengths, block_prompts[:, :, 0],
        jnp.pad(prompt_lengths, (0, n - prompt_lengths.shape[0]))[None],
        jnp.where(lane == 0, section, shard).astype(jnp.int32),
    ])
    half = (local_kv + 1) // 4
    caches = [fetched(head) for head in range(half)]
    x[0] = after(x[0], caches)
    part = project(grid, meta, x, weight, bl, share, chunks)
    part = [piece.reshape(grid.zs, share, part_cols) for piece in part]
    part = [part[c * grid.xs:(c + 1) * grid.xs] for c in range(chunks)]

    def narrow(value):
        return (value * 0.125).astype(jnp.float16)

    def widen(value):
        return value.astype(jnp.float32) * 8.0

    def both(first, second):
        return lax.optimization_barrier((first, second))

    def reduce_x(parts, done=()):
        got = [grid.swap(after(narrow(parts[kx]), done), kx, 0) for kx in range(1, grid.xs)]
        return functools.reduce(jnp.add, [parts[0]] + [widen(value) for value in got])

    def narrow_z(held):
        return [narrow(held[kz]) for kz in range(1, grid.zs)]

    def sum_z(held, sends, beside):
        got = [grid.swap(send, 0, kz + 1) for kz, send in enumerate(sends)]
        parts = [after(held[0], beside)] + [widen(value) for value in got]
        return functools.reduce(jnp.add, parts).astype(jnp.bfloat16)

    def gather_z(value):
        return [value] + [grid.swap(value, 0, kz) for kz in range(1, grid.zs)]

    def gather_x(value):
        return [value] + [grid.swap(value, kx, 0) for kx in range(1, grid.xs)]

    z_then_x = [[(kx, kz) for kz in range(grid.zs)] for kx in range(grid.xs)]
    x_then_z = [[(kx, kz) for kx in range(grid.xs)] for kz in range(grid.zs)]

    def call(c, kx, queries):
        return attend(
            grid, kx, meta, queries, x_then_z if c else z_then_x,
            caches[c * heads:(c + 1) * heads], bl, heads,
        )

    def call_far(c, queries):
        outs = [call(c, kx, queries)[0] for kx in range(1, grid.xs)]
        return outs, [grid.swap(out, kx + 1, 0) for kx, out in enumerate(outs)]

    def send_z(merged):
        return [merged[0]] + [grid.swap(merged[kz], 0, kz) for kz in range(1, grid.zs)]

    caches += [fetched(head, part[0][-1]) for head in range(half, min(heads + half, local_kv))]
    part[0][0] = after(part[0][0], caches)
    held = reduce_x(part[0])
    sends = narrow_z(held)
    if chunks > 1:
        sends, part[1][1] = both(sends, part[1][1])
        later = reduce_x(part[1])
    mine = sum_z(held, sends, ())
    column = gather_z(mine)
    if chunks > 1:
        sends = narrow_z(after(later, mine))
        column = after(column, sends)
    queries = gather_x(jnp.stack(column))
    if chunks == 1:
        outs, mets = call_far(0, queries)
        queries[0] = after(queries[0], outs)
        held, own_q = call(0, 0, queries)
        pieces = send_z(merge_column([held] + mets, heads * GR))
        pieces.append(attend_own(own_q, own, 0, heads))
        return finish(meta, [], pieces, heads)
    caches += [fetched(head, sends) for head in range(heads + half, local_kv)]
    mine = sum_z(later, sends, caches)
    queries[0] = after(queries[0], mine)
    near = jnp.stack(gather_x(mine))
    outs, mets = call_far(0, queries)
    near = after(near, outs)
    queries[0] = after(queries[0], near)
    later = gather_z(near)
    held, own_q = call(0, 0, queries)
    merged = merge_column([held] + mets, heads * GR)
    later[0] = after(later[0], merged)
    outs, mets = call_far(1, later)
    merged, later[0] = both(after(merged, outs), later[0])
    pieces = send_z(merged)
    held, later_q = call(1, 0, later)
    merged = merge_column([held] + mets, heads * GR)
    own_q, later_q = after((own_q, later_q), merged)
    done = finish(meta, [], pieces + [attend_own(own_q, own, 0, heads)], heads)
    pieces = send_z(merged) + [attend_own(later_q, own, heads, heads)]
    return finish(meta, [done], pieces, heads)


def solution(mesh):
    placed = (
        P("sec", "seq", None),
        P("sec", "seq", None),
        P("sec", "seq", "tp"),
        P("sec", "seq", "tp"),
        P("sec", None, "seq", "tp"),
        P(),
        P(),
        P(),
    )
    return jax.shard_map(
        shards, mesh=mesh, in_specs=placed, out_specs=P("sec", "seq", "tp"), check_vma=False
    )
```

```python
import functools
import math

import jax
import jax.numpy as jnp
from jax import lax
from jax.experimental import pallas as pl
from jax.experimental.pallas import tpu as pltpu
from jax.sharding import PartitionSpec as P

HD = 128
GR = 4
NEG = -1e30
LOG2E = 1.4426950408889634
CHUNK = 512
PIECE = 1024
ROUND = 32
EXTRA = 128
SLOT = 16
BIG = 2.0 ** 100
MIB = 1024 * 1024


def dot_nt(a, b):
    return lax.dot_general(a, b, (((1,), (1,)), ((), ())), preferred_element_type=jnp.float32)


class Grid:
    def __init__(self, count):
        self.n = count
        self.xs = 1 << ((count.bit_length() - 1) // 2)
        self.zs = count // self.xs

    def owner(self, shard, kx, kz):
        z, x = shard // self.xs, shard % self.xs
        return (z ^ kz) * self.xs + (x ^ kx)

    def swap(self, value, kx, kz):
        pairs = [(s, self.owner(s, kx, kz)) for s in range(self.n)]
        return lax.ppermute(value, "seq", pairs)


class Facts:
    def __init__(self, meta):
        self.meta = meta
        self.section, self.shard = meta[5, 0], meta[5, 1]

    def length(self, block):
        return self.meta[self.section, block]

    def prompt(self, block):
        return self.meta[2 + self.section, block]

    def prompt_length(self, prompt):
        return self.meta[4, prompt]


def split_kernel(grid, depth, meta, hidden_ref, handed_ref, *out_refs):
    for kx in range(grid.xs):
        for kz in range(grid.zs):
            at = pl.multiple_of(grid.owner(meta[1], kx, kz) * depth, HD)
            total = hidden_ref[0, :, pl.ds(at, depth)].astype(jnp.float32) + handed_ref[
                0, :, pl.ds(at, depth)
            ].astype(jnp.float32)
            out_refs[kx * grid.zs + kz][...] = total.astype(jnp.bfloat16)


def split(grid, meta, hidden, handed, depth):
    bl = hidden.shape[1]
    if depth % HD:
        total = (hidden[0].astype(jnp.float32) + handed[0].astype(jnp.float32)).astype(jnp.bfloat16)
        return [
            lax.dynamic_slice_in_dim(total, grid.owner(meta[1], kx, kz) * depth, depth, 1)
            for kx in range(grid.xs) for kz in range(grid.zs)
        ]
    whole = pl.BlockSpec(memory_space=pltpu.VMEM)
    return pl.pallas_call(
        functools.partial(split_kernel, grid, depth),
        grid_spec=pltpu.PrefetchScalarGridSpec(
            num_scalar_prefetch=1,
            grid=(1,),
            in_specs=[whole, whole],
            out_specs=[whole] * grid.n,
        ),
        out_shape=[jax.ShapeDtypeStruct((bl, depth), jnp.bfloat16)] * grid.n,
        compiler_params=pltpu.CompilerParams(vmem_limit_bytes=16 * MIB),
        name="split",
    )(meta, hidden, handed)


def run_moves(moves):
    for needed, move in moves:
        if needed is None:
            move.start()
        else:
            pl.when(needed)(move.start)
    for needed, move in moves:
        if needed is None:
            move.wait()
        else:
            pl.when(needed)(move.wait)


def fetch_kernel(*refs):
    count = len(refs) // 2
    run_moves([
        (None, pltpu.make_async_copy(refs[i], refs[count + i], refs[-1].at[i]))
        for i in range(count)
    ])


def fetch(arrays):
    anywhere, near = pl.BlockSpec(memory_space=pltpu.HBM), pl.BlockSpec(memory_space=pltpu.VMEM)
    size = sum(math.prod(array.shape) for array in arrays)
    out = pl.pallas_call(
        fetch_kernel,
        in_specs=[anywhere] * len(arrays),
        out_specs=[near] * len(arrays),
        scratch_shapes=[pltpu.SemaphoreType.DMA((len(arrays),))],
        out_shape=[pltpu.VMEM(array.shape, array.dtype) for array in arrays],
        compiler_params=pltpu.CompilerParams(vmem_limit_bytes=4 * MIB),
        cost_estimate=pl.CostEstimate(flops=0, bytes_accessed=2 * size, transcendentals=0),
        name="fetch",
    )(*[pltpu.with_memory_space_constraint(array, pltpu.HBM) for array in arrays])
    return [pltpu.with_memory_space_constraint(array, pltpu.VMEM) for array in out]


def fetch_cache_kernel(n, chunk, width, first, meta, cache_ref, kv_ref, sem):
    count, tile_len = kv_ref.shape[:2]
    facts = Facts(meta)
    moves = []
    for p in range(count):
        asked = facts.prompt(0) == p
        for b in range(1, n):
            asked = asked | (facts.prompt(b) == p)
        for c in range(tile_len // chunk):
            at = pl.ds(c * chunk, chunk)
            needed = asked & (facts.prompt_length(p) > facts.shard * tile_len + c * chunk)
            moves.append((needed, pltpu.make_async_copy(
                cache_ref.at[0, p, at, pl.ds(first * width, width)], kv_ref.at[p, at],
                sem.at[p, c],
            )))
    run_moves(moves)


def fetch_cache(n, meta, cache, width, first):
    count, tile_len = cache.shape[1:3]
    chunk = min(PIECE, tile_len)
    shape = (count, tile_len, width)
    out = pl.pallas_call(
        functools.partial(fetch_cache_kernel, n, chunk, width, first),
        grid_spec=pltpu.PrefetchScalarGridSpec(
            num_scalar_prefetch=1,
            grid=(1,),
            in_specs=[pl.BlockSpec(memory_space=pltpu.HBM)],
            out_specs=pl.BlockSpec(memory_space=pltpu.VMEM),
            scratch_shapes=[pltpu.SemaphoreType.DMA((count, tile_len // chunk))],
        ),
        out_shape=pltpu.VMEM(shape, cache.dtype),
        compiler_params=pltpu.CompilerParams(vmem_limit_bytes=4 * MIB),
        cost_estimate=pl.CostEstimate(
            flops=0, bytes_accessed=2 * math.prod(shape), transcendentals=0
        ),
        name="fetch_cache",
    )(meta, pltpu.with_memory_space_constraint(cache, pltpu.HBM))
    return pltpu.with_memory_space_constraint(out, pltpu.VMEM)


def project_kernel(grid, bl, share, meta, *refs):
    x_refs, w_ref, refs = refs[:grid.n], refs[grid.n], refs[grid.n + 1:]
    out_refs, (xp_ref, starts) = refs[:-2], refs[-2:]

    facts = Facts(meta)
    shard = facts.shard
    offset = jnp.int32(0)
    for b in range(grid.n):
        starts[b] = offset
        offset = offset + facts.length(b)
    lane = lax.broadcasted_iota(jnp.int32, (8, grid.n * bl), 1)
    target = jnp.full(lane.shape, -1, jnp.int32)
    owners = [
        grid.owner(shard, kx, kz) for kx in range(grid.xs) for kz in range(grid.zs)
    ]
    for k, b in enumerate(owners):
        order = lane - k * bl
        used = (order >= 0) & (order < facts.length(b))
        target = jnp.where(used, order + starts[b], target)
    row = lax.broadcasted_iota(jnp.int32, (share, grid.n * bl), 0)
    target = jnp.broadcast_to(target[:1], row.shape)
    picks = [jnp.where(row + b * share == target, 1.0, 0.0) for b in owners]
    pick = jnp.concatenate(picks, axis=0).astype(jnp.bfloat16)
    x = jnp.concatenate([ref[...] for ref in x_refs], axis=0)
    chosen = jnp.dot(pick, x, preferred_element_type=jnp.float32)
    xp_ref[...] = chosen.astype(jnp.bfloat16)

    rows = grid.zs * share
    tile = out_refs[0].shape[1]
    for i, out_ref in enumerate(out_refs):
        chunk, kx = i // grid.xs, i % grid.xs
        out_ref[...] = jnp.dot(
            xp_ref[kx * rows:(kx + 1) * rows], w_ref[0, :, chunk * tile:(chunk + 1) * tile],
            preferred_element_type=jnp.float32,
        )


def project(grid, meta, xs, w, bl, share, chunks):
    k, cols = w.shape[1:]
    rows = grid.n * share
    tile = cols // chunks
    piece = (grid.zs * share, tile)
    whole = pl.BlockSpec(memory_space=pltpu.VMEM)
    return pl.pallas_call(
        functools.partial(project_kernel, grid, bl, share),
        grid_spec=pltpu.PrefetchScalarGridSpec(
            num_scalar_prefetch=1,
            grid=(1,),
            in_specs=[whole] * (grid.n + 1),
            out_specs=[whole] * (chunks * grid.xs),
            scratch_shapes=[
                pltpu.VMEM((rows, k), jnp.bfloat16), pltpu.SMEM((grid.n,), jnp.int32)
            ],
        ),
        out_shape=[jax.ShapeDtypeStruct(piece, jnp.float32)] * (chunks * grid.xs),
        compiler_params=pltpu.CompilerParams(vmem_limit_bytes=20 * MIB),
        cost_estimate=pl.CostEstimate(
            flops=2 * rows * k * cols, bytes_accessed=2 * k * cols + 4 * rows * cols,
            transcendentals=0,
        ),
        name="project",
    )(meta, *xs, w)


def three_terms(value):
    high = value.astype(jnp.bfloat16).astype(jnp.float32)
    mid = (value - high).astype(jnp.bfloat16).astype(jnp.float32)
    return [high, mid, value - high - mid]


def encode(peak, total):
    lane = lax.broadcasted_iota(jnp.int32, peak.shape, 1)
    out = jnp.zeros(peak.shape, jnp.float32)
    for i, term in enumerate(three_terms(peak) + three_terms(total)):
        term = jnp.where(lane < SLOT, term, 0.0)
        out = out + (pltpu.roll(term, i * SLOT, 1) if i else term)
    return out.astype(jnp.bfloat16)


def decode(tile):
    terms = tile.astype(jnp.float32)
    parts = [terms] + [pltpu.roll(terms, EXTRA - i * SLOT, 1) for i in range(1, 6)]
    return parts[0] + parts[1] + parts[2], parts[3] + parts[4] + parts[5]


def merge(refs, heads):
    width = heads * HD
    peaks, totals = zip(*[decode(ref[:, width:]) for ref in refs])
    rows = peaks[0].shape[0]
    peak = functools.reduce(jnp.maximum, peaks)
    weights = [jnp.exp2(one - peak) for one in peaks]
    total = functools.reduce(jnp.add, [w * one for w, one in zip(weights, totals)])
    out = []
    for h in range(heads):
        terms = [
            jnp.broadcast_to(weight[:, h:h + 1], (rows, HD))
            * ref[:, h * HD:(h + 1) * HD].astype(jnp.float32)
            for weight, ref in zip(weights, refs)
        ]
        out.append(functools.reduce(jnp.add, terms))
    return out, peak, total


def merge_kernel(zs, heads, *refs):
    sources, outs = refs[:-zs], refs[-zs:]
    for kz in range(zs):
        parts, peak, total = merge([ref.at[kz] for ref in sources], heads)
        for h in range(heads):
            outs[kz][:, h * HD:(h + 1) * HD] = parts[h].astype(jnp.bfloat16)
        outs[kz][:, heads * HD:] = encode(peak, total)


def merge_column(sources, heads):
    zs, bl, width = sources[0].shape
    return pl.pallas_call(
        functools.partial(merge_kernel, zs, heads),
        out_shape=[jax.ShapeDtypeStruct((bl, width), jnp.bfloat16)] * zs,
        compiler_params=pltpu.CompilerParams(vmem_limit_bytes=16 * MIB),
        name="merge",
    )(*sources)


def attend_kernel(grid, kx, bl, share, heads, tile_len, coords, meta, *refs):
    q_refs, refs = refs[:len(coords)], refs[len(coords):]
    kv_refs, refs = refs[:heads], refs[heads:]
    out_ref, own_q_ref = refs[0], refs[1] if kx == 0 else None
    q32_ref, acc_ref, m_ref, over_ref = refs[-4:]
    facts = Facts(meta)
    shard = facts.shard
    rows = grid.n * share
    for q_ref, places in zip(q_refs, coords):
        for i, (fx, fz) in enumerate(places):
            at = pl.multiple_of(grid.owner(shard, fx, fz) * share, 8)
            q32_ref[pl.ds(at, share), :] = q_ref[i].astype(jnp.float32)
    q32_ref[rows:, :] = jnp.zeros((bl + 8, q32_ref.shape[1]), jnp.float32)

    def one(kz, carry):
        attend_block(
            grid, kx, bl, heads, tile_len, kz, facts,
            kv_refs, out_ref, own_q_ref, q32_ref, acc_ref, m_ref, over_ref,
        )
        return carry

    lax.fori_loop(0, grid.zs, one, 0)


def group_rows(queries, g, used):
    return jnp.concatenate(
        [queries[:used, (g * GR + r) * HD:(g * GR + r + 1) * HD] for r in range(GR)], axis=0
    )


def sums(p, v):
    v = jnp.concatenate([v, jnp.ones(v.shape, jnp.bfloat16)], axis=1)
    return jnp.dot(p, v, preferred_element_type=jnp.float32)


def write_partial(accs, peaks, store, c2):
    used = accs[0].shape[0] // GR
    lane = lax.broadcasted_iota(jnp.int32, (used, EXTRA), 1)
    total = jnp.zeros((used, EXTRA), jnp.float32)
    peak = jnp.zeros((used, EXTRA), jnp.float32)
    for g, (acc, m) in enumerate(zip(accs, peaks)):
        for r in range(GR):
            h = g * GR + r
            at = slice(r * used, (r + 1) * used)
            store(slice(h * HD, (h + 1) * HD), acc[at, :HD].astype(jnp.bfloat16))
            total = jnp.where(lane == h, acc[at, HD:], total)
            peak = jnp.where(lane == h, m[at], peak)
    width = len(accs) * GR * HD
    store(slice(width, width + EXTRA), encode(peak * c2, total))
    return total


def attend_block(grid, kx, bl, heads, tile_len, step, facts,
                 kv_refs, out_ref, own_q_ref, q32_ref, acc_ref, m_ref, over_ref):
    block = grid.owner(facts.shard, kx, step)
    offset = jnp.int32(0)
    for b in range(grid.n):
        offset = offset + jnp.where(b < block, facts.length(b), 0)
    prompt = facts.prompt(block)
    valid = jnp.clip(facts.prompt_length(prompt) - facts.shard * tile_len, 0, tile_len)
    c2 = LOG2E / math.sqrt(HD)
    chunk = min(CHUNK, tile_len)
    width = heads * GR * HD

    rest = offset % 8
    window = q32_ref[pl.ds(pl.multiple_of(offset - rest, 8), bl + 8), :]
    window = pltpu.roll(window, jnp.where(rest == 0, 0, bl + 8 - rest), 0)
    queries = window[:bl].astype(jnp.bfloat16)

    group = functools.partial(group_rows, queries)
    if kx == 0:
        @pl.when(step == 0)
        def _():
            own_q_ref[...] = queries

    def keys(g, at, size):
        return kv_refs[g][prompt, pl.ds(at, size), :HD]

    def vals(g, at, size):
        return kv_refs[g][prompt, pl.ds(at, size), HD:]

    def store(used, columns, value):
        out_ref[step, :used, columns] = value

    def update(g, s, seen, v):
        s = jnp.where(seen, s, NEG)
        before = m_ref[g][:, :1]
        m = jnp.maximum(before, jnp.max(s, axis=1, keepdims=True))
        p = jnp.where(seen, jnp.exp2((s - m) * c2), 0.0).astype(jnp.bfloat16)
        acc_ref[g] = acc_ref[g] * jnp.exp2((before - m) * c2) + sums(p, v)
        m_ref[g] = jnp.broadcast_to(m, m_ref.shape[1:])

    def exact():
        acc_ref[...] = jnp.zeros_like(acc_ref)
        m_ref[...] = jnp.full_like(m_ref, NEG)

        def one(c, carry):
            at = pl.multiple_of(c * chunk, chunk)
            for g in range(heads):
                s = dot_nt(group(g, bl), keys(g, at, chunk))
                here = lax.broadcasted_iota(jnp.int32, s.shape, 1) + at
                update(g, s, here < valid, vals(g, at, chunk))
            return carry

        lax.fori_loop(0, (valid + chunk - 1) // chunk, one, 0)
        write_partial(
            [acc_ref[g] for g in range(heads)], [m_ref[g] for g in range(heads)],
            functools.partial(store, bl), c2,
        )

    length = facts.length(block)

    @pl.when(valid == 0)
    def _():
        over_ref[0] = 0
        out_ref[step, :, :width] = jnp.zeros((bl, width), jnp.bfloat16)
        none = jnp.zeros((bl, EXTRA), jnp.float32)
        out_ref[step, :, width:] = encode(none + NEG, none)

    step_of = min(PIECE, tile_len) // chunk

    def single_pass(used, count):
        items = [(g, c) for c in range(count) for g in range(heads)]
        q = [group(g, used) for g in range(heads)]
        peaks = [None] * heads
        accs = [None] * heads
        ahead = dot_nt(q[0], keys(0, 0, chunk))
        for i, (g, c) in enumerate(items):
            s = ahead
            if i + 1 < len(items):
                ng, nc = items[i + 1]
                ahead = dot_nt(q[ng], keys(ng, nc * chunk, chunk))
            if (c + 1) * chunk > (count - step_of) * chunk:
                here = lax.broadcasted_iota(jnp.int32, s.shape, 1) + c * chunk
                s = jnp.where(here < valid, s, NEG)
            if c == 0:
                peaks[g] = jnp.max(s, axis=1, keepdims=True)
            p = jnp.exp2((s - peaks[g]) * c2).astype(jnp.bfloat16)
            part = sums(p, vals(g, c * chunk, chunk))
            accs[g] = part if c == 0 else accs[g] + part
        total = write_partial(
            accs, [jnp.broadcast_to(m, (GR * used, EXTRA)) for m in peaks],
            functools.partial(store, used), c2,
        )

        over_ref[0] = (jnp.max(jnp.where(total < BIG, 0.0, 1.0)) > 0.5).astype(jnp.int32)

    for count in range(step_of, tile_len // chunk + 1, step_of):
        for used in range(ROUND, bl + 1, ROUND):
            some_keys = (valid > (count - step_of) * chunk) & (valid <= count * chunk)
            some_rows = (length > used - ROUND) & (length <= used)
            pl.when(some_keys & some_rows)(functools.partial(single_pass, used, count))

    pl.when(over_ref[0] > 0)(exact)


def own_kernel(first, heads, bl, q_ref, own_ref, out_ref):
    c2 = LOG2E / math.sqrt(HD)
    queries = q_ref[...]
    accs, peaks = [], []
    for g in range(heads):
        base = (first + g) * 2 * HD
        s = dot_nt(group_rows(queries, g, bl), own_ref[0, :, base:base + HD])
        row = lax.broadcasted_iota(jnp.int32, s.shape, 0) % bl
        seen = lax.broadcasted_iota(jnp.int32, s.shape, 1) <= row
        s = jnp.where(seen, s, NEG)
        m = jnp.max(s, axis=1, keepdims=True)
        p = jnp.where(seen, jnp.exp2((s - m) * c2), 0.0).astype(jnp.bfloat16)
        accs.append(sums(p, own_ref[0, :, base + HD:base + 2 * HD]))
        peaks.append(jnp.broadcast_to(m, (GR * bl, EXTRA)))

    def store(columns, value):
        out_ref[:, columns] = value

    write_partial(accs, peaks, store, c2)


def attend_own(queries, own, first, heads):
    bl = own.shape[1]
    return pl.pallas_call(
        functools.partial(own_kernel, first, heads, bl),
        out_shape=jax.ShapeDtypeStruct((bl, heads * GR * HD + EXTRA), jnp.bfloat16),
        compiler_params=pltpu.CompilerParams(vmem_limit_bytes=16 * MIB),
        name="attend_own",
    )(queries, own)


def attend(grid, kx, meta, queries, coords, caches, bl, heads):
    zs = grid.zs
    _, share, cols = queries[0].shape
    tile_len = caches[0].shape[1]
    width = heads * GR * HD + EXTRA
    whole = pl.BlockSpec(memory_space=pltpu.VMEM)
    shapes = [(zs, bl, width)] + [(bl, cols)] * (kx == 0)
    outs = [jax.ShapeDtypeStruct(shape, jnp.bfloat16) for shape in shapes]
    return pl.pallas_call(
        functools.partial(attend_kernel, grid, kx, bl, share, heads, tile_len, coords),
        grid_spec=pltpu.PrefetchScalarGridSpec(
            num_scalar_prefetch=1,
            grid=(1,),
            in_specs=[whole] * (len(queries) + heads),
            out_specs=[whole] * len(outs),
            scratch_shapes=[
                pltpu.VMEM((grid.n * share + bl + 8, cols), jnp.float32),
                pltpu.VMEM((heads, GR * bl, 2 * HD), jnp.float32),
                pltpu.VMEM((heads, GR * bl, HD), jnp.float32),
                pltpu.SMEM((1,), jnp.int32),
            ],
        ),
        out_shape=outs,
        compiler_params=pltpu.CompilerParams(vmem_limit_bytes=20 * MIB),
        cost_estimate=pl.CostEstimate(
            flops=8 * zs * bl * cols * tile_len,
            bytes_accessed=2 * zs * tile_len * heads * 2 * HD,
            transcendentals=zs * bl * heads * GR * tile_len,
        ),
        name="attend",
    )(meta, *queries, *caches)


def finish_kernel(heads, bl, done, meta, *refs):
    sources, out_ref = refs[:-1], refs[-1]
    pieces = sources[done:]
    facts = Facts(meta)
    length = facts.length(facts.shard)
    row = lax.broadcasted_iota(jnp.int32, (bl, HD), 0)
    width = heads * GR * HD
    for c in range(done):
        out_ref[0, :, c * width:(c + 1) * width] = sources[c][0]
    parts, _, total = merge(pieces, heads * GR)
    for h in range(heads * GR):
        at = done * width + h * HD
        value = parts[h] / jnp.broadcast_to(total[:, h:h + 1], (bl, HD))
        out_ref[0, :, at:at + HD] = jnp.where(row < length, value, 0.0).astype(jnp.bfloat16)


def finish(meta, done, pieces, heads):
    bl = pieces[0].shape[0]
    whole = pl.BlockSpec(memory_space=pltpu.VMEM)
    sources = list(done) + list(pieces)
    return pl.pallas_call(
        functools.partial(finish_kernel, heads, bl, len(done)),
        grid_spec=pltpu.PrefetchScalarGridSpec(
            num_scalar_prefetch=1,
            grid=(1,),
            in_specs=[whole] * len(sources),
            out_specs=whole,
        ),
        out_shape=jax.ShapeDtypeStruct((1, bl, (len(done) + 1) * heads * GR * HD), jnp.bfloat16),
        compiler_params=pltpu.CompilerParams(vmem_limit_bytes=16 * MIB),
        name="finish",
    )(meta, *sources)


def shards(
    hidden_rows,
    carried,
    query_weight,
    response_cache,
    prompt_cache,
    prompt_lengths,
    response_lengths,
    block_prompts,
):
    grid = Grid(lax.axis_size("seq"))
    bl = hidden_rows.shape[1]
    local_kv = response_cache.shape[2] // (2 * HD)
    share = bl * 5 // 8
    chunks = 2 if local_kv % 2 == 0 else 1
    heads = local_kv // chunks
    part_cols = heads * GR * HD
    place = jnp.stack([lax.axis_index("sec"), lax.axis_index("seq")]).astype(jnp.int32)

    def after(value, done):
        return lax.optimization_barrier((value, done))[0]

    def fetched(head, done=()):
        return fetch_cache(grid.n, after(meta, done), prompt_cache, 2 * HD, head)

    handed = lax.ppermute(carried, "sec", [(0, 1)])
    depth = query_weight.shape[1]
    hidden = hidden_rows if depth % HD else fetch([hidden_rows])[0]
    slices = split(grid, place, hidden, handed, depth)
    n = grid.n
    lane = lax.broadcasted_iota(jnp.int32, (1, n), 1)
    section, shard = after((lax.axis_index("sec"), lax.axis_index("seq")), handed)
    meta = jnp.concatenate([
        response_lengths, block_prompts[:, :, 0],
        jnp.pad(prompt_lengths, (0, n - prompt_lengths.shape[0]))[None],
        jnp.where(lane == 0, section, shard).astype(jnp.int32),
    ])
    weight, own = fetch([query_weight, after(response_cache, handed)])
    x = [slices[0]] + [None] * (grid.n - 1)
    for kz in reversed(range(grid.zs)):
        for kx in reversed(range(grid.xs)):
            k = kx * grid.zs + kz
            if k:
                x[k] = grid.swap(slices[k], kx, kz)
    part = project(grid, meta, x, weight, bl, share, chunks)
    part = [piece.reshape(grid.zs, share, part_cols) for piece in part]
    part = [part[c * grid.xs:(c + 1) * grid.xs] for c in range(chunks)]

    def narrow(value):
        return (value * 0.125).astype(jnp.float16)

    def widen(value):
        return value.astype(jnp.float32) * 8.0

    def both(first, second):
        return lax.optimization_barrier((first, second))

    def reduce_x(parts, done=()):
        got = [grid.swap(after(narrow(parts[kx]), done), kx, 0) for kx in range(1, grid.xs)]
        return functools.reduce(jnp.add, [parts[0]] + [widen(value) for value in got])

    def narrow_z(held):
        return [narrow(held[kz]) for kz in range(1, grid.zs)]

    def sum_z(held, sends, beside):
        got = [grid.swap(send, 0, kz + 1) for kz, send in enumerate(sends)]
        parts = [after(held[0], beside)] + [widen(value) for value in got]
        return functools.reduce(jnp.add, parts).astype(jnp.bfloat16)

    def gather_z(value):
        return [value] + [grid.swap(value, 0, kz) for kz in range(1, grid.zs)]

    def gather_x(value):
        return [value] + [grid.swap(value, kx, 0) for kx in range(1, grid.xs)]

    z_then_x = [[(kx, kz) for kz in range(grid.zs)] for kx in range(grid.xs)]
    x_then_z = [[(kx, kz) for kx in range(grid.xs)] for kz in range(grid.zs)]

    def call(c, kx, queries):
        return attend(
            grid, kx, meta, queries, x_then_z if c else z_then_x,
            caches[c * heads:(c + 1) * heads], bl, heads,
        )

    def call_far(c, queries):
        outs = [call(c, kx, queries)[0] for kx in range(1, grid.xs)]
        return outs, [grid.swap(out, kx + 1, 0) for kx, out in enumerate(outs)]

    def send_z(merged):
        return [merged[0]] + [grid.swap(merged[kz], 0, kz) for kz in range(1, grid.zs)]

    half = (local_kv + 1) // 4
    caches = [fetched(head) for head in range(half)]
    part[0][0] = after(part[0][0], caches)
    held = reduce_x(part[0])
    sends = narrow_z(held)
    if chunks > 1:
        sends, part[1][1] = both(sends, part[1][1])
        later = reduce_x(part[1])
    caches += [fetched(head, sends) for head in range(half, heads)]
    mine = sum_z(held, sends, caches)
    column = gather_z(mine)
    if chunks > 1:
        caches += [fetched(head, mine) for head in range(heads, heads + half)]
        sends = narrow_z(after(later, mine))
        column = after(column, (caches, sends))
    queries = gather_x(jnp.stack(column))
    if chunks == 1:
        outs, mets = call_far(0, queries)
        queries[0] = after(queries[0], outs)
        held, own_q = call(0, 0, queries)
        pieces = send_z(merge_column([held] + mets, heads * GR))
        pieces.append(attend_own(own_q, own, 0, heads))
        return finish(meta, [], pieces, heads)
    caches += [fetched(head, sends) for head in range(heads + half, local_kv)]
    mine = sum_z(later, sends, caches)
    queries[0] = after(queries[0], mine)
    near = jnp.stack(gather_x(mine))
    outs, mets = call_far(0, queries)
    near = after(near, outs)
    queries[0] = after(queries[0], near)
    later = gather_z(near)
    held, own_q = call(0, 0, queries)
    merged = merge_column([held] + mets, heads * GR)
    later[0] = after(later[0], merged)
    outs, mets = call_far(1, later)
    merged, later[0] = both(after(merged, outs), later[0])
    pieces = send_z(merged)
    held, later_q = call(1, 0, later)
    merged = merge_column([held] + mets, heads * GR)
    own_q, later_q = after((own_q, later_q), merged)
    done = finish(meta, [], pieces + [attend_own(own_q, own, 0, heads)], heads)
    pieces = send_z(merged) + [attend_own(later_q, own, heads, heads)]
    return finish(meta, [done], pieces, heads)


def solution(mesh):
    placed = (
        P("sec", "seq", None),
        P("sec", "seq", None),
        P("sec", "seq", "tp"),
        P("sec", "seq", "tp"),
        P("sec", None, "seq", "tp"),
        P(),
        P(),
        P(),
    )
    return jax.shard_map(
        shards, mesh=mesh, in_specs=placed, out_specs=P("sec", "seq", "tp"), check_vma=False
    )
```

```python
import functools
import math

import jax
import jax.numpy as jnp
from jax import lax
from jax.experimental import pallas as pl
from jax.experimental.pallas import tpu as pltpu
from jax.sharding import PartitionSpec as P

HD = 128
GR = 4
NEG = -1e30
LOG2E = 1.4426950408889634
CHUNK = 512
PIECE = 1024
ROUND = 32
EXTRA = 128
SLOT = 16
BIG = 2.0 ** 100
MIB = 1024 * 1024


def dot_nt(a, b):
    return lax.dot_general(a, b, (((1,), (1,)), ((), ())), preferred_element_type=jnp.float32)


class Grid:
    def __init__(self, count):
        self.n = count
        self.xs = 1 << ((count.bit_length() - 1) // 2)
        self.zs = count // self.xs

    def owner(self, shard, kx, kz):
        z, x = shard // self.xs, shard % self.xs
        return (z ^ kz) * self.xs + (x ^ kx)

    def swap(self, value, kx, kz):
        pairs = [(s, self.owner(s, kx, kz)) for s in range(self.n)]
        return lax.ppermute(value, "seq", pairs)


class Facts:
    def __init__(self, meta):
        self.meta = meta
        self.section, self.shard = meta[5, 0], meta[5, 1]

    def length(self, block):
        return self.meta[self.section, block]

    def prompt(self, block):
        return self.meta[2 + self.section, block]

    def prompt_length(self, prompt):
        return self.meta[4, prompt]


def split_kernel(grid, depth, meta, hidden_ref, handed_ref, *out_refs):
    for kx in range(grid.xs):
        for kz in range(grid.zs):
            at = pl.multiple_of(grid.owner(meta[1], kx, kz) * depth, HD)
            total = hidden_ref[0, :, pl.ds(at, depth)].astype(jnp.float32) + handed_ref[
                0, :, pl.ds(at, depth)
            ].astype(jnp.float32)
            out_refs[kx * grid.zs + kz][...] = total.astype(jnp.bfloat16)


def split(grid, meta, hidden, handed, depth):
    bl = hidden.shape[1]
    if depth % HD:
        total = (hidden[0].astype(jnp.float32) + handed[0].astype(jnp.float32)).astype(jnp.bfloat16)
        return [
            lax.dynamic_slice_in_dim(total, grid.owner(meta[1], kx, kz) * depth, depth, 1)
            for kx in range(grid.xs) for kz in range(grid.zs)
        ]
    whole = pl.BlockSpec(memory_space=pltpu.VMEM)
    return pl.pallas_call(
        functools.partial(split_kernel, grid, depth),
        grid_spec=pltpu.PrefetchScalarGridSpec(
            num_scalar_prefetch=1,
            grid=(1,),
            in_specs=[whole, whole],
            out_specs=[whole] * grid.n,
        ),
        out_shape=[jax.ShapeDtypeStruct((bl, depth), jnp.bfloat16)] * grid.n,
        compiler_params=pltpu.CompilerParams(vmem_limit_bytes=16 * MIB),
        name="split",
    )(meta, hidden, handed)


def run_moves(moves):
    for needed, move in moves:
        if needed is None:
            move.start()
        else:
            pl.when(needed)(move.start)
    for needed, move in moves:
        if needed is None:
            move.wait()
        else:
            pl.when(needed)(move.wait)


def fetch_kernel(*refs):
    count = len(refs) // 2
    run_moves([
        (None, pltpu.make_async_copy(refs[i], refs[count + i], refs[-1].at[i]))
        for i in range(count)
    ])


def fetch(arrays):
    anywhere, near = pl.BlockSpec(memory_space=pltpu.HBM), pl.BlockSpec(memory_space=pltpu.VMEM)
    size = sum(math.prod(array.shape) for array in arrays)
    out = pl.pallas_call(
        fetch_kernel,
        in_specs=[anywhere] * len(arrays),
        out_specs=[near] * len(arrays),
        scratch_shapes=[pltpu.SemaphoreType.DMA((len(arrays),))],
        out_shape=[pltpu.VMEM(array.shape, array.dtype) for array in arrays],
        compiler_params=pltpu.CompilerParams(vmem_limit_bytes=4 * MIB),
        cost_estimate=pl.CostEstimate(flops=0, bytes_accessed=2 * size, transcendentals=0),
        name="fetch",
    )(*[pltpu.with_memory_space_constraint(array, pltpu.HBM) for array in arrays])
    return [pltpu.with_memory_space_constraint(array, pltpu.VMEM) for array in out]


def fetch_cache_kernel(n, chunk, width, first, meta, cache_ref, kv_ref, sem):
    count, tile_len = kv_ref.shape[:2]
    facts = Facts(meta)
    moves = []
    for p in range(count):
        asked = facts.prompt(0) == p
        for b in range(1, n):
            asked = asked | (facts.prompt(b) == p)
        for c in range(tile_len // chunk):
            at = pl.ds(c * chunk, chunk)
            needed = asked & (facts.prompt_length(p) > facts.shard * tile_len + c * chunk)
            moves.append((needed, pltpu.make_async_copy(
                cache_ref.at[0, p, at, pl.ds(first * width, width)], kv_ref.at[p, at],
                sem.at[p, c],
            )))
    run_moves(moves)


def fetch_cache(n, meta, cache, width, first):
    count, tile_len = cache.shape[1:3]
    chunk = min(PIECE, tile_len)
    shape = (count, tile_len, width)
    out = pl.pallas_call(
        functools.partial(fetch_cache_kernel, n, chunk, width, first),
        grid_spec=pltpu.PrefetchScalarGridSpec(
            num_scalar_prefetch=1,
            grid=(1,),
            in_specs=[pl.BlockSpec(memory_space=pltpu.HBM)],
            out_specs=pl.BlockSpec(memory_space=pltpu.VMEM),
            scratch_shapes=[pltpu.SemaphoreType.DMA((count, tile_len // chunk))],
        ),
        out_shape=pltpu.VMEM(shape, cache.dtype),
        compiler_params=pltpu.CompilerParams(vmem_limit_bytes=4 * MIB),
        cost_estimate=pl.CostEstimate(
            flops=0, bytes_accessed=2 * math.prod(shape), transcendentals=0
        ),
        name="fetch_cache",
    )(meta, pltpu.with_memory_space_constraint(cache, pltpu.HBM))
    return pltpu.with_memory_space_constraint(out, pltpu.VMEM)


def project_kernel(grid, bl, share, meta, *refs):
    x_refs, w_ref, refs = refs[:grid.n], refs[grid.n], refs[grid.n + 1:]
    out_refs, (xp_ref, starts) = refs[:-2], refs[-2:]

    facts = Facts(meta)
    shard = facts.shard
    offset = jnp.int32(0)
    for b in range(grid.n):
        starts[b] = offset
        offset = offset + facts.length(b)
    lane = lax.broadcasted_iota(jnp.int32, (8, grid.n * bl), 1)
    target = jnp.full(lane.shape, -1, jnp.int32)
    owners = [
        grid.owner(shard, kx, kz) for kx in range(grid.xs) for kz in range(grid.zs)
    ]
    for k, b in enumerate(owners):
        order = lane - k * bl
        used = (order >= 0) & (order < facts.length(b))
        target = jnp.where(used, order + starts[b], target)
    row = lax.broadcasted_iota(jnp.int32, (share, grid.n * bl), 0)
    target = jnp.broadcast_to(target[:1], row.shape)
    picks = [jnp.where(row + b * share == target, 1.0, 0.0) for b in owners]
    pick = jnp.concatenate(picks, axis=0).astype(jnp.bfloat16)
    x = jnp.concatenate([ref[...] for ref in x_refs], axis=0)
    chosen = jnp.dot(pick, x, preferred_element_type=jnp.float32)
    xp_ref[...] = chosen.astype(jnp.bfloat16)

    rows = grid.zs * share
    tile = out_refs[0].shape[1]
    for i, out_ref in enumerate(out_refs):
        chunk, kx = i // grid.xs, i % grid.xs
        out_ref[...] = jnp.dot(
            xp_ref[kx * rows:(kx + 1) * rows], w_ref[0, :, chunk * tile:(chunk + 1) * tile],
            preferred_element_type=jnp.float32,
        )


def project(grid, meta, xs, w, bl, share, chunks):
    k, cols = w.shape[1:]
    rows = grid.n * share
    tile = cols // chunks
    piece = (grid.zs * share, tile)
    whole = pl.BlockSpec(memory_space=pltpu.VMEM)
    return pl.pallas_call(
        functools.partial(project_kernel, grid, bl, share),
        grid_spec=pltpu.PrefetchScalarGridSpec(
            num_scalar_prefetch=1,
            grid=(1,),
            in_specs=[whole] * (grid.n + 1),
            out_specs=[whole] * (chunks * grid.xs),
            scratch_shapes=[
                pltpu.VMEM((rows, k), jnp.bfloat16), pltpu.SMEM((grid.n,), jnp.int32)
            ],
        ),
        out_shape=[jax.ShapeDtypeStruct(piece, jnp.float32)] * (chunks * grid.xs),
        compiler_params=pltpu.CompilerParams(vmem_limit_bytes=20 * MIB),
        cost_estimate=pl.CostEstimate(
            flops=2 * rows * k * cols, bytes_accessed=2 * k * cols + 4 * rows * cols,
            transcendentals=0,
        ),
        name="project",
    )(meta, *xs, w)


def three_terms(value):
    high = value.astype(jnp.bfloat16).astype(jnp.float32)
    mid = (value - high).astype(jnp.bfloat16).astype(jnp.float32)
    return [high, mid, value - high - mid]


def encode(peak, total):
    lane = lax.broadcasted_iota(jnp.int32, peak.shape, 1)
    out = jnp.zeros(peak.shape, jnp.float32)
    for i, term in enumerate(three_terms(peak) + three_terms(total)):
        term = jnp.where(lane < SLOT, term, 0.0)
        out = out + (pltpu.roll(term, i * SLOT, 1) if i else term)
    return out.astype(jnp.bfloat16)


def decode(tile):
    terms = tile.astype(jnp.float32)
    parts = [terms] + [pltpu.roll(terms, EXTRA - i * SLOT, 1) for i in range(1, 6)]
    return parts[0] + parts[1] + parts[2], parts[3] + parts[4] + parts[5]


def merge(refs, heads):
    width = heads * HD
    peaks, totals = zip(*[decode(ref[:, width:]) for ref in refs])
    rows = peaks[0].shape[0]
    peak = functools.reduce(jnp.maximum, peaks)
    weights = [jnp.exp2(one - peak) for one in peaks]
    total = functools.reduce(jnp.add, [w * one for w, one in zip(weights, totals)])
    out = []
    for h in range(heads):
        terms = [
            jnp.broadcast_to(weight[:, h:h + 1], (rows, HD))
            * ref[:, h * HD:(h + 1) * HD].astype(jnp.float32)
            for weight, ref in zip(weights, refs)
        ]
        out.append(functools.reduce(jnp.add, terms))
    return out, peak, total


def merge_kernel(zs, heads, *refs):
    sources, outs = refs[:-zs], refs[-zs:]
    for kz in range(zs):
        parts, peak, total = merge([ref.at[kz] for ref in sources], heads)
        for h in range(heads):
            outs[kz][:, h * HD:(h + 1) * HD] = parts[h].astype(jnp.bfloat16)
        outs[kz][:, heads * HD:] = encode(peak, total)


def merge_column(sources, heads):
    zs, bl, width = sources[0].shape
    return pl.pallas_call(
        functools.partial(merge_kernel, zs, heads),
        out_shape=[jax.ShapeDtypeStruct((bl, width), jnp.bfloat16)] * zs,
        compiler_params=pltpu.CompilerParams(vmem_limit_bytes=16 * MIB),
        name="merge",
    )(*sources)


def attend_kernel(grid, kx, bl, share, heads, tile_len, coords, meta, *refs):
    q_refs, refs = refs[:len(coords)], refs[len(coords):]
    kv_refs, refs = refs[:heads], refs[heads:]
    out_ref, own_q_ref = refs[0], refs[1] if kx == 0 else None
    q32_ref, acc_ref, m_ref, over_ref = refs[-4:]
    facts = Facts(meta)
    shard = facts.shard
    rows = grid.n * share
    for q_ref, places in zip(q_refs, coords):
        for i, (fx, fz) in enumerate(places):
            at = pl.multiple_of(grid.owner(shard, fx, fz) * share, 8)
            q32_ref[pl.ds(at, share), :] = q_ref[i].astype(jnp.float32)
    q32_ref[rows:, :] = jnp.zeros((bl + 8, q32_ref.shape[1]), jnp.float32)

    def one(kz, carry):
        attend_block(
            grid, kx, bl, heads, tile_len, kz, facts,
            kv_refs, out_ref, own_q_ref, q32_ref, acc_ref, m_ref, over_ref,
        )
        return carry

    lax.fori_loop(0, grid.zs, one, 0)


def group_rows(queries, g, used):
    return jnp.concatenate(
        [queries[:used, (g * GR + r) * HD:(g * GR + r + 1) * HD] for r in range(GR)], axis=0
    )


def sums(p, v):
    v = jnp.concatenate([v, jnp.ones(v.shape, jnp.bfloat16)], axis=1)
    return jnp.dot(p, v, preferred_element_type=jnp.float32)


def write_partial(accs, peaks, store, c2):
    used = accs[0].shape[0] // GR
    lane = lax.broadcasted_iota(jnp.int32, (used, EXTRA), 1)
    total = jnp.zeros((used, EXTRA), jnp.float32)
    peak = jnp.zeros((used, EXTRA), jnp.float32)
    for g, (acc, m) in enumerate(zip(accs, peaks)):
        for r in range(GR):
            h = g * GR + r
            at = slice(r * used, (r + 1) * used)
            store(slice(h * HD, (h + 1) * HD), acc[at, :HD].astype(jnp.bfloat16))
            total = jnp.where(lane == h, acc[at, HD:], total)
            peak = jnp.where(lane == h, m[at], peak)
    width = len(accs) * GR * HD
    store(slice(width, width + EXTRA), encode(peak * c2, total))
    return total


def attend_block(grid, kx, bl, heads, tile_len, step, facts,
                 kv_refs, out_ref, own_q_ref, q32_ref, acc_ref, m_ref, over_ref):
    block = grid.owner(facts.shard, kx, step)
    offset = jnp.int32(0)
    for b in range(grid.n):
        offset = offset + jnp.where(b < block, facts.length(b), 0)
    prompt = facts.prompt(block)
    valid = jnp.clip(facts.prompt_length(prompt) - facts.shard * tile_len, 0, tile_len)
    c2 = LOG2E / math.sqrt(HD)
    chunk = min(CHUNK, tile_len)
    width = heads * GR * HD

    rest = offset % 8
    window = q32_ref[pl.ds(pl.multiple_of(offset - rest, 8), bl + 8), :]
    window = pltpu.roll(window, jnp.where(rest == 0, 0, bl + 8 - rest), 0)
    queries = window[:bl].astype(jnp.bfloat16)

    group = functools.partial(group_rows, queries)
    if kx == 0:
        @pl.when(step == 0)
        def _():
            own_q_ref[...] = queries

    def keys(g, at, size):
        return kv_refs[g][prompt, pl.ds(at, size), :HD]

    def vals(g, at, size):
        return kv_refs[g][prompt, pl.ds(at, size), HD:]

    def store(used, columns, value):
        out_ref[step, :used, columns] = value

    def update(g, s, seen, v):
        s = jnp.where(seen, s, NEG)
        before = m_ref[g][:, :1]
        m = jnp.maximum(before, jnp.max(s, axis=1, keepdims=True))
        p = jnp.where(seen, jnp.exp2((s - m) * c2), 0.0).astype(jnp.bfloat16)
        acc_ref[g] = acc_ref[g] * jnp.exp2((before - m) * c2) + sums(p, v)
        m_ref[g] = jnp.broadcast_to(m, m_ref.shape[1:])

    def exact():
        acc_ref[...] = jnp.zeros_like(acc_ref)
        m_ref[...] = jnp.full_like(m_ref, NEG)

        def one(c, carry):
            at = pl.multiple_of(c * chunk, chunk)
            for g in range(heads):
                s = dot_nt(group(g, bl), keys(g, at, chunk))
                here = lax.broadcasted_iota(jnp.int32, s.shape, 1) + at
                update(g, s, here < valid, vals(g, at, chunk))
            return carry

        lax.fori_loop(0, (valid + chunk - 1) // chunk, one, 0)
        write_partial(
            [acc_ref[g] for g in range(heads)], [m_ref[g] for g in range(heads)],
            functools.partial(store, bl), c2,
        )

    length = facts.length(block)

    @pl.when(valid == 0)
    def _():
        over_ref[0] = 0
        out_ref[step, :, :width] = jnp.zeros((bl, width), jnp.bfloat16)
        none = jnp.zeros((bl, EXTRA), jnp.float32)
        out_ref[step, :, width:] = encode(none + NEG, none)

    step_of = min(PIECE, tile_len) // chunk

    def single_pass(used, count):
        items = [(g, c) for c in range(count) for g in range(heads)]
        q = [group(g, used) for g in range(heads)]
        peaks = [None] * heads
        accs = [None] * heads
        ahead = dot_nt(q[0], keys(0, 0, chunk))
        for i, (g, c) in enumerate(items):
            s = ahead
            if i + 1 < len(items):
                ng, nc = items[i + 1]
                ahead = dot_nt(q[ng], keys(ng, nc * chunk, chunk))
            if (c + 1) * chunk > (count - step_of) * chunk:
                here = lax.broadcasted_iota(jnp.int32, s.shape, 1) + c * chunk
                s = jnp.where(here < valid, s, NEG)
            if c == 0:
                peaks[g] = jnp.max(s, axis=1, keepdims=True)
            p = jnp.exp2((s - peaks[g]) * c2).astype(jnp.bfloat16)
            part = sums(p, vals(g, c * chunk, chunk))
            accs[g] = part if c == 0 else accs[g] + part
        total = write_partial(
            accs, [jnp.broadcast_to(m, (GR * used, EXTRA)) for m in peaks],
            functools.partial(store, used), c2,
        )

        over_ref[0] = (jnp.max(jnp.where(total < BIG, 0.0, 1.0)) > 0.5).astype(jnp.int32)

    for count in range(step_of, tile_len // chunk + 1, step_of):
        for used in range(ROUND, bl + 1, ROUND):
            some_keys = (valid > (count - step_of) * chunk) & (valid <= count * chunk)
            some_rows = (length > used - ROUND) & (length <= used)
            pl.when(some_keys & some_rows)(functools.partial(single_pass, used, count))

    pl.when(over_ref[0] > 0)(exact)


def own_kernel(first, heads, bl, q_ref, own_ref, out_ref):
    c2 = LOG2E / math.sqrt(HD)
    queries = q_ref[...]
    accs, peaks = [], []
    for g in range(heads):
        base = (first + g) * 2 * HD
        s = dot_nt(group_rows(queries, g, bl), own_ref[0, :, base:base + HD])
        row = lax.broadcasted_iota(jnp.int32, s.shape, 0) % bl
        seen = lax.broadcasted_iota(jnp.int32, s.shape, 1) <= row
        s = jnp.where(seen, s, NEG)
        m = jnp.max(s, axis=1, keepdims=True)
        p = jnp.where(seen, jnp.exp2((s - m) * c2), 0.0).astype(jnp.bfloat16)
        accs.append(sums(p, own_ref[0, :, base + HD:base + 2 * HD]))
        peaks.append(jnp.broadcast_to(m, (GR * bl, EXTRA)))

    def store(columns, value):
        out_ref[:, columns] = value

    write_partial(accs, peaks, store, c2)


def attend_own(queries, own, first, heads):
    bl = own.shape[1]
    return pl.pallas_call(
        functools.partial(own_kernel, first, heads, bl),
        out_shape=jax.ShapeDtypeStruct((bl, heads * GR * HD + EXTRA), jnp.bfloat16),
        compiler_params=pltpu.CompilerParams(vmem_limit_bytes=16 * MIB),
        name="attend_own",
    )(queries, own)


def attend(grid, kx, meta, queries, coords, caches, bl, heads):
    zs = grid.zs
    _, share, cols = queries[0].shape
    tile_len = caches[0].shape[1]
    width = heads * GR * HD + EXTRA
    whole = pl.BlockSpec(memory_space=pltpu.VMEM)
    shapes = [(zs, bl, width)] + [(bl, cols)] * (kx == 0)
    outs = [jax.ShapeDtypeStruct(shape, jnp.bfloat16) for shape in shapes]
    return pl.pallas_call(
        functools.partial(attend_kernel, grid, kx, bl, share, heads, tile_len, coords),
        grid_spec=pltpu.PrefetchScalarGridSpec(
            num_scalar_prefetch=1,
            grid=(1,),
            in_specs=[whole] * (len(queries) + heads),
            out_specs=[whole] * len(outs),
            scratch_shapes=[
                pltpu.VMEM((grid.n * share + bl + 8, cols), jnp.float32),
                pltpu.VMEM((heads, GR * bl, 2 * HD), jnp.float32),
                pltpu.VMEM((heads, GR * bl, HD), jnp.float32),
                pltpu.SMEM((1,), jnp.int32),
            ],
        ),
        out_shape=outs,
        compiler_params=pltpu.CompilerParams(vmem_limit_bytes=20 * MIB),
        cost_estimate=pl.CostEstimate(
            flops=8 * zs * bl * cols * tile_len,
            bytes_accessed=2 * zs * tile_len * heads * 2 * HD,
            transcendentals=zs * bl * heads * GR * tile_len,
        ),
        name="attend",
    )(meta, *queries, *caches)


def finish_kernel(heads, bl, done, meta, *refs):
    sources, out_ref = refs[:-1], refs[-1]
    pieces = sources[done:]
    facts = Facts(meta)
    length = facts.length(facts.shard)
    row = lax.broadcasted_iota(jnp.int32, (bl, HD), 0)
    width = heads * GR * HD
    for c in range(done):
        out_ref[0, :, c * width:(c + 1) * width] = sources[c][0]
    parts, _, total = merge(pieces, heads * GR)
    for h in range(heads * GR):
        at = done * width + h * HD
        value = parts[h] / jnp.broadcast_to(total[:, h:h + 1], (bl, HD))
        out_ref[0, :, at:at + HD] = jnp.where(row < length, value, 0.0).astype(jnp.bfloat16)


def finish(meta, done, pieces, heads):
    bl = pieces[0].shape[0]
    whole = pl.BlockSpec(memory_space=pltpu.VMEM)
    sources = list(done) + list(pieces)
    return pl.pallas_call(
        functools.partial(finish_kernel, heads, bl, len(done)),
        grid_spec=pltpu.PrefetchScalarGridSpec(
            num_scalar_prefetch=1,
            grid=(1,),
            in_specs=[whole] * len(sources),
            out_specs=whole,
        ),
        out_shape=jax.ShapeDtypeStruct((1, bl, (len(done) + 1) * heads * GR * HD), jnp.bfloat16),
        compiler_params=pltpu.CompilerParams(vmem_limit_bytes=16 * MIB),
        name="finish",
    )(meta, *sources)


def shards(
    hidden_rows,
    carried,
    query_weight,
    response_cache,
    prompt_cache,
    prompt_lengths,
    response_lengths,
    block_prompts,
):
    grid = Grid(lax.axis_size("seq"))
    bl = hidden_rows.shape[1]
    local_kv = response_cache.shape[2] // (2 * HD)
    share = bl * 5 // 8
    chunks = 2 if local_kv % 2 == 0 else 1
    heads = local_kv // chunks
    part_cols = heads * GR * HD
    place = jnp.stack([lax.axis_index("sec"), lax.axis_index("seq")]).astype(jnp.int32)

    def after(value, done):
        return lax.optimization_barrier((value, done))[0]

    def fetched(head, done=()):
        return fetch_cache(grid.n, after(meta, done), prompt_cache, 2 * HD, head)

    handed = lax.ppermute(carried, "sec", [(0, 1)])
    depth = query_weight.shape[1]
    hidden = hidden_rows if depth % HD else fetch([hidden_rows])[0]
    slices = split(grid, place, hidden, handed, depth)
    n = grid.n
    lane = lax.broadcasted_iota(jnp.int32, (1, n), 1)
    section, shard = after((lax.axis_index("sec"), lax.axis_index("seq")), handed)
    meta = jnp.concatenate([
        response_lengths, block_prompts[:, :, 0],
        jnp.pad(prompt_lengths, (0, n - prompt_lengths.shape[0]))[None],
        jnp.where(lane == 0, section, shard).astype(jnp.int32),
    ])
    weight, own = fetch([query_weight, after(response_cache, handed)])
    x = [slices[0]] + [None] * (grid.n - 1)
    for kz in reversed(range(grid.zs)):
        for kx in reversed(range(grid.xs)):
            k = kx * grid.zs + kz
            if k:
                x[k] = grid.swap(slices[k], kx, kz)
    part = project(grid, meta, x, weight, bl, share, chunks)
    part = [piece.reshape(grid.zs, share, part_cols) for piece in part]
    part = [part[c * grid.xs:(c + 1) * grid.xs] for c in range(chunks)]

    def narrow(value):
        return (value * 0.125).astype(jnp.float16)

    def widen(value):
        return value.astype(jnp.float32) * 8.0

    def both(first, second):
        return lax.optimization_barrier((first, second))

    def reduce_x(parts, done=()):
        got = [grid.swap(after(narrow(parts[kx]), done), kx, 0) for kx in range(1, grid.xs)]
        return functools.reduce(jnp.add, [parts[0]] + [widen(value) for value in got])

    def narrow_z(held):
        return [narrow(held[kz]) for kz in range(1, grid.zs)]

    def sum_z(held, sends, beside):
        got = [grid.swap(send, 0, kz + 1) for kz, send in enumerate(sends)]
        parts = [after(held[0], beside)] + [widen(value) for value in got]
        return functools.reduce(jnp.add, parts).astype(jnp.bfloat16)

    def gather_z(value):
        return [value] + [grid.swap(value, 0, kz) for kz in range(1, grid.zs)]

    def gather_x(value):
        return [value] + [grid.swap(value, kx, 0) for kx in range(1, grid.xs)]

    z_then_x = [[(kx, kz) for kz in range(grid.zs)] for kx in range(grid.xs)]
    x_then_z = [[(kx, kz) for kx in range(grid.xs)] for kz in range(grid.zs)]

    def call(c, kx, queries):
        return attend(
            grid, kx, meta, queries, x_then_z if c else z_then_x,
            caches[c * heads:(c + 1) * heads], bl, heads,
        )

    def call_far(c, queries):
        outs = [call(c, kx, queries)[0] for kx in range(1, grid.xs)]
        return outs, [grid.swap(out, kx + 1, 0) for kx, out in enumerate(outs)]

    def send_z(merged):
        return [merged[0]] + [grid.swap(merged[kz], 0, kz) for kz in range(1, grid.zs)]

    half = (local_kv + 1) // 4
    caches = [fetched(head) for head in range(heads)]
    part[0][0] = after(part[0][0], caches)
    held = reduce_x(part[0])
    sends = narrow_z(held)
    if chunks > 1:
        sends, part[1][1] = both(sends, part[1][1])
        later = reduce_x(part[1])
    if chunks > 1:
        caches += [fetched(head, sends) for head in range(heads, heads + half)]
    mine = sum_z(held, sends, caches)
    column = gather_z(mine)
    if chunks > 1:
        sends = narrow_z(after(later, mine))
        column = after(column, sends)
    queries = gather_x(jnp.stack(column))
    if chunks == 1:
        outs, mets = call_far(0, queries)
        queries[0] = after(queries[0], outs)
        held, own_q = call(0, 0, queries)
        pieces = send_z(merge_column([held] + mets, heads * GR))
        pieces.append(attend_own(own_q, own, 0, heads))
        return finish(meta, [], pieces, heads)
    caches += [fetched(head, sends) for head in range(heads + half, local_kv)]
    mine = sum_z(later, sends, caches)
    queries[0] = after(queries[0], mine)
    near = jnp.stack(gather_x(mine))
    outs, mets = call_far(0, queries)
    near = after(near, outs)
    queries[0] = after(queries[0], near)
    later = gather_z(near)
    held, own_q = call(0, 0, queries)
    merged = merge_column([held] + mets, heads * GR)
    later[0] = after(later[0], merged)
    outs, mets = call_far(1, later)
    merged, later[0] = both(after(merged, outs), later[0])
    pieces = send_z(merged)
    held, later_q = call(1, 0, later)
    merged = merge_column([held] + mets, heads * GR)
    own_q, later_q = after((own_q, later_q), merged)
    done = finish(meta, [], pieces + [attend_own(own_q, own, 0, heads)], heads)
    pieces = send_z(merged) + [attend_own(later_q, own, heads, heads)]
    return finish(meta, [done], pieces, heads)


def solution(mesh):
    placed = (
        P("sec", "seq", None),
        P("sec", "seq", None),
        P("sec", "seq", "tp"),
        P("sec", "seq", "tp"),
        P("sec", None, "seq", "tp"),
        P(),
        P(),
        P(),
    )
    return jax.shard_map(
        shards, mesh=mesh, in_specs=placed, out_specs=P("sec", "seq", "tp"), check_vma=False
    )
```

```python
import functools
import math

import jax
import jax.numpy as jnp
from jax import lax
from jax.experimental import pallas as pl
from jax.experimental.pallas import tpu as pltpu
from jax.sharding import PartitionSpec as P

HD = 128
GR = 4
NEG = -1e30
LOG2E = 1.4426950408889634
CHUNK = 512
PIECE = 1024
ROUND = 32
EXTRA = 128
SLOT = 16
BIG = 2.0 ** 100
MIB = 1024 * 1024


def dot_nt(a, b):
    return lax.dot_general(a, b, (((1,), (1,)), ((), ())), preferred_element_type=jnp.float32)


class Grid:
    def __init__(self, count):
        self.n = count
        self.xs = 1 << ((count.bit_length() - 1) // 2)
        self.zs = count // self.xs

    def owner(self, shard, kx, kz):
        z, x = shard // self.xs, shard % self.xs
        return (z ^ kz) * self.xs + (x ^ kx)

    def swap(self, value, kx, kz):
        pairs = [(s, self.owner(s, kx, kz)) for s in range(self.n)]
        return lax.ppermute(value, "seq", pairs)


class Facts:
    def __init__(self, meta):
        self.meta = meta
        self.section, self.shard = meta[5, 0], meta[5, 1]

    def length(self, block):
        return self.meta[self.section, block]

    def prompt(self, block):
        return self.meta[2 + self.section, block]

    def prompt_length(self, prompt):
        return self.meta[4, prompt]


def split_kernel(grid, depth, meta, hidden_ref, handed_ref, *out_refs):
    for kx in range(grid.xs):
        for kz in range(grid.zs):
            at = pl.multiple_of(grid.owner(meta[1], kx, kz) * depth, HD)
            total = hidden_ref[0, :, pl.ds(at, depth)].astype(jnp.float32) + handed_ref[
                0, :, pl.ds(at, depth)
            ].astype(jnp.float32)
            out_refs[kx * grid.zs + kz][...] = total.astype(jnp.bfloat16)


def split(grid, meta, hidden, handed, depth):
    bl = hidden.shape[1]
    if depth % HD:
        total = (hidden[0].astype(jnp.float32) + handed[0].astype(jnp.float32)).astype(jnp.bfloat16)
        return [
            lax.dynamic_slice_in_dim(total, grid.owner(meta[1], kx, kz) * depth, depth, 1)
            for kx in range(grid.xs) for kz in range(grid.zs)
        ]
    whole = pl.BlockSpec(memory_space=pltpu.VMEM)
    return pl.pallas_call(
        functools.partial(split_kernel, grid, depth),
        grid_spec=pltpu.PrefetchScalarGridSpec(
            num_scalar_prefetch=1,
            grid=(1,),
            in_specs=[whole, whole],
            out_specs=[whole] * grid.n,
        ),
        out_shape=[jax.ShapeDtypeStruct((bl, depth), jnp.bfloat16)] * grid.n,
        compiler_params=pltpu.CompilerParams(vmem_limit_bytes=16 * MIB),
        name="split",
    )(meta, hidden, handed)


def run_moves(moves):
    for needed, move in moves:
        if needed is None:
            move.start()
        else:
            pl.when(needed)(move.start)
    for needed, move in moves:
        if needed is None:
            move.wait()
        else:
            pl.when(needed)(move.wait)


def fetch_kernel(*refs):
    count = len(refs) // 2
    run_moves([
        (None, pltpu.make_async_copy(refs[i], refs[count + i], refs[-1].at[i]))
        for i in range(count)
    ])


def fetch(arrays):
    anywhere, near = pl.BlockSpec(memory_space=pltpu.HBM), pl.BlockSpec(memory_space=pltpu.VMEM)
    size = sum(math.prod(array.shape) for array in arrays)
    out = pl.pallas_call(
        fetch_kernel,
        in_specs=[anywhere] * len(arrays),
        out_specs=[near] * len(arrays),
        scratch_shapes=[pltpu.SemaphoreType.DMA((len(arrays),))],
        out_shape=[pltpu.VMEM(array.shape, array.dtype) for array in arrays],
        compiler_params=pltpu.CompilerParams(vmem_limit_bytes=4 * MIB),
        cost_estimate=pl.CostEstimate(flops=0, bytes_accessed=2 * size, transcendentals=0),
        name="fetch",
    )(*[pltpu.with_memory_space_constraint(array, pltpu.HBM) for array in arrays])
    return [pltpu.with_memory_space_constraint(array, pltpu.VMEM) for array in out]


def fetch_cache_kernel(n, chunk, width, first, meta, cache_ref, kv_ref, sem):
    count, tile_len = kv_ref.shape[:2]
    facts = Facts(meta)
    moves = []
    for p in range(count):
        asked = facts.prompt(0) == p
        for b in range(1, n):
            asked = asked | (facts.prompt(b) == p)
        for c in range(tile_len // chunk):
            at = pl.ds(c * chunk, chunk)
            needed = asked & (facts.prompt_length(p) > facts.shard * tile_len + c * chunk)
            moves.append((needed, pltpu.make_async_copy(
                cache_ref.at[0, p, at, pl.ds(first * width, width)], kv_ref.at[p, at],
                sem.at[p, c],
            )))
    run_moves(moves)


def fetch_cache(n, meta, cache, width, first):
    count, tile_len = cache.shape[1:3]
    chunk = min(PIECE, tile_len)
    shape = (count, tile_len, width)
    out = pl.pallas_call(
        functools.partial(fetch_cache_kernel, n, chunk, width, first),
        grid_spec=pltpu.PrefetchScalarGridSpec(
            num_scalar_prefetch=1,
            grid=(1,),
            in_specs=[pl.BlockSpec(memory_space=pltpu.HBM)],
            out_specs=pl.BlockSpec(memory_space=pltpu.VMEM),
            scratch_shapes=[pltpu.SemaphoreType.DMA((count, tile_len // chunk))],
        ),
        out_shape=pltpu.VMEM(shape, cache.dtype),
        compiler_params=pltpu.CompilerParams(vmem_limit_bytes=4 * MIB),
        cost_estimate=pl.CostEstimate(
            flops=0, bytes_accessed=2 * math.prod(shape), transcendentals=0
        ),
        name="fetch_cache",
    )(meta, pltpu.with_memory_space_constraint(cache, pltpu.HBM))
    return pltpu.with_memory_space_constraint(out, pltpu.VMEM)


def project_kernel(grid, bl, share, meta, *refs):
    x_refs, w_ref, refs = refs[:grid.n], refs[grid.n], refs[grid.n + 1:]
    out_refs, (xp_ref, starts) = refs[:-2], refs[-2:]

    facts = Facts(meta)
    shard = facts.shard
    offset = jnp.int32(0)
    for b in range(grid.n):
        starts[b] = offset
        offset = offset + facts.length(b)
    lane = lax.broadcasted_iota(jnp.int32, (8, grid.n * bl), 1)
    target = jnp.full(lane.shape, -1, jnp.int32)
    owners = [
        grid.owner(shard, kx, kz) for kx in range(grid.xs) for kz in range(grid.zs)
    ]
    for k, b in enumerate(owners):
        order = lane - k * bl
        used = (order >= 0) & (order < facts.length(b))
        target = jnp.where(used, order + starts[b], target)
    row = lax.broadcasted_iota(jnp.int32, (share, grid.n * bl), 0)
    target = jnp.broadcast_to(target[:1], row.shape)
    picks = [jnp.where(row + b * share == target, 1.0, 0.0) for b in owners]
    pick = jnp.concatenate(picks, axis=0).astype(jnp.bfloat16)
    x = jnp.concatenate([ref[...] for ref in x_refs], axis=0)
    chosen = jnp.dot(pick, x, preferred_element_type=jnp.float32)
    xp_ref[...] = chosen.astype(jnp.bfloat16)

    rows = grid.zs * share
    tile = out_refs[0].shape[1]
    for i, out_ref in enumerate(out_refs):
        chunk, kx = i // grid.xs, i % grid.xs
        out_ref[...] = jnp.dot(
            xp_ref[kx * rows:(kx + 1) * rows], w_ref[0, :, chunk * tile:(chunk + 1) * tile],
            preferred_element_type=jnp.float32,
        )


def project(grid, meta, xs, w, bl, share, chunks):
    k, cols = w.shape[1:]
    rows = grid.n * share
    tile = cols // chunks
    piece = (grid.zs * share, tile)
    whole = pl.BlockSpec(memory_space=pltpu.VMEM)
    return pl.pallas_call(
        functools.partial(project_kernel, grid, bl, share),
        grid_spec=pltpu.PrefetchScalarGridSpec(
            num_scalar_prefetch=1,
            grid=(1,),
            in_specs=[whole] * (grid.n + 1),
            out_specs=[whole] * (chunks * grid.xs),
            scratch_shapes=[
                pltpu.VMEM((rows, k), jnp.bfloat16), pltpu.SMEM((grid.n,), jnp.int32)
            ],
        ),
        out_shape=[jax.ShapeDtypeStruct(piece, jnp.float32)] * (chunks * grid.xs),
        compiler_params=pltpu.CompilerParams(vmem_limit_bytes=20 * MIB),
        cost_estimate=pl.CostEstimate(
            flops=2 * rows * k * cols, bytes_accessed=2 * k * cols + 4 * rows * cols,
            transcendentals=0,
        ),
        name="project",
    )(meta, *xs, w)


def three_terms(value):
    high = value.astype(jnp.bfloat16).astype(jnp.float32)
    mid = (value - high).astype(jnp.bfloat16).astype(jnp.float32)
    return [high, mid, value - high - mid]


def encode(peak, total):
    lane = lax.broadcasted_iota(jnp.int32, peak.shape, 1)
    out = jnp.zeros(peak.shape, jnp.float32)
    for i, term in enumerate(three_terms(peak) + three_terms(total)):
        term = jnp.where(lane < SLOT, term, 0.0)
        out = out + (pltpu.roll(term, i * SLOT, 1) if i else term)
    return out.astype(jnp.bfloat16)


def decode(tile):
    terms = tile.astype(jnp.float32)
    parts = [terms] + [pltpu.roll(terms, EXTRA - i * SLOT, 1) for i in range(1, 6)]
    return parts[0] + parts[1] + parts[2], parts[3] + parts[4] + parts[5]


def merge(refs, heads):
    width = heads * HD
    peaks, totals = zip(*[decode(ref[:, width:]) for ref in refs])
    rows = peaks[0].shape[0]
    peak = functools.reduce(jnp.maximum, peaks)
    weights = [jnp.exp2(one - peak) for one in peaks]
    total = functools.reduce(jnp.add, [w * one for w, one in zip(weights, totals)])
    out = []
    for h in range(heads):
        terms = [
            jnp.broadcast_to(weight[:, h:h + 1], (rows, HD))
            * ref[:, h * HD:(h + 1) * HD].astype(jnp.float32)
            for weight, ref in zip(weights, refs)
        ]
        out.append(functools.reduce(jnp.add, terms))
    return out, peak, total


def merge_kernel(zs, heads, *refs):
    sources, outs = refs[:-zs], refs[-zs:]
    for kz in range(zs):
        parts, peak, total = merge([ref.at[kz] for ref in sources], heads)
        for h in range(heads):
            outs[kz][:, h * HD:(h + 1) * HD] = parts[h].astype(jnp.bfloat16)
        outs[kz][:, heads * HD:] = encode(peak, total)


def merge_column(sources, heads):
    zs, bl, width = sources[0].shape
    return pl.pallas_call(
        functools.partial(merge_kernel, zs, heads),
        out_shape=[jax.ShapeDtypeStruct((bl, width), jnp.bfloat16)] * zs,
        compiler_params=pltpu.CompilerParams(vmem_limit_bytes=16 * MIB),
        name="merge",
    )(*sources)


def attend_kernel(grid, kx, bl, share, heads, tile_len, coords, meta, *refs):
    q_refs, refs = refs[:len(coords)], refs[len(coords):]
    kv_refs, refs = refs[:heads], refs[heads:]
    out_ref, own_q_ref = refs[0], refs[1] if kx == 0 else None
    q32_ref, acc_ref, m_ref, over_ref = refs[-4:]
    facts = Facts(meta)
    shard = facts.shard
    rows = grid.n * share
    for q_ref, places in zip(q_refs, coords):
        for i, (fx, fz) in enumerate(places):
            at = pl.multiple_of(grid.owner(shard, fx, fz) * share, 8)
            q32_ref[pl.ds(at, share), :] = q_ref[i].astype(jnp.float32)
    q32_ref[rows:, :] = jnp.zeros((bl + 8, q32_ref.shape[1]), jnp.float32)

    def one(kz, carry):
        attend_block(
            grid, kx, bl, heads, tile_len, kz, facts,
            kv_refs, out_ref, own_q_ref, q32_ref, acc_ref, m_ref, over_ref,
        )
        return carry

    lax.fori_loop(0, grid.zs, one, 0)


def group_rows(queries, g, used):
    return jnp.concatenate(
        [queries[:used, (g * GR + r) * HD:(g * GR + r + 1) * HD] for r in range(GR)], axis=0
    )


def sums(p, v):
    v = jnp.concatenate([v, jnp.ones(v.shape, jnp.bfloat16)], axis=1)
    return jnp.dot(p, v, preferred_element_type=jnp.float32)


def write_partial(accs, peaks, store, c2):
    used = accs[0].shape[0] // GR
    lane = lax.broadcasted_iota(jnp.int32, (used, EXTRA), 1)
    total = jnp.zeros((used, EXTRA), jnp.float32)
    peak = jnp.zeros((used, EXTRA), jnp.float32)
    for g, (acc, m) in enumerate(zip(accs, peaks)):
        for r in range(GR):
            h = g * GR + r
            at = slice(r * used, (r + 1) * used)
            store(slice(h * HD, (h + 1) * HD), acc[at, :HD].astype(jnp.bfloat16))
            total = jnp.where(lane == h, acc[at, HD:], total)
            peak = jnp.where(lane == h, m[at], peak)
    width = len(accs) * GR * HD
    store(slice(width, width + EXTRA), encode(peak * c2, total))
    return total


def attend_block(grid, kx, bl, heads, tile_len, step, facts,
                 kv_refs, out_ref, own_q_ref, q32_ref, acc_ref, m_ref, over_ref):
    block = grid.owner(facts.shard, kx, step)
    offset = jnp.int32(0)
    for b in range(grid.n):
        offset = offset + jnp.where(b < block, facts.length(b), 0)
    prompt = facts.prompt(block)
    valid = jnp.clip(facts.prompt_length(prompt) - facts.shard * tile_len, 0, tile_len)
    c2 = LOG2E / math.sqrt(HD)
    chunk = min(CHUNK, tile_len)
    width = heads * GR * HD

    rest = offset % 8
    window = q32_ref[pl.ds(pl.multiple_of(offset - rest, 8), bl + 8), :]
    window = pltpu.roll(window, jnp.where(rest == 0, 0, bl + 8 - rest), 0)
    queries = window[:bl].astype(jnp.bfloat16)

    group = functools.partial(group_rows, queries)
    if kx == 0:
        @pl.when(step == 0)
        def _():
            own_q_ref[...] = queries

    def keys(g, at, size):
        return kv_refs[g][prompt, pl.ds(at, size), :HD]

    def vals(g, at, size):
        return kv_refs[g][prompt, pl.ds(at, size), HD:]

    def store(used, columns, value):
        out_ref[step, :used, columns] = value

    def update(g, s, seen, v):
        s = jnp.where(seen, s, NEG)
        before = m_ref[g][:, :1]
        m = jnp.maximum(before, jnp.max(s, axis=1, keepdims=True))
        p = jnp.where(seen, jnp.exp2((s - m) * c2), 0.0).astype(jnp.bfloat16)
        acc_ref[g] = acc_ref[g] * jnp.exp2((before - m) * c2) + sums(p, v)
        m_ref[g] = jnp.broadcast_to(m, m_ref.shape[1:])

    def exact():
        acc_ref[...] = jnp.zeros_like(acc_ref)
        m_ref[...] = jnp.full_like(m_ref, NEG)

        def one(c, carry):
            at = pl.multiple_of(c * chunk, chunk)
            for g in range(heads):
                s = dot_nt(group(g, bl), keys(g, at, chunk))
                here = lax.broadcasted_iota(jnp.int32, s.shape, 1) + at
                update(g, s, here < valid, vals(g, at, chunk))
            return carry

        lax.fori_loop(0, (valid + chunk - 1) // chunk, one, 0)
        write_partial(
            [acc_ref[g] for g in range(heads)], [m_ref[g] for g in range(heads)],
            functools.partial(store, bl), c2,
        )

    length = facts.length(block)

    @pl.when(valid == 0)
    def _():
        over_ref[0] = 0
        out_ref[step, :, :width] = jnp.zeros((bl, width), jnp.bfloat16)
        none = jnp.zeros((bl, EXTRA), jnp.float32)
        out_ref[step, :, width:] = encode(none + NEG, none)

    step_of = min(PIECE, tile_len) // chunk

    def single_pass(used, count):
        items = [(g, c) for c in range(count) for g in range(heads)]
        q = [group(g, used) for g in range(heads)]
        peaks = [None] * heads
        accs = [None] * heads
        ahead = dot_nt(q[0], keys(0, 0, chunk))
        for i, (g, c) in enumerate(items):
            s = ahead
            if i + 1 < len(items):
                ng, nc = items[i + 1]
                ahead = dot_nt(q[ng], keys(ng, nc * chunk, chunk))
            if (c + 1) * chunk > (count - step_of) * chunk:
                here = lax.broadcasted_iota(jnp.int32, s.shape, 1) + c * chunk
                s = jnp.where(here < valid, s, NEG)
            if c == 0:
                peaks[g] = jnp.max(s, axis=1, keepdims=True)
            p = jnp.exp2((s - peaks[g]) * c2).astype(jnp.bfloat16)
            part = sums(p, vals(g, c * chunk, chunk))
            accs[g] = part if c == 0 else accs[g] + part
        total = write_partial(
            accs, [jnp.broadcast_to(m, (GR * used, EXTRA)) for m in peaks],
            functools.partial(store, used), c2,
        )

        over_ref[0] = (jnp.max(jnp.where(total < BIG, 0.0, 1.0)) > 0.5).astype(jnp.int32)

    for count in range(step_of, tile_len // chunk + 1, step_of):
        for used in range(ROUND, bl + 1, ROUND):
            some_keys = (valid > (count - step_of) * chunk) & (valid <= count * chunk)
            some_rows = (length > used - ROUND) & (length <= used)
            pl.when(some_keys & some_rows)(functools.partial(single_pass, used, count))

    pl.when(over_ref[0] > 0)(exact)


def own_kernel(first, heads, bl, q_ref, own_ref, out_ref):
    c2 = LOG2E / math.sqrt(HD)
    queries = q_ref[...]
    accs, peaks = [], []
    for g in range(heads):
        base = (first + g) * 2 * HD
        s = dot_nt(group_rows(queries, g, bl), own_ref[0, :, base:base + HD])
        row = lax.broadcasted_iota(jnp.int32, s.shape, 0) % bl
        seen = lax.broadcasted_iota(jnp.int32, s.shape, 1) <= row
        s = jnp.where(seen, s, NEG)
        m = jnp.max(s, axis=1, keepdims=True)
        p = jnp.where(seen, jnp.exp2((s - m) * c2), 0.0).astype(jnp.bfloat16)
        accs.append(sums(p, own_ref[0, :, base + HD:base + 2 * HD]))
        peaks.append(jnp.broadcast_to(m, (GR * bl, EXTRA)))

    def store(columns, value):
        out_ref[:, columns] = value

    write_partial(accs, peaks, store, c2)


def attend_own(queries, own, first, heads):
    bl = own.shape[1]
    return pl.pallas_call(
        functools.partial(own_kernel, first, heads, bl),
        out_shape=jax.ShapeDtypeStruct((bl, heads * GR * HD + EXTRA), jnp.bfloat16),
        compiler_params=pltpu.CompilerParams(vmem_limit_bytes=16 * MIB),
        name="attend_own",
    )(queries, own)


def attend(grid, kx, meta, queries, coords, caches, bl, heads):
    zs = grid.zs
    _, share, cols = queries[0].shape
    tile_len = caches[0].shape[1]
    width = heads * GR * HD + EXTRA
    whole = pl.BlockSpec(memory_space=pltpu.VMEM)
    shapes = [(zs, bl, width)] + [(bl, cols)] * (kx == 0)
    outs = [jax.ShapeDtypeStruct(shape, jnp.bfloat16) for shape in shapes]
    return pl.pallas_call(
        functools.partial(attend_kernel, grid, kx, bl, share, heads, tile_len, coords),
        grid_spec=pltpu.PrefetchScalarGridSpec(
            num_scalar_prefetch=1,
            grid=(1,),
            in_specs=[whole] * (len(queries) + heads),
            out_specs=[whole] * len(outs),
            scratch_shapes=[
                pltpu.VMEM((grid.n * share + bl + 8, cols), jnp.float32),
                pltpu.VMEM((heads, GR * bl, 2 * HD), jnp.float32),
                pltpu.VMEM((heads, GR * bl, HD), jnp.float32),
                pltpu.SMEM((1,), jnp.int32),
            ],
        ),
        out_shape=outs,
        compiler_params=pltpu.CompilerParams(vmem_limit_bytes=20 * MIB),
        cost_estimate=pl.CostEstimate(
            flops=8 * zs * bl * cols * tile_len,
            bytes_accessed=2 * zs * tile_len * heads * 2 * HD,
            transcendentals=zs * bl * heads * GR * tile_len,
        ),
        name="attend",
    )(meta, *queries, *caches)


def finish_kernel(heads, bl, done, meta, *refs):
    sources, out_ref = refs[:-1], refs[-1]
    pieces = sources[done:]
    facts = Facts(meta)
    length = facts.length(facts.shard)
    row = lax.broadcasted_iota(jnp.int32, (bl, HD), 0)
    width = heads * GR * HD
    for c in range(done):
        out_ref[0, :, c * width:(c + 1) * width] = sources[c][0]
    parts, _, total = merge(pieces, heads * GR)
    for h in range(heads * GR):
        at = done * width + h * HD
        value = parts[h] / jnp.broadcast_to(total[:, h:h + 1], (bl, HD))
        out_ref[0, :, at:at + HD] = jnp.where(row < length, value, 0.0).astype(jnp.bfloat16)


def finish(meta, done, pieces, heads):
    bl = pieces[0].shape[0]
    whole = pl.BlockSpec(memory_space=pltpu.VMEM)
    sources = list(done) + list(pieces)
    return pl.pallas_call(
        functools.partial(finish_kernel, heads, bl, len(done)),
        grid_spec=pltpu.PrefetchScalarGridSpec(
            num_scalar_prefetch=1,
            grid=(1,),
            in_specs=[whole] * len(sources),
            out_specs=whole,
        ),
        out_shape=jax.ShapeDtypeStruct((1, bl, (len(done) + 1) * heads * GR * HD), jnp.bfloat16),
        compiler_params=pltpu.CompilerParams(vmem_limit_bytes=16 * MIB),
        name="finish",
    )(meta, *sources)


def shards(
    hidden_rows,
    carried,
    query_weight,
    response_cache,
    prompt_cache,
    prompt_lengths,
    response_lengths,
    block_prompts,
):
    grid = Grid(lax.axis_size("seq"))
    bl = hidden_rows.shape[1]
    local_kv = response_cache.shape[2] // (2 * HD)
    share = bl * 5 // 8
    chunks = 2 if local_kv % 2 == 0 else 1
    heads = local_kv // chunks
    part_cols = heads * GR * HD
    place = jnp.stack([lax.axis_index("sec"), lax.axis_index("seq")]).astype(jnp.int32)

    def after(value, done):
        return lax.optimization_barrier((value, done))[0]

    def fetched(head, done=()):
        return fetch_cache(grid.n, after(meta, done), prompt_cache, 2 * HD, head)

    handed = lax.ppermute(carried, "sec", [(0, 1)])
    depth = query_weight.shape[1]
    hidden = hidden_rows if depth % HD else fetch([hidden_rows])[0]
    slices = split(grid, place, hidden, handed, depth)
    x = [slices[0]] + [None] * (grid.n - 1)
    for kz in reversed(range(grid.zs)):
        for kx in reversed(range(grid.xs)):
            k = kx * grid.zs + kz
            if k:
                x[k] = grid.swap(slices[k], kx, kz)
    early = x[1:grid.zs][:3]
    weight, own = fetch([query_weight, after(response_cache, early)])
    n = grid.n
    lane = lax.broadcasted_iota(jnp.int32, (1, n), 1)
    section, shard = after((lax.axis_index("sec"), lax.axis_index("seq")), early)
    meta = jnp.concatenate([
        response_lengths, block_prompts[:, :, 0],
        jnp.pad(prompt_lengths, (0, n - prompt_lengths.shape[0]))[None],
        jnp.where(lane == 0, section, shard).astype(jnp.int32),
    ])
    part = project(grid, meta, x, weight, bl, share, chunks)
    part = [piece.reshape(grid.zs, share, part_cols) for piece in part]
    part = [part[c * grid.xs:(c + 1) * grid.xs] for c in range(chunks)]

    def narrow(value):
        return (value * 0.125).astype(jnp.float16)

    def widen(value):
        return value.astype(jnp.float32) * 8.0

    def both(first, second):
        return lax.optimization_barrier((first, second))

    def reduce_x(parts, done=()):
        got = [grid.swap(after(narrow(parts[kx]), done), kx, 0) for kx in range(1, grid.xs)]
        return functools.reduce(jnp.add, [parts[0]] + [widen(value) for value in got])

    def narrow_z(held):
        return [narrow(held[kz]) for kz in range(1, grid.zs)]

    def sum_z(held, sends, beside):
        got = [grid.swap(send, 0, kz + 1) for kz, send in enumerate(sends)]
        parts = [after(held[0], beside)] + [widen(value) for value in got]
        return functools.reduce(jnp.add, parts).astype(jnp.bfloat16)

    def gather_z(value):
        return [value] + [grid.swap(value, 0, kz) for kz in range(1, grid.zs)]

    def gather_x(value):
        return [value] + [grid.swap(value, kx, 0) for kx in range(1, grid.xs)]

    z_then_x = [[(kx, kz) for kz in range(grid.zs)] for kx in range(grid.xs)]
    x_then_z = [[(kx, kz) for kx in range(grid.xs)] for kz in range(grid.zs)]

    def call(c, kx, queries):
        return attend(
            grid, kx, meta, queries, x_then_z if c else z_then_x,
            caches[c * heads:(c + 1) * heads], bl, heads,
        )

    def call_far(c, queries):
        outs = [call(c, kx, queries)[0] for kx in range(1, grid.xs)]
        return outs, [grid.swap(out, kx + 1, 0) for kx, out in enumerate(outs)]

    def send_z(merged):
        return [merged[0]] + [grid.swap(merged[kz], 0, kz) for kz in range(1, grid.zs)]

    half = (local_kv + 1) // 4
    caches = [fetched(head) for head in range(heads)]
    part[0][0] = after(part[0][0], caches)
    held = reduce_x(part[0])
    sends = narrow_z(held)
    if chunks > 1:
        sends, part[1][1] = both(sends, part[1][1])
        later = reduce_x(part[1])
    if chunks > 1:
        caches += [fetched(head, sends) for head in range(heads, heads + half)]
    mine = sum_z(held, sends, caches)
    column = gather_z(mine)
    if chunks > 1:
        sends = narrow_z(after(later, mine))
        column = after(column, sends)
    queries = gather_x(jnp.stack(column))
    if chunks == 1:
        outs, mets = call_far(0, queries)
        queries[0] = after(queries[0], outs)
        held, own_q = call(0, 0, queries)
        pieces = send_z(merge_column([held] + mets, heads * GR))
        pieces.append(attend_own(own_q, own, 0, heads))
        return finish(meta, [], pieces, heads)
    caches += [fetched(head, sends) for head in range(heads + half, local_kv)]
    mine = sum_z(later, sends, caches)
    queries[0] = after(queries[0], mine)
    near = jnp.stack(gather_x(mine))
    outs, mets = call_far(0, queries)
    near = after(near, outs)
    queries[0] = after(queries[0], near)
    later = gather_z(near)
    held, own_q = call(0, 0, queries)
    merged = merge_column([held] + mets, heads * GR)
    later[0] = after(later[0], merged)
    outs, mets = call_far(1, later)
    merged, later[0] = both(after(merged, outs), later[0])
    pieces = send_z(merged)
    held, later_q = call(1, 0, later)
    merged = merge_column([held] + mets, heads * GR)
    own_q, later_q = after((own_q, later_q), merged)
    done = finish(meta, [], pieces + [attend_own(own_q, own, 0, heads)], heads)
    pieces = send_z(merged) + [attend_own(later_q, own, heads, heads)]
    return finish(meta, [done], pieces, heads)


def solution(mesh):
    placed = (
        P("sec", "seq", None),
        P("sec", "seq", None),
        P("sec", "seq", "tp"),
        P("sec", "seq", "tp"),
        P("sec", None, "seq", "tp"),
        P(),
        P(),
        P(),
    )
    return jax.shard_map(
        shards, mesh=mesh, in_specs=placed, out_specs=P("sec", "seq", "tp"), check_vma=False
    )
```
